32 devices in a mesh: tp: 4 (over y, x), dp: 8 (over z, core).
Axes of the slice: x: 2, y: 2, z: 4, core: 2. Of those that a mesh axis runs over, the one named last changes fastest.
Arguments:
- tokens: bfloat16 [2, 8, 256, 2048], P(None, 'dp', 'tp'), may hold values from -6 to 6
- cotangent: bfloat16 [2, 8, 256, 2048], P(None, 'dp', 'tp'), may hold values from -6 to 6
- routes: int32 [2, 8, 256, 8], P(None, 'dp'), may hold values from 0 to 15, all different within a row; in each aligned block of 256 rows (0 to 255, 256 to 511, ..., all dimensions but the last counted through in order) at most 160 rows name the same one
- lengths: int32 [2, 8, 2], P(None, 'dp'), may hold values from 0 to 256, as said below
- attn_gain: float32 [2048], replicated, may hold values from 0.5 to 1.5
- qkv_weight: bfloat16 [2048, 3, 2048], P(None, None, 'tp'), may hold values from -0.125 to 0.125
- qk_gain: float32 [2, 2048], P(None, 'tp'), may hold values from 0.5 to 1.5
- out_weight: bfloat16 [2048, 2048], P('tp'), may hold values from -0.5 to 0.5
- moe_gain: float32 [2048], replicated, may hold values from 0.5 to 1.5
- router: bfloat16 [2048, 16], replicated, may hold values from -0.0625 to 0.0625
- w_gateup: bfloat16 [16, 2048, 2, 1024], P('dp', None, None, 'tp'), may hold values from -0.125 to 0.125
- w_down: bfloat16 [16, 1024, 2048], P('dp', 'tp'), may hold values from -6 to 6
Outputs:
- out: bfloat16 [2, 8, 256, 2048], P(None, 'dp', 'tp')
- token_grad: bfloat16 [2, 8, 256, 2048], P(None, 'dp', 'tp')
- attn_gain_grad: float32 [2048], replicated
- qkv_weight_grad: float32 [2048, 3, 2048], P(None, None, 'tp')
- qk_gain_grad: float32 [2, 2048], P(None, 'tp')
- out_weight_grad: float32 [2048, 2048], P('tp')
- moe_gain_grad: float32 [2048], replicated
- router_grad: float32 [2048, 16], replicated
- gateup_grad: float32 [16, 2048, 2, 1024], P('dp', None, None, 'tp')
- down_grad: float32 [16, 1024, 2048], P('dp', 'tp')
The draws below stay inside these ranges and needn't reach their ends.
Inputs may be any that keep to these rules, and one draw needn't show every extreme that they name: `lengths`: row (m, g) gives block (m, g): up to two sequences laid from the block's first row, a zero length standing for none; the shorter one and the padding after both cover fewer than 64 rows together. In every draw some block holds one sequence of all 256 rows. `routes`: each row names 8 different experts; the 256 rows of one block name one expert at most 160 times.
All inputs are finite; a program needn't handle non-finite values.
Results may differ from the reference program's by a relative error of at most 0.025.
Values may be sent and summed in bfloat16 or wider, within the bound.
No kernel may reach another device: no remote copies, remote signals or barrier semaphores. Data moves between devices by JAX's collectives and lax.ppermute only.
A program may use at most 384 MiB of HBM per device.

```python
import math
import jax
import jax.numpy as jnp
import numpy as np
from jax import lax

D = 2048
HEADS = 16
HD = 128
FF = 1024
TOP = 8
MICRO = 2
MB_ROWS = 64
EXPERTS = 16
GROUP = 256
CAP = 160
N_TP = 4
N_DP = 8


def draw_lengths(key, part):
    key = jax.random.fold_in(key, 11)
    key_pad, key_short, key_flip, key_full = jax.random.split(key, 4)
    half_rows = MB_ROWS // 2
    shape_rows = (MICRO, N_DP)
    padding = jax.random.randint(key_pad, shape_rows, 0, half_rows)
    shorter = jax.random.randint(key_short, shape_rows, 0, half_rows)
    flipped = jax.random.randint(key_flip, shape_rows, 0, 2)
    full_row = jax.random.randint(key_full, (), 0, MICRO * N_DP)
    row_index = jnp.arange(MICRO * N_DP, dtype=jnp.int32).reshape(shape_rows)
    padding = jnp.where(row_index == full_row, 0, padding)
    shorter = jnp.where(row_index == full_row, 0, shorter)
    longer = GROUP - padding - shorter
    leading = jnp.where(flipped == 1, shorter, longer)
    trailing = jnp.where(flipped == 1, longer, shorter)
    return jnp.stack([leading, trailing], axis=-1).astype(jnp.int32)


def block_scale(stream_key, dims, shards, smallest, high):
    def one(dim, shards_of):
        heights = jax.random.uniform(jax.random.fold_in(jax.random.fold_in(stream_key, 6), dim), (shards_of,), jnp.float32, smallest / len(shards), high / len(shards))
        return jnp.repeat(jnp.exp(heights), dims[dim] // shards_of).reshape((-1,) + (1,) * (len(dims) - dim - 1))

    factor_of = one(*shards[0])
    for cut in shards[1:]:
        factor_of = factor_of * one(*cut)
    return factor_of


def shared_out(rng, own, number, rows, number_of, top, limit, slope):
    order = jax.random.permutation(rng, number_of)
    crowded, ordinary = load_shares(number_of, rows * top, limit, slope, True), load_shares(number_of, rows * top, limit, slope, False)
    places = jnp.arange(number_of)

    def named(tallies, rotation):
        used = int((tallies > 0).sum())
        fixed = max(1, used // 4)
        passed = fixed + (places - fixed + rotation * (used - fixed)) % max(1, number_of - fixed)
        return jnp.zeros((number_of,), jnp.int32).at[order[jnp.where(places < fixed, places, passed)]].set(jnp.asarray(tallies, jnp.int32))

    tallies = jnp.where(number % 4 == 0, named(crowded, number // 4), named(ordinary, number - number // 4 - 1))
    mixed = jax.random.permutation(jax.random.fold_in(own, 3), number_of)
    source_of, sink = mixed[0:number_of // 2 * 2:2], mixed[1:number_of // 2 * 2:2]
    margin = jnp.minimum(tallies[source_of] - 1, limit - tallies[sink]) // 2
    margin = jnp.where((source_of == order[0]) | (sink == order[0]) | (tallies[sink] == 0), 0, jnp.maximum(margin, 0))
    passed = jax.random.randint(jax.random.fold_in(own, 4), (number_of // 2,), 0, 1 << 20) % (margin + 1)
    tallies = tallies.at[source_of].add(-passed).at[sink].add(passed)
    labels = jnp.searchsorted(jnp.cumsum(tallies), jnp.arange(rows * top), side="right").astype(jnp.int32)
    table = labels.reshape(top, rows).T
    table = table[jax.random.permutation(jax.random.fold_in(own, 1), rows)]
    rotation = jax.random.randint(jax.random.fold_in(own, 2), (rows, 1), 0, top)
    return jnp.take_along_axis(table, (jnp.arange(top)[None, :] + rotation) % top, axis=1)


def load_shares(amount, total, limit, lean, full):
    loads = [(1 << 20) // math.isqrt(rank ** lean) + 1 for rank in range(1, amount + 1)]
    largest = limit if full else min(limit, max(-(-total // amount), total * loads[0] // sum(loads)))
    least = 1 if total - largest >= amount - 1 else 0
    holding, surplus = [largest] + [least] * (amount - 1), total - largest - least * (amount - 1)
    while surplus > 0:
        movable = [i for i in range(1, amount) if holding[i] < largest] or [i for i in range(1, amount) if holding[i] < limit]
        whole, left = sum([loads[i] for i in movable]), surplus
        for i in movable:
            extra = min(limit - holding[i], max(1, left * loads[i] // whole), surplus)
            holding[i] = holding[i] + extra
            surplus = surplus - extra
    return np.array(holding)


def centred(own_key, extent, scale, most, cuts=(), kind=jnp.bfloat16):
    result = jax.random.normal(own_key, extent, jnp.float32) * scale
    if len(cuts) > 0:
        result = block_scale(own_key, extent, cuts, -0.22, 0.18) * result
    return jnp.clip(result, min=-most, max=most).astype(kind)


def setup_inputs(seed: int = 0) -> dict:
    key_list = jax.random.split(jax.random.key(seed), 13)
    tokens = centred(key_list[0], (MICRO, N_DP, GROUP, D), 1.0, 6.0, ((1, 8), (2, 4)))
    cotangent = centred(key_list[1], (MICRO, N_DP, GROUP, D), 1.0, 6.0, ((1, 8), (2, 4)))
    routes_keys = jax.random.split(jax.random.fold_in(key_list[2], 1), MICRO * N_DP * GROUP // GROUP)
    routes_turns = jax.random.permutation(jax.random.fold_in(key_list[2], 3), MICRO * N_DP * GROUP // GROUP)
    routes = jax.vmap(lambda own, number: shared_out(jax.random.fold_in(key_list[2], 2), own, number, GROUP, EXPERTS, TOP, CAP, 1))(routes_keys, routes_turns).reshape((MICRO, N_DP, GROUP, TOP))
    lengths = draw_lengths(jax.random.fold_in(key_list[12], 71), 0)
    attn_gain = jnp.clip(1.0 + 0.1 * jax.random.normal(key_list[4], (D,), jnp.float32), 0.5, 1.5)
    qkv_weight = centred(key_list[5], (D, 3, D), D ** -0.5, 0.125, ((2, 4),))
    qk_gain = jnp.clip(1.0 + 0.1 * jax.random.normal(key_list[6], (2, D), jnp.float32), 0.5, 1.5)
    out_weight = centred(key_list[7], (D, D), (D // 16) ** -0.5, 0.5, ((0, 4),))
    moe_gain = jnp.clip(1.0 + 0.1 * jax.random.normal(key_list[8], (D,), jnp.float32), 0.5, 1.5)
    router = centred(key_list[9], (D, EXPERTS), (4 * D) ** -0.5, 0.0625)
    w_gateup = centred(key_list[10], (EXPERTS, D, 2, FF), D ** -0.5, 0.125, ((0, 8), (3, 4)))
    w_down = centred(key_list[11], (EXPERTS, FF, D), (max(FF // 1024, 1)) ** -0.5, 6.0, ((0, 8), (1, 4)))
    return {"tokens": tokens, "cotangent": cotangent, "routes": routes, "lengths": lengths, "attn_gain": attn_gain, "qkv_weight": qkv_weight, "qk_gain": qk_gain, "out_weight": out_weight, "moe_gain": moe_gain, "router": router, "w_gateup": w_gateup, "w_down": w_down}


EPSILON = 1e-05
HIGHEST = lax.Precision.HIGHEST

@jax.custom_vjp
def low(v):
    return lax.optimization_barrier(v.astype(jnp.bfloat16)).astype(jnp.float32)

@jax.custom_vjp
def low_back(v):
    return v

def low_keep(v):
    return (low(v), None)

def low_pass(kept, grad):
    return (grad,)

def back_keep(v):
    return (v, None)

def back_low(kept, grad):
    return (low(grad),)
low.defvjp(low_keep, low_pass)
low_back.defvjp(back_keep, back_low)

def rms_scale(values):
    return lax.rsqrt(lax.optimization_barrier(jnp.mean(values * values, axis=-1, keepdims=True)) + EPSILON)

def layout(lengths_row, group_rows):
    places = jnp.arange(group_rows, dtype=jnp.int32)
    first_len = lengths_row[0]
    live_end = lengths_row[0] + lengths_row[1]
    segment = (places >= first_len).astype(jnp.int32) + (places >= live_end).astype(jnp.int32)
    starts = jnp.where(segment == 0, 0, jnp.where(segment == 1, first_len, live_end))
    return (places, segment, places - starts)

def rotary(position, half_dim):
    frequency = jnp.exp(jnp.arange(half_dim, dtype=jnp.float32) * (-2.0 * jnp.log(10000.0) / (2 * half_dim)))
    angles = position.astype(jnp.float32)[:, None] * frequency[None, :]
    return (jnp.cos(angles)[:, None, :], jnp.sin(angles)[:, None, :])

def rotate(values, cosine, sine_table):
    half_dim = values.shape[-1] // 2
    upper_half = values[..., :half_dim]
    lower_half = values[..., half_dim:]
    return jnp.concatenate([upper_half * cosine - lower_half * sine_table, lower_half * cosine + upper_half * sine_table], axis=-1)

def block_forward(tokens, lengths_row, route_block, weights):
    attn_gain, qkv_weight, qk_gain, out_weight, moe_gain, router, w_gateup, w_down = weights
    group_rows = tokens.shape[0]
    model_width = tokens.shape[1]
    experts = router.shape[1]
    quarter = FF // N_TP
    places, segment, position = layout(lengths_row, group_rows)
    normed = low(tokens * rms_scale(tokens) * attn_gain)
    packed = low_back(jnp.dot(normed, qkv_weight.reshape(model_width, 3 * model_width), precision=HIGHEST)).reshape(group_rows, 3, model_width)
    queries = packed[:, 0]
    keys_raw = packed[:, 1]
    values = packed[:, 2]
    queries = queries * rms_scale(queries) * qk_gain[0]
    keys_raw = keys_raw * rms_scale(keys_raw) * qk_gain[1]
    cosine, sine_table = rotary(position, HD // 2)
    q_used = low(rotate(queries.reshape(group_rows, HEADS, HD), cosine, sine_table))
    k_used = low(rotate(keys_raw.reshape(group_rows, HEADS, HD), cosine, sine_table))
    v_used = low(values.reshape(group_rows, HEADS, HD))
    scores = low_back(jnp.einsum('qhd,khd->hqk', q_used, k_used, precision=HIGHEST)) * HD ** (-0.5)
    allowed = (segment[:, None] == segment[None, :]) & (places[None, :] <= places[:, None])
    masked = jnp.where(allowed[None], scores, -1e+30)
    top_score = lax.optimization_barrier(jnp.max(masked, axis=-1, keepdims=True))
    exponent = jnp.where(allowed[None], jnp.exp(masked - top_score), 0.0)
    softmax_weights = exponent / lax.optimization_barrier(jnp.sum(exponent, axis=-1, keepdims=True))
    attended = jnp.einsum('hqk,khd->qhd', low(softmax_weights), v_used, precision=HIGHEST).reshape(group_rows, model_width)
    attended = low(low_back(attended))
    branch = low_back(jnp.dot(attended, out_weight, precision=HIGHEST))
    hidden = tokens + branch
    moe_in = low(hidden * rms_scale(hidden) * moe_gain)
    logits = low_back(jnp.dot(moe_in, router, precision=HIGHEST))
    gate_all = jax.nn.softmax(logits, axis=-1)
    choose = route_block[:, :, None] == jnp.arange(experts, dtype=jnp.int32)[None, None, :]
    route_gates = lax.optimization_barrier(jnp.sum(jnp.where(choose, gate_all[:, None, :], 0.0), axis=-1))
    flat_choose = choose.reshape(group_rows * TOP, experts).astype(jnp.int32)
    slot_ranks = lax.optimization_barrier(jnp.sum((jnp.cumsum(flat_choose, axis=0) - 1) * flat_choose, axis=1))
    slot_of = route_block.reshape(group_rows * TOP) * CAP + slot_ranks
    owners = jnp.zeros((experts * CAP,), jnp.int32).at[slot_of].set(jnp.arange(group_rows * TOP, dtype=jnp.int32))
    filled = jnp.zeros((experts * CAP,), jnp.float32).at[slot_of].set(1.0)
    owner_rows = owners // TOP
    expert_in = moe_in[owner_rows].reshape(experts, CAP, model_width)
    slot_gate = route_gates.reshape(group_rows * TOP)[owners] * filled
    spread = low_back(jnp.broadcast_to(expert_in[:, :, None, :], (experts, CAP, N_TP, model_width)))
    inner_pre = low_back(jnp.einsum('ecqd,edgqf->ecqgf', spread, w_gateup.reshape(experts, model_width, 2, N_TP, quarter), precision=HIGHEST))
    active = low(jax.nn.silu(inner_pre[:, :, :, 0]) * inner_pre[:, :, :, 1])
    pieces = jnp.einsum('ecqf,eqfd->ecqd', active, w_down.reshape(experts, N_TP, quarter, model_width), precision=HIGHEST)
    returned = lax.optimization_barrier(jnp.sum(low(low_back(pieces)), axis=2)).reshape(experts * CAP, model_width)
    mixed = jnp.zeros((group_rows, model_width), jnp.float32).at[owner_rows].add(returned * slot_gate[:, None])
    return hidden + mixed

def reference(tokens, cotangent, routes, lengths, attn_gain, qkv_weight, qk_gain, out_weight, moe_gain, router, w_gateup, w_down):
    blocks = MICRO * N_DP
    token_blocks = tokens.astype(jnp.float32).reshape(blocks, GROUP, D)
    route_blocks = routes.reshape(blocks, GROUP, TOP)
    length_blocks = lengths.reshape(blocks, 2)
    weights = (attn_gain, qkv_weight.astype(jnp.float32), qk_gain, out_weight.astype(jnp.float32), moe_gain, router.astype(jnp.float32), w_gateup.astype(jnp.float32), w_down.astype(jnp.float32))

    def forward(token_input, weight_input):

        def one_block(items):
            return block_forward(items[0], items[1], items[2], weight_input)
        return lax.map(jax.checkpoint(one_block), (token_input, length_blocks, route_blocks))
    outputs, pullback = jax.vjp(forward, token_blocks, weights)
    places = jnp.arange(GROUP, dtype=jnp.int32)
    live = (places[None, :] < (length_blocks[:, 0] + length_blocks[:, 1])[:, None]).astype(jnp.float32)
    cot_blocks = cotangent.astype(jnp.float32).reshape(blocks, GROUP, D) * live[:, :, None]
    token_grads, weight_grads = pullback(cot_blocks)
    shape_out = (MICRO, N_DP, GROUP, D)
    return (outputs.reshape(shape_out).astype(jnp.bfloat16), token_grads.reshape(shape_out).astype(jnp.bfloat16), weight_grads[0], weight_grads[1], weight_grads[2], weight_grads[3], weight_grads[4], weight_grads[5], weight_grads[6], weight_grads[7])
```

```python
import jax
import jax.numpy as jnp
from jax import lax
from jax.sharding import PartitionSpec as P

HD = 128
EPSILON = 1e-05
LANES = 128
BF = jnp.bfloat16
F32 = jnp.float32


def rms_scale(values):
    return lax.rsqrt(jnp.mean(values * values, axis=-1, keepdims=True) + EPSILON)


def contract(left, right, left_dim, right_dim):
    return lax.dot_general(
        left, right, (((left_dim,), (right_dim,)), ((), ())), preferred_element_type=F32
    )


def rotate(values, cosine, sine, sign):
    half = values.shape[-1] // 2
    first, second = values[..., :half], values[..., half:]
    return jnp.concatenate(
        [first * cosine - sign * (second * sine), second * cosine + sign * (first * sine)], axis=-1
    )


def swap_tp(value, bits):
    size = lax.axis_size("tp")
    return lax.ppermute(value, "tp", [(i, i ^ bits) for i in range(size)])


def swap_dp(value, bits):
    size = lax.axis_size("dp")
    return lax.ppermute(value, "dp", [(i, i ^ bits) for i in range(size)])


def add_low(*terms):
    total = terms[0].astype(F32)
    for term in terms[1:]:
        total = total + term.astype(F32)
    return total


def gather_tp(rows):
    size = lax.axis_size("tp")
    return jnp.concatenate([rows] + [swap_tp(rows, k) for k in range(1, size)], axis=0)


def scatter_tp(rows):
    size = lax.axis_size("tp")
    n = rows.shape[0] // size
    return add_low(rows[:n], *[swap_tp(rows[k * n : (k + 1) * n], k) for k in range(1, size)])


def sum_tp(rows):
    size = lax.axis_size("tp")
    n = rows.shape[0] // size
    total = rows
    for k in range(1, size):
        other = swap_tp(rows, k)
        total = total + jnp.concatenate(
            [other[(j ^ k) * n : (j ^ k) * n + n] for j in range(size)], axis=0
        )
    return total


def gather_plane(rows):
    near, far = swap_tp(rows, 1), swap_tp(rows, 2)
    half = rows.shape[0] // 2
    return jnp.concatenate(
        [rows, near, far, swap_tp(near[:half], 2), swap_tp(far[half:], 1)], axis=0
    )


def gather_all(rows, partners):
    rows = jnp.concatenate([swap_dp(rows, 2 * k) if k else rows for k in partners], axis=0)
    rows = gather_plane(rows)
    return jnp.concatenate([rows, swap_dp(rows, 1)], axis=0)


def scatter_plane(rows):
    n, w = rows.shape[0] // 4, rows.shape[1] // LANES // 2 * LANES
    a, b = rows[:, :w], rows[:, w:]
    got_a = swap_tp(jnp.concatenate([a[n : 2 * n], a[3 * n :]], axis=0), 1)
    got_b = swap_tp(b[2 * n :], 2)
    sum_a = add_low(jnp.concatenate([a[:n], a[2 * n : 3 * n]], axis=0), got_a).astype(BF)
    sum_b = add_low(b[: 2 * n], got_b).astype(BF)
    end_a = add_low(sum_a[:n], swap_tp(sum_a[n:], 2))
    end_b = add_low(sum_b[:n], swap_tp(sum_b[n:], 1))
    return jnp.concatenate([end_a, end_b], axis=1).astype(BF)


def scatter_all(rows, partners):
    n = rows.shape[0] // 2
    rows = add_low(rows[:n], swap_dp(rows[n:], 1)).astype(BF)
    rows = scatter_plane(rows)
    n = rows.shape[0] // len(partners)
    pieces = [rows[i * n : (i + 1) * n] for i in range(len(partners))]
    return add_low(*[swap_dp(p, 2 * k) if k else p for p, k in zip(pieces, partners)])


def sum_dp(value):
    return lax.psum(value.astype(BF), "dp").astype(F32)


def experts_of(moe_all, cot_all, router, gate_up, down_all, local_ids):
    width, experts = router.shape
    local = len(gate_up)
    quarter = down_all.shape[0] // local
    expert_ids = jnp.arange(experts, dtype=jnp.int32)
    d_all = cot_all[:, :width]
    mask_all = cot_all[:, width : width + experts].astype(F32)
    probs_all = jax.nn.softmax(jnp.dot(moe_all, router, preferred_element_type=F32), axis=-1)
    gates_all = probs_all * mask_all
    scaled, inner_grads, gate_terms, grads = [], [], [], []
    d_active_all = contract(d_all, down_all, 1, 1)
    for e in range(local):
        here = expert_ids[None, :] == local_ids[e]
        gate = jnp.sum(jnp.where(here, gates_all, 0.0), axis=1, keepdims=True)
        picked = jnp.sum(jnp.where(here, mask_all, 0.0), axis=1, keepdims=True)
        inner = jnp.dot(moe_all, gate_up[e], preferred_element_type=F32)
        gate_pre, up_pre = inner[:, :quarter], inner[:, quarter:]
        sigmoid = jax.nn.sigmoid(gate_pre)
        silu = gate_pre * sigmoid
        active = silu * up_pre
        d_raw = d_active_all[:, e * quarter : (e + 1) * quarter]
        gate_terms.append(jnp.sum(active * d_raw, axis=1, keepdims=True) * picked)
        scaled.append((active * gate).astype(BF))
        d_active = d_raw * gate
        d_gate = d_active * up_pre * sigmoid * (1.0 + gate_pre * (1.0 - sigmoid))
        d_up = d_active * silu
        inner_grads.append(jnp.concatenate([d_gate, d_up], axis=1).astype(BF))
        grads.append(contract(moe_all, inner_grads[e], 0, 0))
    scaled = jnp.concatenate(scaled, axis=1)
    mixed_part = jnp.dot(scaled, down_all, preferred_element_type=F32).astype(BF)
    d_rows = sum(contract(inner_grads[e], gate_up[e], 1, 1) for e in range(local)).astype(BF)
    return mixed_part, d_rows, gate_terms, grads, contract(scaled, d_all, 0, 0)


def shards(
    tokens, cotangent, routes, lengths, attn_gain, qkv_weight, qk_gain, out_weight, moe_gain,
    router, w_gateup, w_down,
):
    tp_size = lax.axis_size("tp")
    dp_size = lax.axis_size("dp")
    tp_rank = lax.axis_index("tp")
    dp_rank = lax.axis_index("dp")
    micro_count, _, own_rows, width = tokens.shape
    group = own_rows * tp_size
    experts = router.shape[1]
    local = w_gateup.shape[0]
    columns = qkv_weight.shape[2]
    heads = columns // HD
    quarter = w_down.shape[1]
    score_scale = HD ** (-0.5)

    qkv_matrix = qkv_weight.reshape(width, 3 * columns)
    gate_up = [w_gateup[e].reshape(width, 2 * quarter) for e in range(local)]
    down_all = w_down.reshape(local * quarter, width)
    expert_ids = jnp.arange(experts, dtype=jnp.int32)
    local_ids = dp_rank * local + jnp.arange(local, dtype=jnp.int32)

    places = jnp.concatenate(
        [(tp_rank ^ k) * own_rows + jnp.arange(own_rows, dtype=jnp.int32) for k in range(tp_size)]
    )
    own_places = tp_rank * own_rows + jnp.arange(own_rows, dtype=jnp.int32)
    frequency = jnp.exp(
        jnp.arange(HD // 2, dtype=F32) * (-2.0 * jnp.log(10000.0) / HD)
    )

    state = []
    for m in range(micro_count):
        first_len = lengths[m, 0, 0]
        live_end = first_len + lengths[m, 0, 1]
        live_own = (own_places < live_end).astype(F32)[:, None]
        d_mixed = cotangent[m, 0].astype(F32) * live_own
        own_routes = lax.dynamic_slice_in_dim(routes[m, 0], tp_rank * own_rows, own_rows, 0)
        chosen = jnp.any(own_routes[:, :, None] == expert_ids[None, None, :], axis=1)
        mask = jnp.pad(chosen.astype(BF), ((0, 0), (0, -experts % LANES)))
        sent = jnp.concatenate([d_mixed.astype(BF), mask], axis=1)
        state.append(dict(first_len=first_len, live_end=live_end, d_mixed=d_mixed, chosen=chosen,
                          cot_sent=sent))

    grad_gate_up = [0.0] * local
    grad_down = 0.0
    grad_out = 0.0
    grad_qkv = 0.0
    grad_qk = 0.0
    grad_router = 0.0
    grad_moe_gain = 0.0
    grad_attn_gain = 0.0
    outputs, input_grads = [], []

    for m in range(micro_count):
        s = state[m]
        x_own = tokens[m, 0].astype(F32)
        x_scale = rms_scale(x_own)
        x_hat = x_own * x_scale
        normed = gather_tp((x_hat * attn_gain).astype(BF))
        packed = jnp.dot(normed, qkv_matrix, preferred_element_type=F32)
        query_raw = packed[:, :columns]
        key_raw = packed[:, columns : 2 * columns]
        value_raw = packed[:, 2 * columns :]
        squares = sum_tp(
            jnp.stack([jnp.sum(query_raw * query_raw, axis=1), jnp.sum(key_raw * key_raw, axis=1)], axis=1)
        )
        scales = lax.rsqrt(squares / width + EPSILON)
        query_scale, key_scale = scales[:, :1], scales[:, 1:]
        query_hat = query_raw * query_scale
        key_hat = key_raw * key_scale
        segment = (places >= s["first_len"]).astype(jnp.int32) + (places >= s["live_end"]).astype(jnp.int32)
        starts = jnp.where(segment == 0, 0, jnp.where(segment == 1, s["first_len"], s["live_end"]))
        angles = (places - starts).astype(F32)[:, None] * frequency[None, :]
        cosine, sine = jnp.cos(angles)[:, None, :], jnp.sin(angles)[:, None, :]
        shape = (group, heads, HD)
        query = rotate((query_hat * qk_gain[0]).reshape(shape), cosine, sine, 1.0).astype(BF)
        key = rotate((key_hat * qk_gain[1]).reshape(shape), cosine, sine, 1.0).astype(BF)
        value = value_raw.reshape(shape).astype(BF)
        allowed = (segment[:, None] == segment[None, :]) & (places[None, :] <= places[:, None])
        scores = jnp.einsum("qhd,khd->hqk", query, key, preferred_element_type=F32) * score_scale
        masked = jnp.where(allowed[None], scores, -1e30)
        top_score = jnp.max(masked, axis=-1, keepdims=True)
        exponent = jnp.where(allowed[None], jnp.exp(masked - top_score), 0.0)
        weights = exponent / jnp.sum(exponent, axis=-1, keepdims=True)
        weights_low = weights.astype(BF)
        attended = (
            jnp.einsum("hqk,khd->qhd", weights_low, value, preferred_element_type=F32)
            .reshape(group, columns)
            .astype(BF)
        )
        branch = scatter_tp(jnp.dot(attended, out_weight, preferred_element_type=F32).astype(BF))
        hidden = x_own + branch
        h_scale = rms_scale(hidden)
        h_hat = hidden * h_scale
        moe_own = (h_hat * moe_gain).astype(BF)
        s.update(x_scale=x_scale, x_hat=x_hat, normed=normed, query_hat=query_hat, key_hat=key_hat,
                 query_scale=query_scale, key_scale=key_scale, cosine=cosine, sine=sine, query=query,
                 key=key, value=value, weights=weights, weights_low=weights_low, attended=attended,
                 hidden=hidden, h_scale=h_scale, h_hat=h_hat, moe_own=moe_own)

    lanes = jnp.arange(experts + (-experts % LANES), dtype=jnp.int32)
    outer = dp_size // 2
    span = min(outer, 4)
    for m in range(micro_count):
        s = state[m]
        back = mixed = 0.0
        for first in range(0, outer, span):
            partners = range(first, first + span)
            cot_sent, moe_sent = s["cot_sent"], s["moe_own"]
            if first:
                cot_sent, moe_sent, back, mixed = lax.optimization_barrier(
                    (cot_sent, moe_sent, back, mixed)
                )
            cot_all = gather_all(cot_sent, partners)
            moe_all = gather_all(moe_sent, partners)
            mixed_part, d_rows, gate_terms, more_gate_up, more_down = experts_of(
                moe_all, cot_all, router, gate_up, down_all, local_ids
            )
            grad_gate_up = [old + new for old, new in zip(grad_gate_up, more_gate_up)]
            grad_down = grad_down + more_down
            gate_part = sum(
                jnp.where(lanes[None, :] == local_ids[e], gate_terms[e], 0.0) for e in range(local)
            ).astype(BF)
            back = back + scatter_all(jnp.concatenate([d_rows, gate_part], axis=1), partners)
            mixed = mixed + scatter_all(mixed_part, partners)
        outputs.append((s["hidden"] + mixed).astype(BF))
        s["back"] = back

    for m in range(micro_count):
        s = state[m]
        back = s["back"]
        expert_grad = back[:, :width]
        probs = jax.nn.softmax(jnp.dot(s["moe_own"], router, preferred_element_type=F32), axis=-1)
        d_choice = back[:, width : width + experts]
        d_logits = (probs * (d_choice - jnp.sum(probs * d_choice, axis=1, keepdims=True))).astype(BF)
        grad_router = grad_router + contract(s["moe_own"], d_logits, 0, 0)
        d_moe_in = expert_grad + contract(d_logits, router, 1, 1)
        h_hat = s["h_hat"]
        grad_moe_gain = grad_moe_gain + jnp.sum(d_moe_in * h_hat, axis=0)
        d_h_hat = d_moe_in * moe_gain
        d_hidden = s["d_mixed"] + s["h_scale"] * (
            d_h_hat - h_hat * jnp.mean(d_h_hat * h_hat, axis=1, keepdims=True)
        )
        d_branch = gather_tp(d_hidden.astype(BF))
        grad_out = grad_out + contract(s["attended"], d_branch, 0, 0)
        query, key, value = s["query"], s["key"], s["value"]
        shape = (group, heads, HD)
        d_attended = contract(d_branch, out_weight, 1, 1).astype(BF).reshape(shape)
        weights = s["weights"]
        d_weights = jnp.einsum("qhd,khd->hqk", d_attended, value, preferred_element_type=F32)
        row_delta = jnp.sum(weights * d_weights, axis=-1, keepdims=True)
        d_scores = (weights * (d_weights - row_delta) * score_scale).astype(BF)
        d_query = jnp.einsum("hqk,khd->qhd", d_scores, key, preferred_element_type=F32)
        d_key = jnp.einsum("hqk,qhd->khd", d_scores, query, preferred_element_type=F32)
        d_value = jnp.einsum("hqk,qhd->khd", s["weights_low"], d_attended, preferred_element_type=F32)
        d_query_norm = rotate(d_query, s["cosine"], s["sine"], -1.0).reshape(group, columns)
        d_key_norm = rotate(d_key, s["cosine"], s["sine"], -1.0).reshape(group, columns)
        grad_qk = grad_qk + jnp.stack(
            [jnp.sum(d_query_norm * s["query_hat"], axis=0), jnp.sum(d_key_norm * s["key_hat"], axis=0)]
        )
        d_query_hat = d_query_norm * qk_gain[0]
        d_key_hat = d_key_norm * qk_gain[1]
        dots = sum_tp(
            jnp.stack(
                [jnp.sum(d_query_hat * s["query_hat"], axis=1), jnp.sum(d_key_hat * s["key_hat"], axis=1)],
                axis=1,
            )
        ) / width
        d_query_raw = s["query_scale"] * (d_query_hat - s["query_hat"] * dots[:, :1])
        d_key_raw = s["key_scale"] * (d_key_hat - s["key_hat"] * dots[:, 1:])
        d_packed = jnp.concatenate(
            [d_query_raw, d_key_raw, d_value.reshape(group, columns)], axis=1
        ).astype(BF)
        grad_qkv = grad_qkv + contract(s["normed"], d_packed, 0, 0)
        d_normed = scatter_tp(contract(d_packed, qkv_matrix, 1, 1).astype(BF))
        x_hat = s["x_hat"]
        grad_attn_gain = grad_attn_gain + jnp.sum(d_normed * x_hat, axis=0)
        d_x_hat = d_normed * attn_gain
        d_tokens = d_hidden + s["x_scale"] * (
            d_x_hat - x_hat * jnp.mean(d_x_hat * x_hat, axis=1, keepdims=True)
        )
        input_grads.append(d_tokens.astype(BF))

    small = jnp.concatenate([grad_attn_gain[None], grad_moe_gain[None], grad_router.T], axis=0)
    small = lax.psum(small, ("dp", "tp"))
    return (
        jnp.stack(outputs)[:, None],
        jnp.stack(input_grads)[:, None],
        small[0],
        sum_dp(grad_qkv).reshape(qkv_weight.shape),
        lax.psum(grad_qk, "dp"),
        sum_dp(grad_out),
        small[1],
        small[2:].T,
        jnp.stack(grad_gate_up).reshape(w_gateup.shape),
        grad_down.reshape(w_down.shape),
    )


def solution(mesh):
    return jax.shard_map(
        shards,
        mesh=mesh,
        in_specs=(
            P(None, "dp", "tp", None),
            P(None, "dp", "tp", None),
            P(None, "dp", None, None),
            P(None, "dp", None),
            P(),
            P(None, None, "tp"),
            P(None, "tp"),
            P("tp", None),
            P(),
            P(),
            P("dp", None, None, "tp"),
            P("dp", "tp", None),
        ),
        out_specs=(
            P(None, "dp", "tp", None),
            P(None, "dp", "tp", None),
            P(),
            P(None, None, "tp"),
            P(None, "tp"),
            P("tp", None),
            P(),
            P(),
            P("dp", None, None, "tp"),
            P("dp", "tp", None),
        ),
        check_vma=False,
    )
```

```python
import functools

import jax
import jax.numpy as jnp
from jax import lax
from jax.experimental import pallas as pl
from jax.experimental.pallas import tpu as pltpu
from jax.sharding import PartitionSpec as P

HD = 128
EPSILON = 1e-05
LANES = 128
BF = jnp.bfloat16
F32 = jnp.float32
VMEM_BYTES = 56 * 1024 * 1024
EXPERT_TILE = 512
COST_SCALE = 8


def rms_scale(values):
    return lax.rsqrt(jnp.mean(values * values, axis=-1, keepdims=True) + EPSILON)


def contract(left, right, left_dim, right_dim):
    return lax.dot_general(
        left, right, (((left_dim,), (right_dim,)), ((), ())), preferred_element_type=F32
    )


def swap_tp(value, bits):
    size = lax.axis_size("tp")
    return lax.ppermute(value, "tp", [(i, i ^ bits) for i in range(size)])


def swap_dp(value, bits):
    size = lax.axis_size("dp")
    return lax.ppermute(value, "dp", [(i, i ^ bits) for i in range(size)])


def sync(*values):
    return lax.optimization_barrier(values)


def after(value, *deps):
    return lax.optimization_barrier((value, *deps))[0]


def add_low(*terms):
    total = terms[0].astype(F32)
    for term in terms[1:]:
        total = total + term.astype(F32)
    return total


def gather_tp(rows):
    size = lax.axis_size("tp")
    return jnp.concatenate([rows] + [swap_tp(rows, k) for k in range(1, size)], axis=-2)


def scatter_tp(rows):
    size = lax.axis_size("tp")
    n = rows.shape[-2] // size
    pieces = [rows[..., k * n : (k + 1) * n, :] for k in range(size)]
    return add_low(*[swap_tp(p, k) if k else p for k, p in enumerate(pieces)])


def scatter_tp_first(rows, later):
    size = lax.axis_size("tp")
    n = rows.shape[-2] // size
    pieces = [rows[..., k * n : (k + 1) * n, :] for k in range(size)]
    *pieces, later = lax.optimization_barrier((*pieces, later))
    return add_low(*[swap_tp(p, k) if k else p for k, p in enumerate(pieces)]), later


def sum_tp(rows):
    size = lax.axis_size("tp")
    n = rows.shape[-2] // size
    total = rows
    for k in range(1, size):
        other = swap_tp(rows, k)
        total = total + jnp.concatenate(
            [other[..., (j ^ k) * n : (j ^ k) * n + n, :] for j in range(size)], axis=-2
        )
    return total


def gather_outer(rows, partners):
    return jnp.concatenate([swap_dp(rows, 2 * k) if k else rows for k in partners], axis=-2)


def gather_plane_near(rows):
    return swap_tp(rows, 1), swap_tp(rows, 2)


def gather_plane_far(rows, near, far):
    n = rows.shape[-2] // 2

    def top(value):
        return value[..., :n, :]

    def low(value):
        return value[..., n:, :]

    sent_a, sent_b = lax.optimization_barrier((top(near), low(far)))
    far_a, far_b = swap_tp(sent_a, 2), swap_tp(sent_b, 1)
    return jnp.concatenate(
        [top(rows), top(far), top(near), far_a, low(rows), low(near), low(far), far_b], axis=-2
    )


def scatter_core(own, other):
    return add_low(own, swap_dp(other, 1)).astype(BF)


def cut(rows, count):
    n = rows.shape[-2] // count
    return [rows[..., i * n : (i + 1) * n, :] for i in range(count)]


def scatter_plane_near(rows):
    keep_a, send_a, keep_b, send_b = cut(rows, 4)
    send_a, send_b = lax.optimization_barrier((send_a, send_b))
    got_a, got_b = swap_tp(send_a, 1), swap_tp(send_b, 2)
    return add_low(keep_a, got_a).astype(BF), add_low(keep_b, got_b).astype(BF)


def scatter_plane_far(part_a, part_b):
    (keep_a, send_a), (keep_b, send_b) = cut(part_a, 2), cut(part_b, 2)
    send_a, send_b = lax.optimization_barrier((send_a, send_b))
    got_a, got_b = swap_tp(send_a, 2), swap_tp(send_b, 1)
    return add_low(keep_a, got_a).astype(BF), add_low(keep_b, got_b).astype(BF)


def scatter_outer(part_a, part_b, partners):
    half = len(partners) // 2
    pieces = cut(part_a, half) + cut(part_b, half)
    return add_low(*[swap_dp(p, 2 * k) if k else p for p, k in zip(pieces, partners)])


def sum_dp(value):
    return lax.psum(value.astype(BF), "dp").astype(F32)


def call_kernel(body, ins, outs, grid=(), in_specs=None, out_specs=None, flops=0, moved=0, **extra):
    whole = pl.BlockSpec(memory_space=pltpu.VMEM)
    return pl.pallas_call(
        body,
        out_shape=outs,
        grid=grid,
        in_specs=in_specs or [whole] * len(ins),
        out_specs=out_specs or [whole] * len(outs),
        compiler_params=pltpu.CompilerParams(vmem_limit_bytes=VMEM_BYTES),
        cost_estimate=pl.CostEstimate(
            flops=flops // COST_SCALE, bytes_accessed=moved // COST_SCALE, transcendentals=0
        ),
        **extra,
    )(*ins)


def project_kernel(rows_ref, weight_ref, packed_ref, squares_ref):
    part = pl.program_id(0)
    packed = jnp.dot(rows_ref[...], weight_ref[...], preferred_element_type=F32)
    packed_ref[...] = packed
    lane = lax.broadcasted_iota(jnp.int32, squares_ref.shape, 1)

    @pl.when(part == 0)
    def _():
        squares_ref[...] = jnp.zeros_like(squares_ref)

    @pl.when(part < 2)
    def _():
        total = jnp.sum(packed * packed, axis=1, keepdims=True)
        squares_ref[...] += jnp.where(lane == part, total, 0.0)


def project(normed, qkv_parts):
    micro, group, width = normed.shape
    columns = qkv_parts.shape[2]
    rows = micro * group
    packed, squares = call_kernel(
        project_kernel,
        (normed.reshape(rows, width), qkv_parts),
        [
            jax.ShapeDtypeStruct((rows, 3 * columns), F32),
            jax.ShapeDtypeStruct((rows, LANES), F32),
        ],
        grid=(3,),
        in_specs=[
            pl.BlockSpec((rows, width), lambda i: (0, 0)),
            pl.BlockSpec((None, width, columns), lambda i: (i, 0, 0)),
        ],
        out_specs=[
            pl.BlockSpec((rows, columns), lambda i: (0, i)),
            pl.BlockSpec((rows, LANES), lambda i: (0, 0)),
        ],
        flops=2 * rows * width * 3 * columns,
        moved=2 * width * 3 * columns,
    )
    return packed.reshape(micro, group, 3 * columns), squares.reshape(micro, group, LANES)


def attend_kernel(
    packed_ref, squares_ref, gain_ref, cos_ref, sin_ref, allowed_ref, out_weight_ref,
    used_ref, weights_ref, attended_ref, branch_ref, *, width,
):
    columns = packed_ref.shape[1] // 3
    heads = columns // HD
    cosine, sine = cos_ref[...], sin_ref[...]
    allowed = allowed_ref[...] > 0.0
    scales = lax.rsqrt(squares_ref[:, :2] / width + EPSILON)
    for h in range(heads):
        used = []
        for part in range(2):
            at = slice(part * columns + h * HD, part * columns + (h + 1) * HD)
            values = packed_ref[:, at] * scales[:, part : part + 1]
            values = values * gain_ref[part : part + 1, h * HD : (h + 1) * HD]
            values = (values * cosine + pltpu.roll(values, HD // 2, 1) * sine).astype(BF)
            used_ref[:, at] = values
            used.append(values)
        at = slice(2 * columns + h * HD, 2 * columns + (h + 1) * HD)
        value = packed_ref[:, at].astype(BF)
        used_ref[:, at] = value
        scores = contract(used[0], used[1], 1, 1) * HD ** (-0.5)
        masked = jnp.where(allowed, scores, -1e30)
        top_score = jnp.max(masked, axis=-1, keepdims=True)
        exponent = jnp.where(allowed, jnp.exp(masked - top_score), 0.0)
        weights = exponent / jnp.sum(exponent, axis=-1, keepdims=True)
        weights_ref[h] = weights
        attended_ref[:, h * HD : (h + 1) * HD] = jnp.dot(
            weights.astype(BF), value, preferred_element_type=F32
        ).astype(BF)
    branch_ref[...] = jnp.dot(
        attended_ref[...], out_weight_ref[...], preferred_element_type=F32
    ).astype(BF)


def attend(packed, squares, gain, cosine, sine, allowed, out_weight):
    micro, group = packed.shape[:2]
    columns, width = out_weight.shape
    heads = columns // HD

    def each(*shape):
        return pl.BlockSpec((None,) + shape, lambda m: (m,) + (0,) * len(shape))

    return call_kernel(
        functools.partial(attend_kernel, width=width),
        (packed, squares, gain, cosine, sine, allowed, out_weight),
        [
            jax.ShapeDtypeStruct((micro, group, 3 * columns), BF),
            jax.ShapeDtypeStruct((micro, heads, group, group), F32),
            jax.ShapeDtypeStruct((micro, group, columns), BF),
            jax.ShapeDtypeStruct((micro, group, width), BF),
        ],
        grid=(micro,),
        in_specs=[
            each(group, 3 * columns),
            each(group, LANES),
            pl.BlockSpec((2, columns), lambda m: (0, 0)),
            each(group, HD),
            each(group, HD),
            each(group, group),
            pl.BlockSpec((columns, width), lambda m: (0, 0)),
        ],
        out_specs=[
            each(group, 3 * columns),
            each(heads, group, group),
            each(group, columns),
            each(group, width),
        ],
        flops=2 * micro * group * columns * (width + 2 * group),
        moved=16 * micro * group * width,
    )


def attend_back_kernel(
    d_branch_ref, out_weight_ref, used_ref, weights_ref, packed_ref, squares_ref, gain_ref, cos_ref,
    sin_ref, d_hat_ref, d_value_ref, dots_ref, gain_grad_ref, *, width,
):
    columns = packed_ref.shape[1] // 3
    heads = columns // HD
    cosine, sine = cos_ref[...], sin_ref[...]
    scales = lax.rsqrt(squares_ref[:, :2] / width + EPSILON)
    d_attended = contract(d_branch_ref[...], out_weight_ref[...], 1, 1).astype(BF)
    dots = [0.0, 0.0]
    gain_grad_ref[...] = jnp.zeros_like(gain_grad_ref)
    for h in range(heads):
        own = slice(h * HD, (h + 1) * HD)
        query, key, value = (
            used_ref[:, part * columns + h * HD : part * columns + (h + 1) * HD] for part in range(3)
        )
        d_out = d_attended[:, own]
        weights = weights_ref[h]
        d_weights = contract(d_out, value, 1, 1)
        row_delta = jnp.sum(weights * d_weights, axis=-1, keepdims=True)
        d_scores = (weights * (d_weights - row_delta) * HD ** (-0.5)).astype(BF)
        d_value_ref[:, own] = contract(weights.astype(BF), d_out, 0, 0).astype(BF)
        grads = (
            jnp.dot(d_scores, key, preferred_element_type=F32),
            contract(d_scores, query, 0, 0),
        )
        for part in range(2):
            at = slice(part * columns + h * HD, part * columns + (h + 1) * HD)
            hat = packed_ref[:, at] * scales[:, part : part + 1]
            grad = grads[part] * cosine - pltpu.roll(grads[part], HD // 2, 1) * sine
            gain_grad_ref[part : part + 1, own] = jnp.sum(grad * hat, axis=0, keepdims=True)
            grad = grad * gain_ref[part : part + 1, own]
            d_hat_ref[:, at] = grad
            dots[part] = dots[part] + jnp.sum(grad * hat, axis=1, keepdims=True)
    lane = lax.broadcasted_iota(jnp.int32, dots_ref.shape, 1)
    dots_ref[...] = jnp.where(lane == 0, dots[0], jnp.where(lane == 1, dots[1], 0.0))


def attend_back(m, d_branch, out_weight, used, weights, packed, squares, gain, cosine, sine):
    group = packed.shape[1]
    columns, width = out_weight.shape
    heads = columns // HD

    def pick(*shape):
        return pl.BlockSpec((None,) + shape, lambda i: (m,) + (0,) * len(shape))

    def full(*shape):
        return pl.BlockSpec(shape, lambda i: (0,) * len(shape))

    return call_kernel(
        functools.partial(attend_back_kernel, width=width),
        (d_branch, out_weight, used, weights, packed, squares, gain, cosine, sine),
        [
            jax.ShapeDtypeStruct((group, 2 * columns), F32),
            jax.ShapeDtypeStruct((group, columns), BF),
            jax.ShapeDtypeStruct((group, LANES), F32),
            jax.ShapeDtypeStruct((8, columns), F32),
        ],
        grid=(1,),
        in_specs=[
            pick(group, width),
            full(columns, width),
            pick(group, 3 * columns),
            pick(heads, group, group),
            pick(group, 3 * columns),
            pick(group, LANES),
            full(2, columns),
            pick(group, HD),
            pick(group, HD),
        ],
        out_specs=[
            full(group, 2 * columns),
            full(group, columns),
            full(group, LANES),
            full(8, columns),
        ],
        flops=2 * group * columns * (width + 5 * group),
        moved=20 * group * width,
    )


def unproject_kernel(
    d_hat_ref, d_value_ref, dots_ref, packed_ref, squares_ref, weight_ref, normed_ref, d_packed_ref,
    d_normed_ref, gain_grad_ref, *, width,
):
    columns = d_value_ref.shape[1]
    scales = lax.rsqrt(squares_ref[:, :2] / width + EPSILON)
    for part in range(2):
        at = slice(part * columns, (part + 1) * columns)
        scale = scales[:, part : part + 1]
        hat = packed_ref[:, at] * scale
        mean = dots_ref[:, part : part + 1] / width
        d_packed_ref[:, at] = (scale * (d_hat_ref[:, at] - hat * mean)).astype(BF)
    d_packed_ref[:, 2 * columns :] = d_value_ref[...]
    total = 0.0
    for part in range(3):
        at = slice(part * columns, (part + 1) * columns)
        total = total + contract(d_packed_ref[:, at], weight_ref[part], 1, 1)
    d_normed_ref[...] = total.astype(BF)
    column = jnp.sum(total * normed_ref[...].astype(F32), axis=0, keepdims=True)
    gain_grad_ref[...] = jnp.broadcast_to(column, gain_grad_ref.shape)


def unproject(m, d_hat, d_value, dots, packed, squares, qkv_parts, normed):
    group, columns = d_value.shape
    width = qkv_parts.shape[1]

    def pick(*shape):
        return pl.BlockSpec((None,) + shape, lambda i: (m,) + (0,) * len(shape))

    def full(*shape):
        return pl.BlockSpec(shape, lambda i: (0,) * len(shape))

    return call_kernel(
        functools.partial(unproject_kernel, width=width),
        (d_hat, d_value, dots, packed, squares, qkv_parts, normed),
        [
            jax.ShapeDtypeStruct((group, 3 * columns), BF),
            jax.ShapeDtypeStruct((group, width), BF),
            jax.ShapeDtypeStruct((8, width), F32),
        ],
        grid=(1,),
        in_specs=[
            full(group, 2 * columns),
            full(group, columns),
            pick(group, LANES),
            pick(group, 3 * columns),
            pick(group, LANES),
            full(3, width, columns),
            pick(group, width),
        ],
        out_specs=[full(group, 3 * columns), full(group, width), full(8, width)],
        flops=2 * group * width * 3 * columns,
        moved=2 * width * 3 * columns + 8 * group * width,
    )


def rows_product_kernel(*refs, count):
    lefts, rights, starts, out_ref = refs[:count], refs[count : 2 * count], refs[2 * count : -1], refs[-1]
    total = starts[0][...] if starts else 0.0
    for left, right in zip(lefts, rights):
        total = total + contract(left[...], right[...], 0, 0)
    out_ref[...] = total


def rows_product(lefts, rights, start, tile, width, columns):
    count = len(lefts)
    rows = sum(left.shape[0] for left in lefts)
    once = pl.Buffered(1)
    starts = [] if start is None else [start]
    return call_kernel(
        functools.partial(rows_product_kernel, count=count),
        (*lefts, *rights, *starts),
        [jax.ShapeDtypeStruct((width, columns), F32)],
        grid=(width // tile,),
        in_specs=[pl.BlockSpec((left.shape[0], tile), lambda i: (0, i)) for left in lefts]
        + [
            pl.BlockSpec((right.shape[0], columns), lambda i: (0, 0), pipeline_mode=once)
            for right in rights
        ]
        + [pl.BlockSpec((tile, columns), lambda i: (i, 0)) for _ in starts],
        out_specs=[pl.BlockSpec((tile, columns), lambda i: (i, 0))],
        flops=2 * rows * width * columns,
        moved=2 * rows * (width + columns) + 4 * width * columns,
    )[0]


def qkv_product_kernel(left_ref, right_ref, out_ref):
    out_ref[...] = contract(left_ref[...], right_ref[...], 0, 0).astype(BF)


def qkv_product(normed, d_packed):
    rows, width = normed.shape
    columns = d_packed.shape[1] // 3
    tile = min(width, 1024)
    return call_kernel(
        qkv_product_kernel,
        (normed, d_packed),
        [jax.ShapeDtypeStruct((3, width, columns), BF)],
        grid=(3, width // tile),
        in_specs=[
            pl.BlockSpec((rows, tile), lambda p, i: (0, i)),
            pl.BlockSpec((rows, columns), lambda p, i: (0, p)),
        ],
        out_specs=[pl.BlockSpec((None, tile, columns), lambda p, i: (p, i, 0))],
        flops=2 * rows * width * 3 * columns,
        moved=2 * width * 3 * columns,
    )[0]


def experts_kernel(
    ids_ref, moe_ref, cot_ref, router_ref, gate_up_ref, down_ref, d_rows_ref, scaled_ref, d_inner_ref,
    *, experts, local,
):
    width = moe_ref.shape[1]
    quarter = down_ref.shape[0] // local
    rows = moe_ref[...]
    lane = lax.broadcasted_iota(jnp.int32, (rows.shape[0], LANES), 1)
    logits = jnp.dot(rows, router_ref[...], preferred_element_type=F32)
    logits = jnp.where(lane < experts, logits, -1e30)
    exponent = jnp.exp(logits - jnp.max(logits, axis=1, keepdims=True))
    probs = exponent / jnp.sum(exponent, axis=1, keepdims=True)
    mask = cot_ref[:, width:].astype(F32)
    gates = probs * mask
    back = jnp.zeros_like(probs)
    for e in range(local):
        here = lane == ids_ref[0] + e
        gate = jnp.sum(jnp.where(here, gates, 0.0), axis=1, keepdims=True)
        at = slice(e * quarter, (e + 1) * quarter)
        gate_at = slice(2 * e * quarter, (2 * e + 1) * quarter)
        up_at = slice((2 * e + 1) * quarter, (2 * e + 2) * quarter)
        d_raw = contract(cot_ref[:, :width], down_ref[at, :], 1, 1)
        gate_pre = jnp.dot(rows, gate_up_ref[:, gate_at], preferred_element_type=F32)
        up_pre = jnp.dot(rows, gate_up_ref[:, up_at], preferred_element_type=F32)
        sigmoid = 1.0 / (1.0 + jnp.exp(-gate_pre))
        silu = gate_pre * sigmoid
        active = silu * up_pre
        term = jnp.sum(active * d_raw, axis=1, keepdims=True)
        back = jnp.where(here, term, back)
        scaled_ref[:, at] = (active * gate).astype(BF)
        d_active = d_raw * gate
        d_inner_ref[:, gate_at] = (
            d_active * up_pre * sigmoid * (1.0 + gate_pre * (1.0 - sigmoid))
        ).astype(BF)
        d_inner_ref[:, up_at] = (d_active * silu).astype(BF)
    d_rows_ref[:, width:] = jnp.where(mask > 0.0, back, 0.0).astype(BF)
    d_rows_ref[:, :width] = contract(d_inner_ref[...], gate_up_ref[...], 1, 1).astype(BF)


def run_experts(first_id, moe_all, cot_all, router_wide, gate_up, down, experts, local):
    total, width = moe_all.shape
    tile = min(total, EXPERT_TILE)
    inner = gate_up.shape[1]
    once = pl.Buffered(1)
    return call_kernel(
        functools.partial(experts_kernel, experts=experts, local=local),
        (first_id, moe_all, cot_all, router_wide, gate_up, down),
        [
            jax.ShapeDtypeStruct((total, width + LANES), BF),
            jax.ShapeDtypeStruct((total, inner // 2), BF),
            jax.ShapeDtypeStruct((total, inner), BF),
        ],
        grid=(total // tile,),
        in_specs=[
            pl.BlockSpec(memory_space=pltpu.SMEM),
            pl.BlockSpec((tile, width), lambda i: (i, 0)),
            pl.BlockSpec((tile, width + LANES), lambda i: (i, 0)),
            pl.BlockSpec((width, LANES), lambda i: (0, 0), pipeline_mode=once),
            pl.BlockSpec((width, inner), lambda i: (0, 0), pipeline_mode=once),
            pl.BlockSpec((inner // 2, width), lambda i: (0, 0), pipeline_mode=once),
        ],
        out_specs=[
            pl.BlockSpec((tile, width + LANES), lambda i: (i, 0)),
            pl.BlockSpec((tile, inner // 2), lambda i: (i, 0)),
            pl.BlockSpec((tile, inner), lambda i: (i, 0)),
        ],
        flops=2 * total * width * inner * 5 // 2,
        moved=total * width * 6,
    )


def shards(
    tokens, cotangent, routes, lengths, attn_gain, qkv_weight, qk_gain, out_weight, moe_gain,
    router, w_gateup, w_down,
):
    tp_size = lax.axis_size("tp")
    dp_size = lax.axis_size("dp")
    tp_rank = lax.axis_index("tp")
    dp_rank = lax.axis_index("dp")
    micro_count, _, own_rows, width = tokens.shape
    group = own_rows * tp_size
    experts = router.shape[1]
    local = w_gateup.shape[0]
    columns = qkv_weight.shape[2]
    quarter = w_down.shape[1]

    qkv_parts = jnp.transpose(qkv_weight, (1, 0, 2))
    gate_up = jnp.concatenate([w_gateup[e].reshape(width, 2 * quarter) for e in range(local)], axis=1)
    down = w_down.reshape(local * quarter, width)
    router_wide = jnp.pad(router, ((0, 0), (0, -experts % LANES)))
    expert_ids = jnp.arange(experts, dtype=jnp.int32)
    first_id = (dp_rank * local).astype(jnp.int32).reshape(1)

    places = jnp.concatenate(
        [(tp_rank ^ k) * own_rows + jnp.arange(own_rows, dtype=jnp.int32) for k in range(tp_size)]
    )
    own_places = tp_rank * own_rows + jnp.arange(own_rows, dtype=jnp.int32)
    frequency = jnp.exp(
        jnp.arange(HD // 2, dtype=F32) * (-2.0 * jnp.log(10000.0) / HD)
    )

    first_len = lengths[:, 0, 0][:, None]
    live_end = first_len + lengths[:, 0, 1][:, None]
    live_own = (own_places[None, :] < live_end).astype(F32)[:, :, None]
    d_mixed = cotangent[:, 0].astype(F32) * live_own
    own_routes = lax.dynamic_slice_in_dim(routes[:, 0], tp_rank * own_rows, own_rows, 1)
    chosen = jnp.any(own_routes[..., None] == expert_ids, axis=2)
    mask = jnp.pad(chosen.astype(BF), ((0, 0), (0, 0), (0, -experts % LANES)))
    cot_sent = jnp.concatenate([d_mixed.astype(BF), mask], axis=2)

    grad_router = 0.0
    grad_moe_gain = 0.0

    outer = dp_size // 2
    span = min(outer, 4)
    parts = [range(first, first + span) for first in range(0, outer, span)]
    zone = parts[0]

    x_own = tokens[:, 0].astype(F32)
    x_scale = rms_scale(x_own)
    x_hat = x_own * x_scale

    def experts_of(moe_half, cot_half):
        return run_experts(first_id, moe_half, cot_half, router_wide, gate_up, down, experts, local)

    def gate_up_grads(start, moe, ran):
        inner = 2 * local * quarter
        return rows_product(moe, [r[2] for r in ran], start, 256, width, inner)

    def down_grads(start, cot, ran):
        return rows_product([r[1] for r in ran], cot, start, 256, local * quarter, width)

    def mix(ran):
        return jnp.dot(ran[1], down, preferred_element_type=F32).astype(BF)

    normed = gather_tp((x_hat * attn_gain).astype(BF))
    cot_z = [swap_dp(cot_sent, 2 * k) for k in zone[1:-1]]
    normed, cot_late = sync(normed, cot_sent)
    cot_z.append(swap_dp(cot_late, 2 * zone[-1]))

    segment = (places >= first_len).astype(jnp.int32) + (places >= live_end).astype(jnp.int32)
    starts = jnp.where(segment == 0, 0, jnp.where(segment == 1, first_len, live_end))
    angles = (places - starts).astype(F32)[:, :, None] * frequency
    cosine, sine = jnp.cos(angles), jnp.sin(angles)
    cosine = jnp.concatenate([cosine, cosine], axis=2)
    sine = jnp.concatenate([-sine, sine], axis=2)
    allowed = (segment[:, :, None] == segment[:, None, :]) & (places[None, :] <= places[:, None])

    packed, squares = project(normed, qkv_parts)
    squares = sum_tp(squares)
    used, weights, attended, branch = attend(
        packed, squares, qk_gain, cosine, sine, allowed.astype(F32), out_weight
    )
    branch, *cot_z = sync(branch, cot_sent, *cot_z)
    branch_own, cot_z = scatter_tp_first(branch, jnp.concatenate(cot_z, axis=1))
    cot_z0, cot_z1 = cot_z[0], cot_z[1]
    cot_near0 = gather_plane_near(cot_z0)
    hidden = x_own + branch_own
    h_scale = rms_scale(hidden)
    h_hat = hidden * h_scale
    moe_own = (h_hat * moe_gain).astype(BF)
    moe_z0 = gather_outer(moe_own[0], zone)

    moe_z0, moe_own1, cot_z0, cot_z1, *cot_near0 = sync(moe_z0, moe_own[1], cot_z0, cot_z1, *cot_near0)
    moe_near0 = gather_plane_near(moe_z0)
    moe_z1 = gather_outer(moe_own1, zone)

    moe_z0, moe_z1, cot_z0, cot_z1, *near = sync(moe_z0, moe_z1, cot_z0, cot_z1, *cot_near0, *moe_near0)
    cot_half0 = gather_plane_far(cot_z0, *near[:2])
    moe_half0 = gather_plane_far(moe_z0, *near[2:])

    moe_half0, cot_half0, moe_z1, cot_z1 = sync(moe_half0, cot_half0, moe_z1, cot_z1)
    moe_other0, cot_other0 = swap_dp(moe_half0, 1), swap_dp(cot_half0, 1)
    cot_near1 = gather_plane_near(cot_z1)
    own0 = experts_of(moe_half0, cot_half0)

    moe_other0, cot_other0, moe_z1, cot_z1, *rest = sync(
        moe_other0, cot_other0, moe_z1, cot_z1, *cot_near1, *own0
    )
    cot_near1, own0 = rest[:2], rest[2:]
    moe_near1 = gather_plane_near(moe_z1)
    other0 = experts_of(moe_other0, cot_other0)

    moe_z1, cot_z1, *rest = sync(moe_z1, cot_z1, *cot_near1, *moe_near1, *own0, *other0)
    own0, other0 = rest[4:7], rest[7:]
    core0 = scatter_core(own0[0], other0[0])
    cot_half1 = gather_plane_far(cot_z1, *rest[:2])
    moe_half1 = gather_plane_far(moe_z1, *rest[2:4])
    mix0 = [mix(own0), mix(other0)]
    ran0, moe0, cot0 = (own0, other0), (moe_half0, moe_other0), (cot_half0, cot_other0)
    d_gate_up = gate_up_grads(None, moe0, ran0)

    core0, cot_half1, moe_half1, d_gate_up, *mix0 = sync(core0, cot_half1, moe_half1, d_gate_up, *mix0)
    near0 = scatter_plane_near(core0)
    moe_other1, cot_other1 = swap_dp(moe_half1, 1), swap_dp(cot_half1, 1)
    mix_core0 = scatter_core(*mix0)
    own1 = experts_of(moe_half1, cot_half1)

    moe_other1, cot_other1, mix_core0, *rest = sync(moe_other1, cot_other1, mix_core0, *near0, *own1)
    near0, own1 = rest[:2], rest[2:]
    far0 = scatter_plane_far(*near0)
    other1 = experts_of(moe_other1, cot_other1)

    mix_core0, *rest = sync(mix_core0, *far0, *own1, *other1)
    far0, own1, other1 = rest[:2], rest[2:5], rest[5:]
    core1 = scatter_core(own1[0], other1[0])
    back0 = scatter_outer(*far0, zone)
    mix1 = [mix(own1), mix(other1)]
    ran1, moe1, cot1 = (own1, other1), (moe_half1, moe_other1), (cot_half1, cot_other1)
    d_down = down_grads(None, cot0, ran0)

    core1, back0, mix_core0, d_down, *mix1 = sync(core1, back0, mix_core0, d_down, *mix1)
    near1 = scatter_plane_near(core1)
    mix_core1 = scatter_core(*mix1)
    d_gate_up = gate_up_grads(d_gate_up, moe1, ran1)

    back0, mix_core0, mix_core1, d_gate_up, *near1 = sync(back0, mix_core0, mix_core1, d_gate_up, *near1)
    far1 = scatter_plane_far(*near1)
    d_down = down_grads(d_down, cot1, ran1)

    back0, mix_core0, mix_core1, d_gate_up, d_down, *far1 = sync(
        back0, mix_core0, mix_core1, d_gate_up, d_down, *far1
    )
    back1 = scatter_outer(*far1, zone)
    mix_near0 = scatter_plane_near(mix_core0)
    d_gate_up_out = d_gate_up.reshape(width, local, 2, quarter)
    d_gate_up_out = jnp.stack([d_gate_up_out[:, e] for e in range(local)])
    if len(parts) == 1:
        back1, back0, d_gate_up_out, mix_core1, *mix_near0 = sync(
            back1, back0, d_gate_up_out, mix_core1, *mix_near0
        )
    back = [back0, back1]
    more = [0.0, 0.0]
    if len(parts) > 1:
        for later in parts[1:]:
            for m in range(micro_count):
                sent, moe_sent, d_gate_up, d_down, back[m], more[m] = sync(
                    cot_sent[m], moe_own[m], d_gate_up, d_down, back[m], more[m]
                )
                halves = []
                for rows in (sent, moe_sent):
                    rows = gather_outer(rows, later)
                    rows = gather_plane_far(rows, *gather_plane_near(rows))
                    halves.append((rows, swap_dp(rows, 1)))
                cot, moe = halves
                ran = [experts_of(moe[j], cot[j]) for j in range(2)]
                d_gate_up = gate_up_grads(d_gate_up, moe, ran)
                d_down = down_grads(d_down, cot, ran)
                terms = []
                for pair in ([r[0] for r in ran], [mix(r) for r in ran]):
                    near = scatter_plane_near(scatter_core(*pair))
                    terms.append(scatter_outer(*scatter_plane_far(*near), later))
                back[m], more[m] = back[m] + terms[0], more[m] + terms[1]
        d_gate_up_out = d_gate_up.reshape(width, local, 2, quarter)
        d_gate_up_out = jnp.stack([d_gate_up_out[:, e] for e in range(local)])

    d_branches, d_hiddens = [], []
    for m in range(micro_count):
        expert_grad = back[m][:, :width]
        probs = jax.nn.softmax(jnp.dot(moe_own[m], router, preferred_element_type=F32), axis=-1)
        d_choice = back[m][:, width : width + experts]
        d_logits = (probs * (d_choice - jnp.sum(probs * d_choice, axis=1, keepdims=True))).astype(BF)
        grad_router = grad_router + contract(moe_own[m], d_logits, 0, 0)
        d_moe_in = expert_grad + contract(d_logits, router, 1, 1)
        grad_moe_gain = grad_moe_gain + jnp.sum(d_moe_in * h_hat[m], axis=0)
        d_h_hat = d_moe_in * moe_gain
        d_hiddens.append(
            d_mixed[m]
            + h_scale[m] * (d_h_hat - h_hat[m] * jnp.mean(d_h_hat * h_hat[m], axis=1, keepdims=True))
        )
    d_branch = gather_tp(jnp.stack(d_hiddens).astype(BF))
    d_branch, mix_core1, *mix_near0 = sync(d_branch, mix_core1, *mix_near0)
    backs = [
        attend_back(
            m, d_branch, out_weight, used, weights, packed, squares, qk_gain, cosine, sine
        )
        for m in range(micro_count)
    ]
    grad_qk = sum(gain_grad for _, _, _, gain_grad in backs)[:2]
    dots = sum_tp(jnp.stack([b[2] for b in backs]))
    grad_out = contract(attended.reshape(-1, columns), d_branch.reshape(-1, width), 0, 0).astype(BF)
    dots, grad_out, mix_core1, *mix_near0 = sync(dots, grad_out, mix_core1, *mix_near0)
    mix_far0 = scatter_plane_far(*mix_near0)
    mix_near1 = scatter_plane_near(mix_core1)
    ends = [
        unproject(m, *backs[m][:2], dots, packed, squares, qkv_parts, normed) for m in range(micro_count)
    ]
    d_packed = jnp.concatenate([end[0] for end in ends])
    grad_qkv = qkv_product(normed.reshape(-1, width), d_packed)
    shared = [grad_qkv[p] for p in range(3)]
    shared += [grad_out[:, i : i + columns] for i in range(0, width, columns)]
    shared, *rest = sync(jnp.concatenate(shared), *mix_far0, *mix_near1, ends[0][1], ends[1][1])
    mix_far0, mix_near1, d_normed = rest[:2], rest[2:4], rest[4:]

    shared = lax.psum_scatter(shared, "dp", scatter_dimension=0, tiled=True)
    mix_far1 = scatter_plane_far(*mix_near1)
    d_normed0 = scatter_tp(d_normed[0])
    d_normed0, d_normed1, *rest = sync(d_normed0, d_normed[1], *mix_far0, *mix_far1)
    mix_far0, mix_far1 = rest[:2], rest[2:]
    d_normed1 = scatter_tp(d_normed1)
    grad_attn_gain = sum(end[2] for end in ends)[0] / attn_gain
    wide_qk = jnp.pad(grad_qk, ((0, 0), (0, width - columns)))
    small = jnp.concatenate([grad_attn_gain[None], grad_moe_gain[None], grad_router.T], axis=0)
    d_normed0, d_normed1, small, *rest = sync(d_normed0, d_normed1, small, *mix_far0, *mix_far1)
    mix_far0, mix_far1 = rest[:2], rest[2:]
    total = small
    for k in range(1, tp_size):
        total = total + swap_tp(small, k)
    small = jnp.concatenate([total, wide_qk], axis=0)
    small = small + swap_dp(small, 1)
    input_grads = []
    for m, d_normed in enumerate((d_normed0, d_normed1)):
        d_x_hat = d_normed * attn_gain
        d_tokens = d_hiddens[m] + x_scale[m] * (
            d_x_hat - x_hat[m] * jnp.mean(d_x_hat * x_hat[m], axis=1, keepdims=True)
        )
        input_grads.append(d_tokens.astype(BF))
    shared, small, d_tokens, *rest = sync(shared, small, jnp.stack(input_grads), *mix_far0, *mix_far1)
    mix_far0, mix_far1 = rest[:2], rest[2:]
    shared = lax.all_gather(shared, "dp", axis=0, tiled=True)
    terms = [swap_dp(small, 2 * k) for k in range(1, outer)]
    small = sum(terms, small)
    mixed0 = scatter_outer(*mix_far0, zone)
    small, mixed0, *mix_far1 = sync(small, mixed0, *mix_far1)
    mixed = jnp.stack([mixed0 + more[0], scatter_outer(*mix_far1, zone) + more[1]])
    out = (hidden + mixed).astype(BF)
    shared, out = sync(shared, out)
    total_qkv = shared[: 3 * width].reshape(3, width, columns)
    total_out = shared[3 * width :].reshape(width // columns, columns, columns)
    total_out = jnp.concatenate([piece for piece in total_out], axis=1).astype(F32)
    return (
        out[:, None],
        d_tokens[:, None],
        small[0],
        jnp.transpose(total_qkv.astype(F32), (1, 0, 2)),
        small[-2:, :columns],
        total_out,
        small[1],
        small[2 : 2 + experts].T,
        d_gate_up_out.reshape(w_gateup.shape),
        d_down.reshape(w_down.shape),
    )


def solution(mesh):
    return jax.shard_map(
        shards,
        mesh=mesh,
        in_specs=(
            P(None, "dp", "tp", None),
            P(None, "dp", "tp", None),
            P(None, "dp", None, None),
            P(None, "dp", None),
            P(),
            P(None, None, "tp"),
            P(None, "tp"),
            P("tp", None),
            P(),
            P(),
            P("dp", None, None, "tp"),
            P("dp", "tp", None),
        ),
        out_specs=(
            P(None, "dp", "tp", None),
            P(None, "dp", "tp", None),
            P(),
            P(None, None, "tp"),
            P(None, "tp"),
            P("tp", None),
            P(),
            P(),
            P("dp", None, None, "tp"),
            P("dp", "tp", None),
        ),
        check_vma=False,
    )
```

```python
import functools

import jax
import jax.numpy as jnp
from jax import lax
from jax.experimental import pallas as pl
from jax.experimental.pallas import tpu as pltpu
from jax.sharding import PartitionSpec as P

HD = 128
EPSILON = 1e-05
LANES = 128
BF = jnp.bfloat16
F32 = jnp.float32
VMEM_BYTES = 56 * 1024 * 1024
EXPERT_TILE = 512
COST_SCALE = 8


def rms_scale(values):
    return lax.rsqrt(jnp.mean(values * values, axis=-1, keepdims=True) + EPSILON)


def contract(left, right, left_dim, right_dim):
    return lax.dot_general(
        left, right, (((left_dim,), (right_dim,)), ((), ())), preferred_element_type=F32
    )


def swap_tp(value, bits):
    size = lax.axis_size("tp")
    return lax.ppermute(value, "tp", [(i, i ^ bits) for i in range(size)])


def swap_dp(value, bits):
    size = lax.axis_size("dp")
    return lax.ppermute(value, "dp", [(i, i ^ bits) for i in range(size)])


def sync(*values):
    return lax.optimization_barrier(values)


def after(value, *deps):
    return lax.optimization_barrier((value, *deps))[0]


def add_low(*terms):
    total = terms[0].astype(F32)
    for term in terms[1:]:
        total = total + term.astype(F32)
    return total


def gather_tp(rows):
    size = lax.axis_size("tp")
    return jnp.concatenate([rows] + [swap_tp(rows, k) for k in range(1, size)], axis=-2)


def scatter_tp(rows):
    size = lax.axis_size("tp")
    n = rows.shape[-2] // size
    pieces = [rows[..., k * n : (k + 1) * n, :] for k in range(size)]
    return add_low(*[swap_tp(p, k) if k else p for k, p in enumerate(pieces)])


def scatter_tp_first(rows, later):
    size = lax.axis_size("tp")
    n = rows.shape[-2] // size
    pieces = [rows[..., k * n : (k + 1) * n, :] for k in range(size)]
    *pieces, later = lax.optimization_barrier((*pieces, later))
    return add_low(*[swap_tp(p, k) if k else p for k, p in enumerate(pieces)]), later


def sum_tp(rows):
    size = lax.axis_size("tp")
    n = rows.shape[-2] // size
    total = rows
    for k in range(1, size):
        other = swap_tp(rows, k)
        total = total + jnp.concatenate(
            [other[..., (j ^ k) * n : (j ^ k) * n + n, :] for j in range(size)], axis=-2
        )
    return total


def gather_outer(rows, partners):
    return jnp.concatenate([swap_dp(rows, 2 * k) if k else rows for k in partners], axis=-2)


def gather_plane_near(rows):
    return swap_tp(rows, 1), swap_tp(rows, 2)


def gather_plane_far(rows, near, far):
    n = rows.shape[-2] // 2

    def top(value):
        return value[..., :n, :]

    def low(value):
        return value[..., n:, :]

    sent_a, sent_b = lax.optimization_barrier((top(near), low(far)))
    far_a, far_b = swap_tp(sent_a, 2), swap_tp(sent_b, 1)
    return jnp.concatenate(
        [top(rows), top(far), top(near), far_a, low(rows), low(near), low(far), far_b], axis=-2
    )


def cut(rows, count):
    n = rows.shape[-2] // count
    return [rows[..., i * n : (i + 1) * n, :] for i in range(count)]


def add_pieces(left, right):
    return [add_low(one, two).astype(BF) for one, two in zip(left, right)]


def scatter_core(own, other):
    return add_pieces(cut(own, 4), cut(swap_dp(other, 1), 4))


def scatter_plane_near(quarters):
    keep_a, send_a, keep_b, send_b = quarters
    got_a, got_b = swap_tp(send_a, 1), swap_tp(send_b, 2)
    return add_pieces(cut(keep_a, 2), cut(got_a, 2)) + add_pieces(cut(keep_b, 2), cut(got_b, 2))


def scatter_plane_far(eighths, partners):
    keep_a, send_a, keep_b, send_b = eighths
    got_a, got_b = swap_tp(send_a, 2), swap_tp(send_b, 1)
    half = len(partners) // 2
    return add_pieces(cut(keep_a, half), cut(got_a, half)) + add_pieces(cut(keep_b, half), cut(got_b, half))


def scatter_outer(pieces, partners):
    return add_low(*[swap_dp(p, 2 * k) if k else p for p, k in zip(pieces, partners)])


def call_kernel(body, ins, outs, grid=(), in_specs=None, out_specs=None, flops=0, moved=0, **extra):
    whole = pl.BlockSpec(memory_space=pltpu.VMEM)
    return pl.pallas_call(
        body,
        out_shape=outs,
        grid=grid,
        in_specs=in_specs or [whole] * len(ins),
        out_specs=out_specs or [whole] * len(outs),
        compiler_params=pltpu.CompilerParams(vmem_limit_bytes=VMEM_BYTES),
        cost_estimate=pl.CostEstimate(
            flops=flops // COST_SCALE, bytes_accessed=moved // COST_SCALE, transcendentals=0
        ),
        **extra,
    )(*ins)


def project_kernel(rows_ref, gain_ref, weight_ref, normed_ref, packed_ref, squares_ref):
    part = pl.program_id(0)

    @pl.when(part == 0)
    def _():
        rows = rows_ref[...].astype(F32)
        normed_ref[...] = (rows * rms_scale(rows) * gain_ref[...]).astype(BF)
        squares_ref[...] = jnp.zeros_like(squares_ref)

    packed = jnp.dot(normed_ref[...], weight_ref[...], preferred_element_type=F32)
    packed_ref[...] = packed
    lane = lax.broadcasted_iota(jnp.int32, squares_ref.shape, 1)

    @pl.when(part < 2)
    def _():
        total = jnp.sum(packed * packed, axis=1, keepdims=True)
        squares_ref[...] += jnp.where(lane == part, total, 0.0)


def project(gathered, gain, qkv_parts):
    micro, group, width = gathered.shape
    columns = qkv_parts.shape[2]
    rows = micro * group
    normed, packed, squares = call_kernel(
        project_kernel,
        (gathered.reshape(rows, width), gain[None], qkv_parts),
        [
            jax.ShapeDtypeStruct((rows, width), BF),
            jax.ShapeDtypeStruct((rows, 3 * columns), F32),
            jax.ShapeDtypeStruct((rows, LANES), F32),
        ],
        grid=(3,),
        in_specs=[
            pl.BlockSpec((rows, width), lambda i: (0, 0)),
            pl.BlockSpec((1, width), lambda i: (0, 0)),
            pl.BlockSpec((None, width, columns), lambda i: (i, 0, 0)),
        ],
        out_specs=[
            pl.BlockSpec((rows, width), lambda i: (0, 0)),
            pl.BlockSpec((rows, columns), lambda i: (0, i)),
            pl.BlockSpec((rows, LANES), lambda i: (0, 0)),
        ],
        flops=2 * rows * width * 3 * columns,
        moved=2 * width * 3 * columns,
    )
    return (value.reshape(micro, group, -1) for value in (normed, packed, squares))


def attend_kernel(
    packed_ref, squares_ref, gain_ref, cos_ref, sin_ref, allowed_ref, out_weight_ref,
    used_ref, weights_ref, attended_ref, branch_ref, *, width,
):
    columns = packed_ref.shape[1] // 3
    heads = columns // HD
    cosine, sine = cos_ref[...], sin_ref[...]
    allowed = allowed_ref[...] > 0.0
    scales = lax.rsqrt(squares_ref[:, :2] / width + EPSILON)
    for h in range(heads):
        used = []
        for part in range(2):
            at = slice(part * columns + h * HD, part * columns + (h + 1) * HD)
            values = packed_ref[:, at] * scales[:, part : part + 1]
            values = values * gain_ref[part : part + 1, h * HD : (h + 1) * HD]
            values = (values * cosine + pltpu.roll(values, HD // 2, 1) * sine).astype(BF)
            used_ref[:, at] = values
            used.append(values)
        at = slice(2 * columns + h * HD, 2 * columns + (h + 1) * HD)
        value = packed_ref[:, at].astype(BF)
        used_ref[:, at] = value
        scores = contract(used[0], used[1], 1, 1) * HD ** (-0.5)
        masked = jnp.where(allowed, scores, -1e30)
        top_score = jnp.max(masked, axis=-1, keepdims=True)
        exponent = jnp.where(allowed, jnp.exp(masked - top_score), 0.0)
        weights = exponent / jnp.sum(exponent, axis=-1, keepdims=True)
        weights_ref[h] = weights
        attended_ref[:, h * HD : (h + 1) * HD] = jnp.dot(
            weights.astype(BF), value, preferred_element_type=F32
        ).astype(BF)
    branch_ref[...] = jnp.dot(
        attended_ref[...], out_weight_ref[...], preferred_element_type=F32
    ).astype(BF)


def attend(packed, squares, gain, cosine, sine, allowed, out_weight):
    micro, group = packed.shape[:2]
    columns, width = out_weight.shape
    heads = columns // HD

    def each(*shape):
        return pl.BlockSpec((None,) + shape, lambda m: (m,) + (0,) * len(shape))

    return call_kernel(
        functools.partial(attend_kernel, width=width),
        (packed, squares, gain, cosine, sine, allowed, out_weight),
        [
            jax.ShapeDtypeStruct((micro, group, 3 * columns), BF),
            jax.ShapeDtypeStruct((micro, heads, group, group), F32),
            jax.ShapeDtypeStruct((micro, group, columns), BF),
            jax.ShapeDtypeStruct((micro, group, width), BF),
        ],
        grid=(micro,),
        in_specs=[
            each(group, 3 * columns),
            each(group, LANES),
            pl.BlockSpec((2, columns), lambda m: (0, 0)),
            each(group, HD),
            each(group, HD),
            each(group, group),
            pl.BlockSpec((columns, width), lambda m: (0, 0)),
        ],
        out_specs=[
            each(group, 3 * columns),
            each(heads, group, group),
            each(group, columns),
            each(group, width),
        ],
        flops=2 * micro * group * columns * (width + 2 * group),
        moved=16 * micro * group * width,
    )


def attend_back_kernel(
    d_branch_ref, out_weight_ref, used_ref, weights_ref, packed_ref, squares_ref, gain_ref, cos_ref,
    sin_ref, d_hat_ref, d_value_ref, dots_ref, gain_grad_ref, *, width,
):
    columns = packed_ref.shape[1] // 3
    heads = columns // HD
    cosine, sine = cos_ref[...], sin_ref[...]
    scales = lax.rsqrt(squares_ref[:, :2] / width + EPSILON)
    d_attended = contract(d_branch_ref[...], out_weight_ref[...], 1, 1).astype(BF)
    dots = [0.0, 0.0]
    gain_grad_ref[...] = jnp.zeros_like(gain_grad_ref)
    for h in range(heads):
        own = slice(h * HD, (h + 1) * HD)
        query, key, value = (
            used_ref[:, part * columns + h * HD : part * columns + (h + 1) * HD] for part in range(3)
        )
        d_out = d_attended[:, own]
        weights = weights_ref[h]
        d_weights = contract(d_out, value, 1, 1)
        row_delta = jnp.sum(weights * d_weights, axis=-1, keepdims=True)
        d_scores = (weights * (d_weights - row_delta) * HD ** (-0.5)).astype(BF)
        d_value_ref[:, own] = contract(weights.astype(BF), d_out, 0, 0).astype(BF)
        grads = (
            jnp.dot(d_scores, key, preferred_element_type=F32),
            contract(d_scores, query, 0, 0),
        )
        for part in range(2):
            at = slice(part * columns + h * HD, part * columns + (h + 1) * HD)
            hat = packed_ref[:, at] * scales[:, part : part + 1]
            grad = grads[part] * cosine - pltpu.roll(grads[part], HD // 2, 1) * sine
            gain_grad_ref[part : part + 1, own] = jnp.sum(grad * hat, axis=0, keepdims=True)
            grad = grad * gain_ref[part : part + 1, own]
            d_hat_ref[:, at] = grad
            dots[part] = dots[part] + jnp.sum(grad * hat, axis=1, keepdims=True)
    lane = lax.broadcasted_iota(jnp.int32, dots_ref.shape, 1)
    dots_ref[...] = jnp.where(lane == 0, dots[0], jnp.where(lane == 1, dots[1], 0.0))


def attend_back(m, d_branch, out_weight, used, weights, packed, squares, gain, cosine, sine):
    group = packed.shape[1]
    columns, width = out_weight.shape
    heads = columns // HD

    def pick(*shape):
        return pl.BlockSpec((None,) + shape, lambda i: (m,) + (0,) * len(shape))

    def full(*shape):
        return pl.BlockSpec(shape, lambda i: (0,) * len(shape))

    return call_kernel(
        functools.partial(attend_back_kernel, width=width),
        (d_branch, out_weight, used, weights, packed, squares, gain, cosine, sine),
        [
            jax.ShapeDtypeStruct((group, 2 * columns), F32),
            jax.ShapeDtypeStruct((group, columns), BF),
            jax.ShapeDtypeStruct((group, LANES), F32),
            jax.ShapeDtypeStruct((8, columns), F32),
        ],
        grid=(1,),
        in_specs=[
            full(group, width),
            full(columns, width),
            pick(group, 3 * columns),
            pick(heads, group, group),
            pick(group, 3 * columns),
            pick(group, LANES),
            full(2, columns),
            pick(group, HD),
            pick(group, HD),
        ],
        out_specs=[
            full(group, 2 * columns),
            full(group, columns),
            full(group, LANES),
            full(8, columns),
        ],
        flops=2 * group * columns * (width + 5 * group),
        moved=20 * group * width,
    )


def unproject_kernel(
    d_hat_ref, d_value_ref, dots_ref, packed_ref, squares_ref, weight_ref, normed_ref, d_packed_ref,
    d_normed_ref, gain_grad_ref, *, width,
):
    columns = d_value_ref.shape[1]
    scales = lax.rsqrt(squares_ref[:, :2] / width + EPSILON)
    for part in range(2):
        at = slice(part * columns, (part + 1) * columns)
        scale = scales[:, part : part + 1]
        hat = packed_ref[:, at] * scale
        mean = dots_ref[:, part : part + 1] / width
        d_packed_ref[:, at] = (scale * (d_hat_ref[:, at] - hat * mean)).astype(BF)
    d_packed_ref[:, 2 * columns :] = d_value_ref[...]
    total = 0.0
    for part in range(3):
        at = slice(part * columns, (part + 1) * columns)
        total = total + contract(d_packed_ref[:, at], weight_ref[part], 1, 1)
    d_normed_ref[...] = total.astype(BF)
    column = jnp.sum(total * normed_ref[...].astype(F32), axis=0, keepdims=True)
    gain_grad_ref[...] = jnp.broadcast_to(column, gain_grad_ref.shape)


def unproject(m, d_hat, d_value, dots, packed, squares, qkv_parts, normed):
    group, columns = d_value.shape
    width = qkv_parts.shape[1]

    def pick(*shape):
        return pl.BlockSpec((None,) + shape, lambda i: (m,) + (0,) * len(shape))

    def full(*shape):
        return pl.BlockSpec(shape, lambda i: (0,) * len(shape))

    return call_kernel(
        functools.partial(unproject_kernel, width=width),
        (d_hat, d_value, dots, packed, squares, qkv_parts, normed),
        [
            jax.ShapeDtypeStruct((group, 3 * columns), BF),
            jax.ShapeDtypeStruct((group, width), BF),
            jax.ShapeDtypeStruct((8, width), F32),
        ],
        grid=(1,),
        in_specs=[
            full(group, 2 * columns),
            full(group, columns),
            full(group, LANES),
            pick(group, 3 * columns),
            pick(group, LANES),
            full(3, width, columns),
            pick(group, width),
        ],
        out_specs=[full(group, 3 * columns), full(group, width), full(8, width)],
        flops=2 * group * width * 3 * columns,
        moved=2 * width * 3 * columns + 8 * group * width,
    )


def rows_product_kernel(*refs, count):
    lefts, rights, starts, out_ref = refs[:count], refs[count : 2 * count], refs[2 * count : -1], refs[-1]
    total = starts[0][...] if starts else 0.0
    for left, right in zip(lefts, rights):
        total = total + contract(left[...], right[...], 0, 0)
    out_ref[...] = total


def rows_product(lefts, rights, start, tile, width, columns):
    count = len(lefts)
    rows = sum(left.shape[0] for left in lefts)
    once = pl.Buffered(1)
    starts = [] if start is None else [start]
    return call_kernel(
        functools.partial(rows_product_kernel, count=count),
        (*lefts, *rights, *starts),
        [jax.ShapeDtypeStruct((width, columns), F32)],
        grid=(width // tile,),
        in_specs=[pl.BlockSpec((left.shape[0], tile), lambda i: (0, i)) for left in lefts]
        + [
            pl.BlockSpec((right.shape[0], columns), lambda i: (0, 0), pipeline_mode=once)
            for right in rights
        ]
        + [pl.BlockSpec((tile, columns), lambda i: (i, 0)) for _ in starts],
        out_specs=[pl.BlockSpec((tile, columns), lambda i: (i, 0))],
        flops=2 * rows * width * columns,
        moved=2 * rows * (width + columns) + 4 * width * columns,
    )[0]


def shared_grads_kernel(normed_ref, d_packed0_ref, d_packed1_ref, attended_ref, d_branch0_ref, d_branch1_ref, out_ref):
    columns = attended_ref.shape[2]

    @pl.when(pl.program_id(0) < 3)
    def _():
        total = contract(normed_ref[0], d_packed0_ref[...], 0, 0)
        out_ref[...] = (total + contract(normed_ref[1], d_packed1_ref[...], 0, 0)).astype(BF)

    @pl.when(pl.program_id(0) == 3)
    def _():
        for start in range(0, out_ref.shape[0], columns):
            at = slice(start, start + columns)
            total = contract(attended_ref[0], d_branch0_ref[:, at], 0, 0)
            out_ref[at, :] = (total + contract(attended_ref[1], d_branch1_ref[:, at], 0, 0)).astype(BF)


def shared_grads(normed, d_packed, attended, d_branch):
    micro, group, width = normed.shape
    columns = attended.shape[2]
    tile = width // 2
    packed_spec = pl.BlockSpec((group, columns), lambda p, i: (0, jnp.minimum(p, 2)))
    branch_spec = pl.BlockSpec((group, tile), lambda p, i: (0, jnp.where(p == 3, i, 0)))
    return call_kernel(
        shared_grads_kernel,
        (normed, *d_packed, attended, *d_branch),
        [jax.ShapeDtypeStruct((4 * width, columns), BF)],
        grid=(4, 2),
        in_specs=[
            pl.BlockSpec((micro, group, tile), lambda p, i: (0, 0, i)),
            packed_spec,
            packed_spec,
            pl.BlockSpec((micro, group, columns), lambda p, i: (0, 0, 0)),
            branch_spec,
            branch_spec,
        ],
        out_specs=[pl.BlockSpec((tile, columns), lambda p, i: (2 * p + i, 0))],
        flops=2 * micro * group * width * 4 * columns,
        moved=2 * width * 4 * columns,
    )[0]


def experts_kernel(
    ids_ref, moe_ref, cot_ref, router_ref, gate_up_ref, down_ref, d_rows_ref, scaled_ref, d_inner_ref,
    *, experts, local,
):
    width = moe_ref.shape[1]
    quarter = down_ref.shape[0] // local
    rows = moe_ref[...]
    lane = lax.broadcasted_iota(jnp.int32, (rows.shape[0], LANES), 1)
    logits = jnp.dot(rows, router_ref[...], preferred_element_type=F32)
    logits = jnp.where(lane < experts, logits, -1e30)
    exponent = jnp.exp(logits - jnp.max(logits, axis=1, keepdims=True))
    probs = exponent / jnp.sum(exponent, axis=1, keepdims=True)
    mask = cot_ref[:, width:].astype(F32)
    gates = probs * mask
    back = jnp.zeros_like(probs)
    for e in range(local):
        here = lane == ids_ref[0] + e
        gate = jnp.sum(jnp.where(here, gates, 0.0), axis=1, keepdims=True)
        at = slice(e * quarter, (e + 1) * quarter)
        gate_at = slice(2 * e * quarter, (2 * e + 1) * quarter)
        up_at = slice((2 * e + 1) * quarter, (2 * e + 2) * quarter)
        d_raw = contract(cot_ref[:, :width], down_ref[at, :], 1, 1)
        gate_pre = jnp.dot(rows, gate_up_ref[:, gate_at], preferred_element_type=F32)
        up_pre = jnp.dot(rows, gate_up_ref[:, up_at], preferred_element_type=F32)
        sigmoid = 1.0 / (1.0 + jnp.exp(-gate_pre))
        silu = gate_pre * sigmoid
        active = silu * up_pre
        term = jnp.sum(active * d_raw, axis=1, keepdims=True)
        back = jnp.where(here, term, back)
        scaled_ref[:, at] = (active * gate).astype(BF)
        d_active = d_raw * gate
        d_inner_ref[:, gate_at] = (
            d_active * up_pre * sigmoid * (1.0 + gate_pre * (1.0 - sigmoid))
        ).astype(BF)
        d_inner_ref[:, up_at] = (d_active * silu).astype(BF)
    d_rows_ref[:, width:] = jnp.where(mask > 0.0, back, 0.0).astype(BF)
    d_rows_ref[:, :width] = contract(d_inner_ref[...], gate_up_ref[...], 1, 1).astype(BF)


def run_experts(first_id, moe_all, cot_all, router_wide, gate_up, down, experts, local):
    total, width = moe_all.shape
    tile = min(total, EXPERT_TILE)
    inner = gate_up.shape[1]
    once = pl.Buffered(1)
    return call_kernel(
        functools.partial(experts_kernel, experts=experts, local=local),
        (first_id, moe_all, cot_all, router_wide, gate_up, down),
        [
            jax.ShapeDtypeStruct((total, width + LANES), BF),
            jax.ShapeDtypeStruct((total, inner // 2), BF),
            jax.ShapeDtypeStruct((total, inner), BF),
        ],
        grid=(total // tile,),
        in_specs=[
            pl.BlockSpec(memory_space=pltpu.SMEM),
            pl.BlockSpec((tile, width), lambda i: (i, 0)),
            pl.BlockSpec((tile, width + LANES), lambda i: (i, 0)),
            pl.BlockSpec((width, LANES), lambda i: (0, 0), pipeline_mode=once),
            pl.BlockSpec((width, inner), lambda i: (0, 0), pipeline_mode=once),
            pl.BlockSpec((inner // 2, width), lambda i: (0, 0), pipeline_mode=once),
        ],
        out_specs=[
            pl.BlockSpec((tile, width + LANES), lambda i: (i, 0)),
            pl.BlockSpec((tile, inner // 2), lambda i: (i, 0)),
            pl.BlockSpec((tile, inner), lambda i: (i, 0)),
        ],
        flops=2 * total * width * inner * 5 // 2,
        moved=total * width * 6,
    )


def shards(
    tokens, cotangent, routes, lengths, attn_gain, qkv_weight, qk_gain, out_weight, moe_gain,
    router, w_gateup, w_down,
):
    tp_size = lax.axis_size("tp")
    dp_size = lax.axis_size("dp")
    tp_rank = lax.axis_index("tp")
    dp_rank = lax.axis_index("dp")
    micro_count, _, own_rows, width = tokens.shape
    group = own_rows * tp_size
    experts = router.shape[1]
    local = w_gateup.shape[0]
    columns = qkv_weight.shape[2]
    quarter = w_down.shape[1]

    qkv_parts = jnp.transpose(qkv_weight, (1, 0, 2))
    gate_up = jnp.concatenate([w_gateup[e].reshape(width, 2 * quarter) for e in range(local)], axis=1)
    down = w_down.reshape(local * quarter, width)
    router_wide = jnp.pad(router, ((0, 0), (0, -experts % LANES)))
    expert_ids = jnp.arange(experts, dtype=jnp.int32)
    first_id = (dp_rank * local).astype(jnp.int32).reshape(1)

    places = jnp.concatenate(
        [(tp_rank ^ k) * own_rows + jnp.arange(own_rows, dtype=jnp.int32) for k in range(tp_size)]
    )
    own_places = tp_rank * own_rows + jnp.arange(own_rows, dtype=jnp.int32)
    frequency = jnp.exp(
        jnp.arange(HD // 2, dtype=F32) * (-2.0 * jnp.log(10000.0) / HD)
    )

    first_len = lengths[:, 0, 0][:, None]
    live_end = first_len + lengths[:, 0, 1][:, None]
    live_own = (own_places[None, :] < live_end).astype(F32)[:, :, None]
    d_mixed = cotangent[:, 0].astype(F32) * live_own
    own_routes = lax.dynamic_slice_in_dim(routes[:, 0], tp_rank * own_rows, own_rows, 1)
    chosen = jnp.any(own_routes[..., None] == expert_ids, axis=2)
    mask = jnp.pad(chosen.astype(BF), ((0, 0), (0, 0), (0, -experts % LANES)))
    cot_sent = jnp.concatenate([d_mixed.astype(BF), mask], axis=2)


    outer = dp_size // 2
    span = min(outer, 4)
    parts = [range(first, first + span) for first in range(0, outer, span)]
    zone = parts[0]

    x_own = tokens[:, 0].astype(F32)
    x_scale = rms_scale(x_own)
    x_hat = x_own * x_scale

    def experts_of(moe_half, cot_half):
        return run_experts(first_id, moe_half, cot_half, router_wide, gate_up, down, experts, local)

    def gate_up_grads(start, moe, ran):
        inner = 2 * local * quarter
        return rows_product(moe, [r[2] for r in ran], start, 256, width, inner)

    def down_grads(start, cot, ran):
        return rows_product([r[1] for r in ran], cot, start, 256, local * quarter, width)

    def mix(ran):
        return jnp.dot(ran[1], down, preferred_element_type=F32).astype(BF)

    gathered = gather_tp(tokens[:, 0])
    cot_z = [swap_dp(cot_sent, 2 * k) for k in zone[1:-1]]
    gathered, cot_late = sync(gathered, cot_sent)
    cot_z.append(swap_dp(cot_late, 2 * zone[-1]))

    segment = (places >= first_len).astype(jnp.int32) + (places >= live_end).astype(jnp.int32)
    starts = jnp.where(segment == 0, 0, jnp.where(segment == 1, first_len, live_end))
    angles = (places - starts).astype(F32)[:, :, None] * frequency
    cosine, sine = jnp.cos(angles), jnp.sin(angles)
    cosine = jnp.concatenate([cosine, cosine], axis=2)
    sine = jnp.concatenate([-sine, sine], axis=2)
    allowed = (segment[:, :, None] == segment[:, None, :]) & (places[None, :] <= places[:, None])

    normed, packed, squares = project(gathered, attn_gain, qkv_parts)
    squares = sum_tp(squares)
    used, weights, attended, branch = attend(
        packed, squares, qk_gain, cosine, sine, allowed.astype(F32), out_weight
    )
    branch, gate_up, down, router_wide, *cot_z = sync(branch, gate_up, down, router_wide, cot_sent, *cot_z)
    branch_own, cot_z = scatter_tp_first(branch, jnp.concatenate(cot_z, axis=1))
    cot_z0, cot_z1 = cot_z[0], cot_z[1]
    cot_near0 = gather_plane_near(cot_z0)
    hidden = x_own + branch_own
    h_scale = rms_scale(hidden)
    h_hat = hidden * h_scale
    moe_own = (h_hat * moe_gain).astype(BF)
    moe_z0 = gather_outer(moe_own[0], zone)

    moe_z0, moe_own1, cot_z0, cot_z1, *cot_near0 = sync(moe_z0, moe_own[1], cot_z0, cot_z1, *cot_near0)
    moe_near0 = gather_plane_near(moe_z0)
    moe_z1 = gather_outer(moe_own1, zone)

    moe_z0, moe_z1, cot_z0, cot_z1, *near = sync(moe_z0, moe_z1, cot_z0, cot_z1, *cot_near0, *moe_near0)
    cot_half0 = gather_plane_far(cot_z0, *near[:2])
    moe_half0 = gather_plane_far(moe_z0, *near[2:])

    moe_half0, cot_half0, moe_z1, cot_z1 = sync(moe_half0, cot_half0, moe_z1, cot_z1)
    moe_other0, cot_other0 = swap_dp(moe_half0, 1), swap_dp(cot_half0, 1)
    cot_near1 = gather_plane_near(cot_z1)
    own0 = experts_of(moe_half0, cot_half0)

    moe_other0, cot_other0, moe_z1, cot_z1, *rest = sync(
        moe_other0, cot_other0, moe_z1, cot_z1, *cot_near1, *own0
    )
    cot_near1, own0 = rest[:2], rest[2:]
    moe_near1 = gather_plane_near(moe_z1)
    other0 = experts_of(moe_other0, cot_other0)

    moe_z1, cot_z1, *rest = sync(moe_z1, cot_z1, *cot_near1, *moe_near1, *own0, *other0)
    own0, other0 = rest[4:7], rest[7:]
    core0 = scatter_core(own0[0], other0[0])
    cot_half1 = gather_plane_far(cot_z1, *rest[:2])
    moe_half1 = gather_plane_far(moe_z1, *rest[2:4])
    mix0 = [mix(own0), mix(other0)]

    cot_half1, moe_half1, *rest = sync(cot_half1, moe_half1, *core0, *mix0, *own0, *other0)
    core0, mix0, own0, other0 = rest[:4], rest[4:6], rest[6:9], rest[9:]
    near0 = scatter_plane_near(core0)
    moe_other1, cot_other1 = swap_dp(moe_half1, 1), swap_dp(cot_half1, 1)
    own1 = experts_of(moe_half1, cot_half1)

    moe_other1, cot_other1, *rest = sync(moe_other1, cot_other1, *near0, *own1)
    near0, own1 = rest[:4], rest[4:]
    far0 = scatter_plane_far(near0, zone)
    other1 = experts_of(moe_other1, cot_other1)

    rest = sync(*far0, *mix0, *own1, *other1)
    far0, rest = rest[:span], rest[span:]
    mix0, own1, other1 = rest[:2], rest[2:5], rest[5:]
    core1 = scatter_core(own1[0], other1[0])
    back0 = scatter_outer(far0, zone)
    mix_core0 = scatter_core(*mix0)
    mix1 = [mix(own1), mix(other1)]

    back0, *rest = sync(back0, *core1, *mix_core0, *mix1, *own1, *other1)
    core1, mix_core0, mix1, own1, other1 = rest[:4], rest[4:8], rest[8:10], rest[10:13], rest[13:]
    near1 = scatter_plane_near(core1)
    mix_core1 = scatter_core(*mix1)

    def into_hidden(m, back):
        expert_grad = back[:, :width]
        probs = jax.nn.softmax(jnp.dot(moe_own[m], router, preferred_element_type=F32), axis=-1)
        d_choice = back[:, width : width + experts]
        d_logits = (probs * (d_choice - jnp.sum(probs * d_choice, axis=1, keepdims=True))).astype(BF)
        d_moe_in = expert_grad + contract(d_logits, router, 1, 1)
        d_h_hat = d_moe_in * moe_gain
        d_hidden = d_mixed[m] + h_scale[m] * (
            d_h_hat - h_hat[m] * jnp.mean(d_h_hat * h_hat[m], axis=1, keepdims=True)
        )
        small = (contract(moe_own[m], d_logits, 0, 0), jnp.sum(d_moe_in * h_hat[m], axis=0))
        return d_hidden, small

    def into_attention(m, d_branch):
        return attend_back(
            m, d_branch, out_weight, used, weights, packed, squares, qk_gain, cosine, sine
        )

    def into_packed(m, back, dots):
        return unproject(m, *back[:2], dots, packed, squares, qkv_parts, normed)

    ran0, moe0, cot0 = (own0, other0), (moe_half0, moe_other0), (cot_half0, cot_other0)
    ran1, moe1, cot1 = (own1, other1), (moe_half1, moe_other1), (cot_half1, cot_other1)
    whole = len(parts) == 1
    if whole:
        d_hidden0, small0 = into_hidden(0, back0)
        back0 = d_hidden0
    back0, *rest = sync(back0, *near1, *mix_core0, *mix_core1)
    near1, mix_core0, mix_core1 = rest[:4], rest[4:8], rest[8:]
    far1 = scatter_plane_far(near1, zone)
    if whole:
        d_branch0 = gather_tp(back0.astype(BF))
        d_branch0, *rest = sync(d_branch0, *far1, *mix_core0, *mix_core1)
    else:
        back0, *rest = sync(back0, *far1, *mix_core0, *mix_core1)
    far1, mix_core0, mix_core1 = rest[:span], rest[span : span + 4], rest[span + 4 :]
    back1 = scatter_outer(far1, zone)
    mix_near0 = scatter_plane_near(mix_core0)
    d_gate_up = d_down = None
    more = [0.0, 0.0]
    if whole:
        to_packed0 = into_attention(0, d_branch0)
        back1, *rest = sync(back1, *to_packed0, *mix_near0, *mix_core1)
        to_packed0, mix_near0, mix_core1 = rest[:4], rest[4:8], rest[8:]
    else:
        back = [back0, back1]
        d_gate_up = gate_up_grads(None, moe0 + moe1, ran0 + ran1)
        d_down = down_grads(None, cot0 + cot1, ran0 + ran1)
        for later in parts[1:]:
            for m in range(micro_count):
                sent, moe_sent, d_gate_up, d_down, back[m], more[m] = sync(
                    cot_sent[m], moe_own[m], d_gate_up, d_down, back[m], more[m]
                )
                halves = []
                for rows in (sent, moe_sent):
                    rows = gather_outer(rows, later)
                    rows = gather_plane_far(rows, *gather_plane_near(rows))
                    halves.append((rows, swap_dp(rows, 1)))
                cot, moe = halves
                ran = [experts_of(moe[j], cot[j]) for j in range(2)]
                d_gate_up = gate_up_grads(d_gate_up, moe, ran)
                d_down = down_grads(d_down, cot, ran)
                terms = []
                for pair in ([r[0] for r in ran], [mix(r) for r in ran]):
                    near = scatter_plane_near(scatter_core(*pair))
                    terms.append(scatter_outer(scatter_plane_far(near, later), later))
                back[m], more[m] = back[m] + terms[0], more[m] + terms[1]
        d_hidden0, small0 = into_hidden(0, back[0])
        back1 = back[1]
        d_branch0 = gather_tp(d_hidden0.astype(BF))
        to_packed0 = into_attention(0, d_branch0)

    d_hidden1, small1 = into_hidden(1, back1)
    d_branch1 = gather_tp(d_hidden1.astype(BF))
    dots0 = sum_tp(to_packed0[2])
    d_branch1, dots0, *rest = sync(d_branch1, dots0, *mix_near0, *mix_core1)
    mix_near0, mix_core1 = rest[:4], rest[4:]
    to_packed1 = into_attention(1, d_branch1)
    mix_far0 = scatter_plane_far(mix_near0, zone)
    dots1 = sum_tp(to_packed1[2])
    end0 = into_packed(0, to_packed0, dots0)
    dots1, *rest = sync(dots1, *end0, *mix_far0)
    end0, mix_far0 = rest[:3], rest[3:]
    mixed0 = scatter_outer(mix_far0, zone)
    end1 = into_packed(1, to_packed1, dots1)
    shared = shared_grads(normed, (end0[0], end1[0]), attended, (d_branch0, d_branch1))
    shared, mixed0, *rest = sync(shared, mixed0, *mix_core1, *end0[1:], *end1[1:])
    mix_core1, d_normed, attn_terms = rest[:4], (rest[4], rest[6]), (rest[5], rest[7])

    shared = lax.psum_scatter(shared, "dp", scatter_dimension=0, tiled=True)
    mix_near1 = scatter_plane_near(mix_core1)
    d_normed0 = scatter_tp(d_normed[0])
    grad_attn_gain = (attn_terms[0] + attn_terms[1])[0] / attn_gain
    grad_qk = (to_packed0[3] + to_packed1[3])[:2]
    wide_qk = jnp.pad(grad_qk, ((0, 0), (0, width - columns)))
    grad_router, grad_moe_gain = (one + two for one, two in zip(small0, small1))
    small = jnp.concatenate([grad_attn_gain[None], grad_moe_gain[None], grad_router.T], axis=0)
    small, d_normed0, d_normed1, *mix_near1 = sync(small, d_normed0, d_normed[1], *mix_near1)
    mix_far1 = scatter_plane_far(mix_near1, zone)
    total = small
    for k in range(1, tp_size):
        total = total + swap_tp(small, k)
    small = jnp.concatenate([total, wide_qk], axis=0)
    small, d_normed0, d_normed1, *mix_far1 = sync(small, d_normed0, d_normed1, *mix_far1)
    mixed1 = scatter_outer(mix_far1, zone)
    small = (small + swap_dp(small, 1)).astype(BF)
    shared, mixed1, small, d_normed0, d_normed1 = sync(shared, mixed1, small, d_normed0, d_normed1)
    shared = lax.all_gather(shared, "dp", axis=0, tiled=True)
    small = add_low(small, *[swap_dp(small, 2 * k) for k in range(1, outer)])
    d_normed1 = scatter_tp(d_normed1)
    if whole:
        d_gate_up = gate_up_grads(None, moe0 + moe1, ran0 + ran1)
        d_down = down_grads(None, cot0 + cot1, ran0 + ran1)
    input_grads = []
    for m, (d_hidden, d_rows) in enumerate(((d_hidden0, d_normed0), (d_hidden1, d_normed1))):
        d_x_hat = d_rows * attn_gain
        d_tokens = d_hidden + x_scale[m] * (
            d_x_hat - x_hat[m] * jnp.mean(d_x_hat * x_hat[m], axis=1, keepdims=True)
        )
        input_grads.append(d_tokens.astype(BF))
    mixed = jnp.stack([mixed0 + more[0], mixed1 + more[1]])
    out = (hidden + mixed).astype(BF)
    d_gate_up = d_gate_up.reshape(width, local, 2, quarter)
    d_gate_up_out = jnp.stack([d_gate_up[:, e] for e in range(local)])
    shared, small, d_tokens, out, d_gate_up_out, d_down = sync(
        shared, small, jnp.stack(input_grads), out, d_gate_up_out, d_down
    )
    total_qkv = shared[: 3 * width].reshape(3, width, columns)
    total_out = shared[3 * width :].reshape(width // columns, columns, columns)
    total_out = jnp.concatenate([piece for piece in total_out], axis=1).astype(F32)
    return (
        out[:, None],
        d_tokens[:, None],
        small[0],
        jnp.transpose(total_qkv.astype(F32), (1, 0, 2)),
        small[-2:, :columns],
        total_out,
        small[1],
        small[2 : 2 + experts].T,
        d_gate_up_out.reshape(w_gateup.shape),
        d_down.reshape(w_down.shape),
    )


def solution(mesh):
    return jax.shard_map(
        shards,
        mesh=mesh,
        in_specs=(
            P(None, "dp", "tp", None),
            P(None, "dp", "tp", None),
            P(None, "dp", None, None),
            P(None, "dp", None),
            P(),
            P(None, None, "tp"),
            P(None, "tp"),
            P("tp", None),
            P(),
            P(),
            P("dp", None, None, "tp"),
            P("dp", "tp", None),
        ),
        out_specs=(
            P(None, "dp", "tp", None),
            P(None, "dp", "tp", None),
            P(),
            P(None, None, "tp"),
            P(None, "tp"),
            P("tp", None),
            P(),
            P(),
            P("dp", None, None, "tp"),
            P("dp", "tp", None),
        ),
        check_vma=False,
    )
```

```python
import functools

import jax
import jax.numpy as jnp
from jax import lax
from jax.experimental import pallas as pl
from jax.experimental.pallas import tpu as pltpu
from jax.sharding import PartitionSpec as P

HD = 128
EPSILON = 1e-05
LANES = 128
BF = jnp.bfloat16
F32 = jnp.float32
VMEM_BYTES = 56 * 1024 * 1024
EXPERT_TILE = 256
COST_SCALE = 8


def rms_scale(values):
    return lax.rsqrt(jnp.mean(values * values, axis=-1, keepdims=True) + EPSILON)


def contract(left, right, left_dim, right_dim):
    return lax.dot_general(
        left, right, (((left_dim,), (right_dim,)), ((), ())), preferred_element_type=F32
    )


def swap_tp(value, bits):
    size = lax.axis_size("tp")
    return lax.ppermute(value, "tp", [(i, i ^ bits) for i in range(size)])


def swap_dp(value, bits):
    size = lax.axis_size("dp")
    return lax.ppermute(value, "dp", [(i, i ^ bits) for i in range(size)])


def sync(*values):
    return lax.optimization_barrier(values)


def after(value, *deps):
    return lax.optimization_barrier((value, *deps))[0]


def add_low(*terms):
    total = terms[0].astype(F32)
    for term in terms[1:]:
        total = total + term.astype(F32)
    return total


def gather_tp(rows):
    size = lax.axis_size("tp")
    return jnp.concatenate([rows] + [swap_tp(rows, k) for k in range(1, size)], axis=-2)


def scatter_tp(rows):
    size = lax.axis_size("tp")
    n = rows.shape[-2] // size
    pieces = [rows[..., k * n : (k + 1) * n, :] for k in range(size)]
    return add_low(*[swap_tp(p, k) if k else p for k, p in enumerate(pieces)])


def scatter_tp_first(rows, later):
    size = lax.axis_size("tp")
    n = rows.shape[-2] // size
    pieces = [rows[..., k * n : (k + 1) * n, :] for k in range(size)]
    *pieces, later = lax.optimization_barrier((*pieces, later))
    return add_low(*[swap_tp(p, k) if k else p for k, p in enumerate(pieces)]), later


def sum_tp(rows):
    size = lax.axis_size("tp")
    n = rows.shape[-2] // size
    total = rows
    for k in range(1, size):
        other = swap_tp(rows, k)
        total = total + jnp.concatenate(
            [other[..., (j ^ k) * n : (j ^ k) * n + n, :] for j in range(size)], axis=-2
        )
    return total


def gather_outer(rows, partners):
    return jnp.concatenate([swap_dp(rows, 2 * k) if k else rows for k in partners], axis=-2)


def gather_plane_near(rows):
    return swap_tp(rows, 1), swap_tp(rows, 2)


def gather_plane_far(rows, near, far):
    n = rows.shape[-2] // 2

    def top(value):
        return value[..., :n, :]

    def low(value):
        return value[..., n:, :]

    sent_a, sent_b = lax.optimization_barrier((top(near), low(far)))
    far_a, far_b = swap_tp(sent_a, 2), swap_tp(sent_b, 1)
    return jnp.concatenate(
        [top(rows), top(far), top(near), far_a, low(rows), low(near), low(far), far_b], axis=-2
    )


def cut(rows, count):
    n = rows.shape[-2] // count
    return [rows[..., i * n : (i + 1) * n, :] for i in range(count)]


def add_pieces(left, right):
    return [add_low(one, two).astype(BF) for one, two in zip(left, right)]


def scatter_core(own, other):
    return add_pieces(cut(own, 4), cut(swap_dp(other, 1), 4))


def scatter_plane_near(quarters):
    keep_a, send_a, keep_b, send_b = quarters
    got_a, got_b = swap_tp(send_a, 1), swap_tp(send_b, 2)
    return add_pieces(cut(keep_a, 2), cut(got_a, 2)) + add_pieces(cut(keep_b, 2), cut(got_b, 2))


def scatter_plane_far(eighths, partners):
    keep_a, send_a, keep_b, send_b = eighths
    got_a, got_b = swap_tp(send_a, 2), swap_tp(send_b, 1)
    half = len(partners) // 2
    return add_pieces(cut(keep_a, half), cut(got_a, half)) + add_pieces(cut(keep_b, half), cut(got_b, half))


def scatter_outer(pieces, partners):
    return add_low(*[swap_dp(p, 2 * k) if k else p for p, k in zip(pieces, partners)])


def scatter_pairs_near(pieces):
    own, one, two, three = pieces
    got_own, got_three = cut(swap_dp(jnp.concatenate([one, two], axis=0), 2), 2)
    return [add_low(own, got_own), add_low(three, got_three).astype(BF)]


def scatter_pairs_far(own, three):
    return own + swap_dp(three, 6).astype(F32)


def call_kernel(body, ins, outs, grid=(), in_specs=None, out_specs=None, flops=0, moved=0, **extra):
    whole = pl.BlockSpec(memory_space=pltpu.VMEM)
    return pl.pallas_call(
        body,
        out_shape=outs,
        grid=grid,
        in_specs=in_specs or [whole] * len(ins),
        out_specs=out_specs or [whole] * len(outs),
        compiler_params=pltpu.CompilerParams(vmem_limit_bytes=VMEM_BYTES),
        cost_estimate=pl.CostEstimate(
            flops=flops // COST_SCALE, bytes_accessed=moved // COST_SCALE, transcendentals=0
        ),
        **extra,
    )(*ins)


def project_kernel(rows_ref, gain_ref, weight_ref, normed_ref, packed_ref, squares_ref):
    part = pl.program_id(0)

    @pl.when(part == 0)
    def _():
        rows = rows_ref[...].astype(F32)
        normed_ref[...] = (rows * rms_scale(rows) * gain_ref[...]).astype(BF)
        squares_ref[...] = jnp.zeros_like(squares_ref)

    packed = jnp.dot(normed_ref[...], weight_ref[...], preferred_element_type=F32)
    packed_ref[...] = packed
    lane = lax.broadcasted_iota(jnp.int32, squares_ref.shape, 1)

    @pl.when(part < 2)
    def _():
        total = jnp.sum(packed * packed, axis=1, keepdims=True)
        squares_ref[...] += jnp.where(lane == part, total, 0.0)


def project(gathered, gain, qkv_parts):
    micro, group, width = gathered.shape
    columns = qkv_parts.shape[2]
    rows = micro * group
    normed, packed, squares = call_kernel(
        project_kernel,
        (gathered.reshape(rows, width), gain[None], qkv_parts),
        [
            jax.ShapeDtypeStruct((rows, width), BF),
            jax.ShapeDtypeStruct((rows, 3 * columns), F32),
            jax.ShapeDtypeStruct((rows, LANES), F32),
        ],
        grid=(3,),
        in_specs=[
            pl.BlockSpec((rows, width), lambda i: (0, 0)),
            pl.BlockSpec((1, width), lambda i: (0, 0)),
            pl.BlockSpec((None, width, columns), lambda i: (i, 0, 0)),
        ],
        out_specs=[
            pl.BlockSpec((rows, width), lambda i: (0, 0)),
            pl.BlockSpec((rows, columns), lambda i: (0, i)),
            pl.BlockSpec((rows, LANES), lambda i: (0, 0)),
        ],
        flops=2 * rows * width * 3 * columns,
        moved=2 * width * 3 * columns,
    )
    return (value.reshape(micro, group, -1) for value in (normed, packed, squares))


def attend_kernel(
    packed_ref, squares_ref, gain_ref, cos_ref, sin_ref, allowed_ref, out_weight_ref,
    used_ref, weights_ref, attended_ref, branch_ref, *, width,
):
    columns = packed_ref.shape[1] // 3
    heads = columns // HD
    cosine, sine = cos_ref[...], sin_ref[...]
    allowed = allowed_ref[...] > 0.0
    scales = lax.rsqrt(squares_ref[:, :2] / width + EPSILON)
    for h in range(heads):
        used = []
        for part in range(2):
            at = slice(part * columns + h * HD, part * columns + (h + 1) * HD)
            values = packed_ref[:, at] * scales[:, part : part + 1]
            values = values * gain_ref[part : part + 1, h * HD : (h + 1) * HD]
            values = (values * cosine + pltpu.roll(values, HD // 2, 1) * sine).astype(BF)
            used_ref[:, at] = values
            used.append(values)
        at = slice(2 * columns + h * HD, 2 * columns + (h + 1) * HD)
        value = packed_ref[:, at].astype(BF)
        used_ref[:, at] = value
        scores = contract(used[0], used[1], 1, 1) * HD ** (-0.5)
        masked = jnp.where(allowed, scores, -1e30)
        top_score = jnp.max(masked, axis=-1, keepdims=True)
        exponent = jnp.where(allowed, jnp.exp(masked - top_score), 0.0)
        weights = exponent / jnp.sum(exponent, axis=-1, keepdims=True)
        weights_ref[h] = weights
        attended_ref[:, h * HD : (h + 1) * HD] = jnp.dot(
            weights.astype(BF), value, preferred_element_type=F32
        ).astype(BF)
    branch_ref[...] = jnp.dot(
        attended_ref[...], out_weight_ref[...], preferred_element_type=F32
    ).astype(BF)


def attend(packed, squares, gain, cosine, sine, allowed, out_weight):
    micro, group = packed.shape[:2]
    columns, width = out_weight.shape
    heads = columns // HD

    def each(*shape):
        return pl.BlockSpec((None,) + shape, lambda m: (m,) + (0,) * len(shape))

    return call_kernel(
        functools.partial(attend_kernel, width=width),
        (packed, squares, gain, cosine, sine, allowed, out_weight),
        [
            jax.ShapeDtypeStruct((micro, group, 3 * columns), BF),
            jax.ShapeDtypeStruct((micro, heads, group, group), F32),
            jax.ShapeDtypeStruct((micro, group, columns), BF),
            jax.ShapeDtypeStruct((micro, group, width), BF),
        ],
        grid=(micro,),
        in_specs=[
            each(group, 3 * columns),
            each(group, LANES),
            pl.BlockSpec((2, columns), lambda m: (0, 0)),
            each(group, HD),
            each(group, HD),
            each(group, group),
            pl.BlockSpec((columns, width), lambda m: (0, 0)),
        ],
        out_specs=[
            each(group, 3 * columns),
            each(heads, group, group),
            each(group, columns),
            each(group, width),
        ],
        flops=2 * micro * group * columns * (width + 2 * group),
        moved=16 * micro * group * width,
    )


def attend_back_kernel(
    d_branch_ref, out_weight_ref, used_ref, weights_ref, packed_ref, squares_ref, gain_ref, cos_ref,
    sin_ref, d_hat_ref, d_value_ref, dots_ref, gain_grad_ref, *, width,
):
    columns = packed_ref.shape[1] // 3
    heads = columns // HD
    cosine, sine = cos_ref[...], sin_ref[...]
    scales = lax.rsqrt(squares_ref[:, :2] / width + EPSILON)
    d_attended = contract(d_branch_ref[...], out_weight_ref[...], 1, 1).astype(BF)
    dots = [0.0, 0.0]
    gain_grad_ref[...] = jnp.zeros_like(gain_grad_ref)
    for h in range(heads):
        own = slice(h * HD, (h + 1) * HD)
        query, key, value = (
            used_ref[:, part * columns + h * HD : part * columns + (h + 1) * HD] for part in range(3)
        )
        d_out = d_attended[:, own]
        weights = weights_ref[h]
        d_weights = contract(d_out, value, 1, 1)
        row_delta = jnp.sum(weights * d_weights, axis=-1, keepdims=True)
        d_scores = (weights * (d_weights - row_delta) * HD ** (-0.5)).astype(BF)
        d_value_ref[:, own] = contract(weights.astype(BF), d_out, 0, 0).astype(BF)
        grads = (
            jnp.dot(d_scores, key, preferred_element_type=F32),
            contract(d_scores, query, 0, 0),
        )
        for part in range(2):
            at = slice(part * columns + h * HD, part * columns + (h + 1) * HD)
            hat = packed_ref[:, at] * scales[:, part : part + 1]
            grad = grads[part] * cosine - pltpu.roll(grads[part], HD // 2, 1) * sine
            gain_grad_ref[part : part + 1, own] = jnp.sum(grad * hat, axis=0, keepdims=True)
            grad = grad * gain_ref[part : part + 1, own]
            d_hat_ref[:, at] = grad
            dots[part] = dots[part] + jnp.sum(grad * hat, axis=1, keepdims=True)
    lane = lax.broadcasted_iota(jnp.int32, dots_ref.shape, 1)
    dots_ref[...] = jnp.where(lane == 0, dots[0], jnp.where(lane == 1, dots[1], 0.0))


def attend_back(m, d_branch, out_weight, used, weights, packed, squares, gain, cosine, sine):
    group = packed.shape[1]
    columns, width = out_weight.shape
    heads = columns // HD

    def pick(*shape):
        return pl.BlockSpec((None,) + shape, lambda i: (m,) + (0,) * len(shape))

    def full(*shape):
        return pl.BlockSpec(shape, lambda i: (0,) * len(shape))

    return call_kernel(
        functools.partial(attend_back_kernel, width=width),
        (d_branch, out_weight, used, weights, packed, squares, gain, cosine, sine),
        [
            jax.ShapeDtypeStruct((group, 2 * columns), F32),
            jax.ShapeDtypeStruct((group, columns), BF),
            jax.ShapeDtypeStruct((group, LANES), F32),
            jax.ShapeDtypeStruct((8, columns), F32),
        ],
        grid=(1,),
        in_specs=[
            full(group, width),
            full(columns, width),
            pick(group, 3 * columns),
            pick(heads, group, group),
            pick(group, 3 * columns),
            pick(group, LANES),
            full(2, columns),
            pick(group, HD),
            pick(group, HD),
        ],
        out_specs=[
            full(group, 2 * columns),
            full(group, columns),
            full(group, LANES),
            full(8, columns),
        ],
        flops=2 * group * columns * (width + 5 * group),
        moved=20 * group * width,
    )


def unproject_kernel(
    d_hat_ref, d_value_ref, dots_ref, packed_ref, squares_ref, weight_ref, normed_ref, d_packed_ref,
    d_normed_ref, gain_grad_ref, *, width,
):
    columns = d_value_ref.shape[1]
    scales = lax.rsqrt(squares_ref[:, :2] / width + EPSILON)
    for part in range(2):
        at = slice(part * columns, (part + 1) * columns)
        scale = scales[:, part : part + 1]
        hat = packed_ref[:, at] * scale
        mean = dots_ref[:, part : part + 1] / width
        d_packed_ref[:, at] = (scale * (d_hat_ref[:, at] - hat * mean)).astype(BF)
    d_packed_ref[:, 2 * columns :] = d_value_ref[...]
    total = 0.0
    for part in range(3):
        at = slice(part * columns, (part + 1) * columns)
        total = total + contract(d_packed_ref[:, at], weight_ref[part], 1, 1)
    d_normed_ref[...] = total.astype(BF)
    column = jnp.sum(total * normed_ref[...].astype(F32), axis=0, keepdims=True)
    gain_grad_ref[...] = jnp.broadcast_to(column, gain_grad_ref.shape)


def unproject(m, d_hat, d_value, dots, packed, squares, qkv_parts, normed):
    group, columns = d_value.shape
    width = qkv_parts.shape[1]

    def pick(*shape):
        return pl.BlockSpec((None,) + shape, lambda i: (m,) + (0,) * len(shape))

    def full(*shape):
        return pl.BlockSpec(shape, lambda i: (0,) * len(shape))

    return call_kernel(
        functools.partial(unproject_kernel, width=width),
        (d_hat, d_value, dots, packed, squares, qkv_parts, normed),
        [
            jax.ShapeDtypeStruct((group, 3 * columns), BF),
            jax.ShapeDtypeStruct((group, width), BF),
            jax.ShapeDtypeStruct((8, width), F32),
        ],
        grid=(1,),
        in_specs=[
            full(group, 2 * columns),
            full(group, columns),
            full(group, LANES),
            pick(group, 3 * columns),
            pick(group, LANES),
            full(3, width, columns),
            pick(group, width),
        ],
        out_specs=[full(group, 3 * columns), full(group, width), full(8, width)],
        flops=2 * group * width * 3 * columns,
        moved=2 * width * 3 * columns + 8 * group * width,
    )


def rows_product_kernel(*refs, count):
    lefts, rights, starts, out_ref = refs[:count], refs[count : 2 * count], refs[2 * count : -1], refs[-1]
    total = starts[0][...] if starts else 0.0
    for left, right in zip(lefts, rights):
        total = total + contract(left[...], right[...], 0, 0)
    out_ref[...] = total


def rows_product(lefts, rights, start, tile, width, columns):
    count = len(lefts)
    rows = sum(left.shape[0] for left in lefts)
    once = pl.Buffered(1)
    starts = [] if start is None else [start]
    return call_kernel(
        functools.partial(rows_product_kernel, count=count),
        (*lefts, *rights, *starts),
        [jax.ShapeDtypeStruct((width, columns), F32)],
        grid=(width // tile,),
        in_specs=[pl.BlockSpec((left.shape[0], tile), lambda i: (0, i)) for left in lefts]
        + [
            pl.BlockSpec((right.shape[0], columns), lambda i: (0, 0), pipeline_mode=once)
            for right in rights
        ]
        + [pl.BlockSpec((tile, columns), lambda i: (i, 0)) for _ in starts],
        out_specs=[pl.BlockSpec((tile, columns), lambda i: (i, 0))],
        flops=2 * rows * width * columns,
        moved=2 * rows * (width + columns) + 4 * width * columns,
    )[0]


def rows_pair(left0_ref, left1_ref, right0, right1):
    return (contract(left0_ref[...], right0, 0, 0) + contract(left1_ref[...], right1, 0, 0)).astype(BF)


def early_grads_kernel(
    normed0_ref, normed1_ref, d_value0_ref, d_value1_ref, attended0_ref, attended1_ref, d_branch0_ref,
    d_branch1_ref, out_ref,
):
    columns = attended0_ref.shape[1]

    @pl.when(pl.program_id(0) == 0)
    def _():
        out_ref[...] = rows_pair(normed0_ref, normed1_ref, d_value0_ref[...], d_value1_ref[...])

    @pl.when(pl.program_id(0) == 1)
    def _():
        for start in range(0, out_ref.shape[0], columns):
            at = slice(start, start + columns)
            out_ref[at, :] = rows_pair(
                attended0_ref, attended1_ref, d_branch0_ref[:, at], d_branch1_ref[:, at]
            )


def early_grads(normed, d_value, attended, d_branch):
    micro, group, width = normed.shape
    columns = attended.shape[2]
    tile = width // 2
    normed_specs = [pl.BlockSpec((None, group, tile), lambda p, i, m=m: (m, 0, i)) for m in range(micro)]
    value_spec = pl.BlockSpec((group, columns), lambda p, i: (0, 0))
    attended_specs = [pl.BlockSpec((None, group, columns), lambda p, i, m=m: (m, 0, 0)) for m in range(micro)]
    branch_spec = pl.BlockSpec((group, tile), lambda p, i: (0, jnp.where(p == 1, i, 0)))
    return call_kernel(
        early_grads_kernel,
        (normed, normed, *d_value, attended, attended, *d_branch),
        [jax.ShapeDtypeStruct((2 * width, columns), BF)],
        grid=(2, 2),
        in_specs=normed_specs + [value_spec] * 2 + attended_specs + [branch_spec] * 2,
        out_specs=[pl.BlockSpec((tile, columns), lambda p, i: (2 * p + i, 0))],
        flops=2 * micro * group * width * 2 * columns,
        moved=2 * width * 2 * columns,
    )[0]


def late_grads_kernel(normed0_ref, normed1_ref, d_packed0_ref, d_packed1_ref, out_ref):
    out_ref[...] = rows_pair(normed0_ref, normed1_ref, d_packed0_ref[...], d_packed1_ref[...])


def late_grads(normed, d_packed):
    micro, group, width = normed.shape
    columns = d_packed[0].shape[1] // 3
    tile = width // 2
    normed_specs = [pl.BlockSpec((None, group, tile), lambda i, p, m=m: (m, 0, i)) for m in range(micro)]
    return call_kernel(
        late_grads_kernel,
        (normed, normed, *d_packed),
        [jax.ShapeDtypeStruct((2 * width, columns), BF)],
        grid=(2, 2),
        in_specs=normed_specs + [pl.BlockSpec((group, columns), lambda i, p: (0, p))] * 2,
        out_specs=[pl.BlockSpec((tile, columns), lambda i, p: (2 * p + i, 0))],
        flops=2 * micro * group * width * 2 * columns,
        moved=2 * width * 2 * columns,
    )[0]


def experts_kernel(
    ids_ref, moe_ref, cot_ref, router_ref, gate_up_ref, down_ref, d_rows_ref, scaled_ref, d_inner_ref,
    *, experts, local,
):
    width = moe_ref.shape[1]
    quarter = down_ref.shape[0] // local
    rows = moe_ref[...]
    lane = lax.broadcasted_iota(jnp.int32, (rows.shape[0], LANES), 1)
    logits = jnp.dot(rows, router_ref[...], preferred_element_type=F32)
    logits = jnp.where(lane < experts, logits, -1e30)
    exponent = jnp.exp(logits - jnp.max(logits, axis=1, keepdims=True))
    probs = exponent / jnp.sum(exponent, axis=1, keepdims=True)
    mask = cot_ref[:, width:].astype(F32)
    gates = probs * mask
    back = jnp.zeros_like(probs)
    for e in range(local):
        here = lane == ids_ref[0] + e
        gate = jnp.sum(jnp.where(here, gates, 0.0), axis=1, keepdims=True)
        at = slice(e * quarter, (e + 1) * quarter)
        gate_at = slice(2 * e * quarter, (2 * e + 1) * quarter)
        up_at = slice((2 * e + 1) * quarter, (2 * e + 2) * quarter)
        d_raw = contract(cot_ref[:, :width], down_ref[at, :], 1, 1)
        gate_pre = jnp.dot(rows, gate_up_ref[:, gate_at], preferred_element_type=F32)
        up_pre = jnp.dot(rows, gate_up_ref[:, up_at], preferred_element_type=F32)
        sigmoid = 1.0 / (1.0 + jnp.exp(-gate_pre))
        silu = gate_pre * sigmoid
        active = silu * up_pre
        term = jnp.sum(active * d_raw, axis=1, keepdims=True)
        back = jnp.where(here, term, back)
        scaled_ref[:, at] = (active * gate).astype(BF)
        d_active = d_raw * gate
        d_inner_ref[:, gate_at] = (
            d_active * up_pre * sigmoid * (1.0 + gate_pre * (1.0 - sigmoid))
        ).astype(BF)
        d_inner_ref[:, up_at] = (d_active * silu).astype(BF)
    d_rows_ref[:, width:] = jnp.where(mask > 0.0, back, 0.0).astype(BF)
    d_rows_ref[:, :width] = contract(d_inner_ref[...], gate_up_ref[...], 1, 1).astype(BF)


def run_experts(first_id, moe_all, cot_all, router_wide, gate_up, down, experts, local):
    total, width = moe_all.shape
    tile = min(total, EXPERT_TILE)
    inner = gate_up.shape[1]
    once = pl.Buffered(1)
    return call_kernel(
        functools.partial(experts_kernel, experts=experts, local=local),
        (first_id, moe_all, cot_all, router_wide, gate_up, down),
        [
            jax.ShapeDtypeStruct((total, width + LANES), BF),
            jax.ShapeDtypeStruct((total, inner // 2), BF),
            jax.ShapeDtypeStruct((total, inner), BF),
        ],
        grid=(total // tile,),
        in_specs=[
            pl.BlockSpec(memory_space=pltpu.SMEM),
            pl.BlockSpec((tile, width), lambda i: (i, 0)),
            pl.BlockSpec((tile, width + LANES), lambda i: (i, 0)),
            pl.BlockSpec((width, LANES), lambda i: (0, 0), pipeline_mode=once),
            pl.BlockSpec((width, inner), lambda i: (0, 0), pipeline_mode=once),
            pl.BlockSpec((inner // 2, width), lambda i: (0, 0), pipeline_mode=once),
        ],
        out_specs=[
            pl.BlockSpec((tile, width + LANES), lambda i: (i, 0)),
            pl.BlockSpec((tile, inner // 2), lambda i: (i, 0)),
            pl.BlockSpec((tile, inner), lambda i: (i, 0)),
        ],
        flops=2 * total * width * inner * 5 // 2,
        moved=total * width * 6,
    )


def shards(
    tokens, cotangent, routes, lengths, attn_gain, qkv_weight, qk_gain, out_weight, moe_gain,
    router, w_gateup, w_down,
):
    tp_size = lax.axis_size("tp")
    dp_size = lax.axis_size("dp")
    tp_rank = lax.axis_index("tp")
    dp_rank = lax.axis_index("dp")
    micro_count, _, own_rows, width = tokens.shape
    group = own_rows * tp_size
    experts = router.shape[1]
    local = w_gateup.shape[0]
    columns = qkv_weight.shape[2]
    quarter = w_down.shape[1]

    qkv_parts = jnp.transpose(qkv_weight, (1, 0, 2))
    gate_up = jnp.concatenate([w_gateup[e].reshape(width, 2 * quarter) for e in range(local)], axis=1)
    down = w_down.reshape(local * quarter, width)
    router_wide = jnp.pad(router, ((0, 0), (0, -experts % LANES)))
    expert_ids = jnp.arange(experts, dtype=jnp.int32)
    first_id = (dp_rank * local).astype(jnp.int32).reshape(1)

    places = jnp.concatenate(
        [(tp_rank ^ k) * own_rows + jnp.arange(own_rows, dtype=jnp.int32) for k in range(tp_size)]
    )
    own_places = tp_rank * own_rows + jnp.arange(own_rows, dtype=jnp.int32)
    frequency = jnp.exp(
        jnp.arange(HD // 2, dtype=F32) * (-2.0 * jnp.log(10000.0) / HD)
    )

    first_len = lengths[:, 0, 0][:, None]
    live_end = first_len + lengths[:, 0, 1][:, None]
    live_own = (own_places[None, :] < live_end).astype(F32)[:, :, None]
    d_mixed = cotangent[:, 0].astype(F32) * live_own
    own_routes = lax.dynamic_slice_in_dim(routes[:, 0], tp_rank * own_rows, own_rows, 1)
    chosen = jnp.any(own_routes[..., None] == expert_ids, axis=2)
    mask = jnp.pad(chosen.astype(BF), ((0, 0), (0, 0), (0, -experts % LANES)))
    cot_sent = jnp.concatenate([d_mixed.astype(BF), mask], axis=2)


    outer = dp_size // 2
    span = min(outer, 4)
    parts = [range(first, first + span) for first in range(0, outer, span)]
    zone = parts[0]

    x_own = tokens[:, 0].astype(F32)
    x_scale = rms_scale(x_own)
    x_hat = x_own * x_scale

    def experts_of(moe_half, cot_half):
        return run_experts(first_id, moe_half, cot_half, router_wide, gate_up, down, experts, local)

    def gate_up_grads(start, moe, ran):
        inner = 2 * local * quarter
        return rows_product(moe, [r[2] for r in ran], start, 256, width, inner)

    def down_grads(start, cot, ran):
        return rows_product([r[1] for r in ran], cot, start, 256, local * quarter, width)

    def mix(ran):
        return jnp.dot(ran[1], down, preferred_element_type=F32).astype(BF)

    gathered = gather_tp(tokens[:, 0])
    cot_z = [swap_dp(cot_sent, 2 * k) for k in zone[1:-1]]
    gathered, cot_late = sync(gathered, cot_sent)
    cot_z.append(swap_dp(cot_late, 2 * zone[-1]))

    segment = (places >= first_len).astype(jnp.int32) + (places >= live_end).astype(jnp.int32)
    starts = jnp.where(segment == 0, 0, jnp.where(segment == 1, first_len, live_end))
    angles = (places - starts).astype(F32)[:, :, None] * frequency
    cosine, sine = jnp.cos(angles), jnp.sin(angles)
    cosine = jnp.concatenate([cosine, cosine], axis=2)
    sine = jnp.concatenate([-sine, sine], axis=2)
    allowed = (segment[:, :, None] == segment[:, None, :]) & (places[None, :] <= places[:, None])

    normed, packed, squares = project(gathered, attn_gain, qkv_parts)
    squares = sum_tp(squares)
    used, weights, attended, branch = attend(
        packed, squares, qk_gain, cosine, sine, allowed.astype(F32), out_weight
    )
    branch, gate_up, down, router_wide, *cot_z = sync(branch, gate_up, down, router_wide, cot_sent, *cot_z)
    branch_own, cot_z = scatter_tp_first(branch, jnp.concatenate(cot_z, axis=1))
    cot_z0, cot_z1 = cot_z[0], cot_z[1]
    cot_near0 = gather_plane_near(cot_z0)
    hidden = x_own + branch_own
    h_scale = rms_scale(hidden)
    h_hat = hidden * h_scale
    moe_own = (h_hat * moe_gain).astype(BF)
    moe_z0 = gather_outer(moe_own[0], zone)

    moe_z0, moe_own1, cot_z0, cot_z1, *cot_near0 = sync(moe_z0, moe_own[1], cot_z0, cot_z1, *cot_near0)
    moe_near0 = gather_plane_near(moe_z0)
    moe_z1 = gather_outer(moe_own1, zone)

    moe_z0, moe_z1, cot_z0, cot_z1, *near = sync(moe_z0, moe_z1, cot_z0, cot_z1, *cot_near0, *moe_near0)
    cot_half0 = gather_plane_far(cot_z0, *near[:2])
    moe_half0 = gather_plane_far(moe_z0, *near[2:])

    moe_half0, cot_half0, moe_z1, cot_z1 = sync(moe_half0, cot_half0, moe_z1, cot_z1)
    moe_other0, cot_other0 = swap_dp(moe_half0, 1), swap_dp(cot_half0, 1)
    cot_near1 = gather_plane_near(cot_z1)
    own0 = experts_of(moe_half0, cot_half0)

    moe_other0, cot_other0, moe_z1, cot_z1, *rest = sync(
        moe_other0, cot_other0, moe_z1, cot_z1, *cot_near1, *own0
    )
    cot_near1, own0 = rest[:2], rest[2:]
    moe_near1 = gather_plane_near(moe_z1)
    other0 = experts_of(moe_other0, cot_other0)

    moe_z1, cot_z1, *rest = sync(moe_z1, cot_z1, *cot_near1, *moe_near1, *own0, *other0)
    own0, other0 = rest[4:7], rest[7:]
    core0 = scatter_core(own0[0], other0[0])
    cot_half1 = gather_plane_far(cot_z1, *rest[:2])
    moe_half1 = gather_plane_far(moe_z1, *rest[2:4])
    mix0 = [mix(own0), mix(other0)]

    cot_half1, moe_half1, *rest = sync(cot_half1, moe_half1, *core0, *mix0, *own0, *other0)
    core0, mix0, own0, other0 = rest[:4], rest[4:6], rest[6:9], rest[9:]
    near0 = scatter_plane_near(core0)
    moe_other1, cot_other1 = swap_dp(moe_half1, 1), swap_dp(cot_half1, 1)
    own1 = experts_of(moe_half1, cot_half1)

    moe_other1, cot_other1, *rest = sync(moe_other1, cot_other1, *near0, *own1)
    near0, own1 = rest[:4], rest[4:]
    far0 = scatter_plane_far(near0, zone)
    other1 = experts_of(moe_other1, cot_other1)

    rest = sync(*far0, *mix0, *own1, *other1)
    far0, rest = rest[:span], rest[span:]
    mix0, own1, other1 = rest[:2], rest[2:5], rest[5:]
    core1 = scatter_core(own1[0], other1[0])
    back0 = scatter_outer(far0, zone)
    mix_core0 = scatter_core(*mix0)
    mix1 = [mix(own1), mix(other1)]

    back0, *rest = sync(back0, *core1, *mix_core0, *mix1, *own1, *other1)
    core1, mix_core0, mix1, own1, other1 = rest[:4], rest[4:8], rest[8:10], rest[10:13], rest[13:]
    near1 = scatter_plane_near(core1)
    mix_core1 = scatter_core(*mix1)

    def into_hidden(m, back):
        expert_grad = back[:, :width]
        probs = jax.nn.softmax(jnp.dot(moe_own[m], router, preferred_element_type=F32), axis=-1)
        d_choice = back[:, width : width + experts]
        d_logits = (probs * (d_choice - jnp.sum(probs * d_choice, axis=1, keepdims=True))).astype(BF)
        d_moe_in = expert_grad + contract(d_logits, router, 1, 1)
        d_h_hat = d_moe_in * moe_gain
        d_hidden = d_mixed[m] + h_scale[m] * (
            d_h_hat - h_hat[m] * jnp.mean(d_h_hat * h_hat[m], axis=1, keepdims=True)
        )
        small = (contract(moe_own[m], d_logits, 0, 0), jnp.sum(d_moe_in * h_hat[m], axis=0))
        return d_hidden, small

    def into_attention(m, d_branch):
        return attend_back(
            m, d_branch, out_weight, used, weights, packed, squares, qk_gain, cosine, sine
        )

    def into_packed(m, back, dots):
        return unproject(m, *back[:2], dots, packed, squares, qkv_parts, normed)

    ran0, moe0, cot0 = (own0, other0), (moe_half0, moe_other0), (cot_half0, cot_other0)
    ran1, moe1, cot1 = (own1, other1), (moe_half1, moe_other1), (cot_half1, cot_other1)
    whole = len(parts) == 1
    if whole:
        d_hidden0, small0 = into_hidden(0, back0)
        back0 = d_hidden0
    back0, *rest = sync(back0, *near1, *mix_core0, *mix_core1)
    near1, mix_core0, mix_core1 = rest[:4], rest[4:8], rest[8:]
    far1 = scatter_plane_far(near1, zone)
    if whole:
        d_branch0 = gather_tp(back0.astype(BF))
        d_branch0, *rest = sync(d_branch0, *far1, *mix_core0, *mix_core1)
    else:
        back0, *rest = sync(back0, *far1, *mix_core0, *mix_core1)
    far1, mix_core0, mix_core1 = rest[:span], rest[span : span + 4], rest[span + 4 :]
    back1 = scatter_outer(far1, zone)
    mix_near0 = scatter_plane_near(mix_core0)
    d_gate_up = d_down = None
    more = [0.0, 0.0]
    if whole:
        to_packed0 = into_attention(0, d_branch0)
        back1, *rest = sync(back1, *to_packed0, *mix_near0, *mix_core1)
        to_packed0, mix_near0, mix_core1 = rest[:4], rest[4:8], rest[8:]
    else:
        back = [back0, back1]
        d_gate_up = gate_up_grads(None, moe0 + moe1, ran0 + ran1)
        d_down = down_grads(None, cot0 + cot1, ran0 + ran1)
        for later in parts[1:]:
            for m in range(micro_count):
                sent, moe_sent, d_gate_up, d_down, back[m], more[m] = sync(
                    cot_sent[m], moe_own[m], d_gate_up, d_down, back[m], more[m]
                )
                halves = []
                for rows in (sent, moe_sent):
                    rows = gather_outer(rows, later)
                    rows = gather_plane_far(rows, *gather_plane_near(rows))
                    halves.append((rows, swap_dp(rows, 1)))
                cot, moe = halves
                ran = [experts_of(moe[j], cot[j]) for j in range(2)]
                d_gate_up = gate_up_grads(d_gate_up, moe, ran)
                d_down = down_grads(d_down, cot, ran)
                terms = []
                for pair in ([r[0] for r in ran], [mix(r) for r in ran]):
                    near = scatter_plane_near(scatter_core(*pair))
                    terms.append(scatter_outer(scatter_plane_far(near, later), later))
                back[m], more[m] = back[m] + terms[0], more[m] + terms[1]
        d_hidden0, small0 = into_hidden(0, back[0])
        back1 = back[1]
        d_branch0 = gather_tp(d_hidden0.astype(BF))
        to_packed0 = into_attention(0, d_branch0)

    d_hidden1, small1 = into_hidden(1, back1)
    d_branch1 = gather_tp(d_hidden1.astype(BF))
    dots0 = sum_tp(to_packed0[2])
    d_branch1, dots0, *rest = sync(d_branch1, dots0, *mix_near0, *mix_core1)
    mix_near0, mix_core1 = rest[:4], rest[4:]
    to_packed1 = into_attention(1, d_branch1)
    mix_far0 = scatter_plane_far(mix_near0, zone)
    dots1 = sum_tp(to_packed1[2])
    d_value = (to_packed0[1], to_packed1[1])
    early = early_grads(normed, d_value, attended, (d_branch0, d_branch1))
    early = lax.psum_scatter(early, "dp", scatter_dimension=0, tiled=True)
    end0 = into_packed(0, to_packed0, dots0)
    dots1, *rest = sync(dots1, *end0, *mix_far0)
    end0, mix_far0 = rest[:3], rest[3:]
    mixed0 = scatter_pairs_far(*scatter_pairs_near(mix_far0))
    end1 = into_packed(1, to_packed1, dots1)
    late = late_grads(normed, (end0[0], end1[0]))
    late, *rest = sync(late, *mix_core1, *end0[1:], *end1[1:])
    mix_core1, d_normed, attn_terms = rest[:4], (rest[4], rest[6]), (rest[5], rest[7])

    late = lax.psum_scatter(late, "dp", scatter_dimension=0, tiled=True)
    mix_near1 = scatter_plane_near(mix_core1)
    d_normed0 = scatter_tp(d_normed[0])
    grad_attn_gain = (attn_terms[0] + attn_terms[1])[0] / attn_gain
    grad_qk = (to_packed0[3] + to_packed1[3])[:2]
    wide_qk = jnp.pad(grad_qk, ((0, 0), (0, width - columns)))
    grad_router, grad_moe_gain = (one + two for one, two in zip(small0, small1))
    small = jnp.concatenate([grad_attn_gain[None], grad_moe_gain[None], grad_router.T], axis=0)
    small, mixed0, d_normed0, d_normed1, *mix_near1 = sync(small, mixed0, d_normed0, d_normed[1], *mix_near1)
    mix_far1 = scatter_plane_far(mix_near1, zone)
    total = small
    for k in range(1, tp_size):
        total = total + swap_tp(small, k)
    small = jnp.concatenate([total, wide_qk], axis=0)
    small, d_normed0, d_normed1, *mix_far1 = sync(small, d_normed0, d_normed1, *mix_far1)
    mixed1 = scatter_pairs_near(mix_far1)
    small = (small + swap_dp(small, 1)).astype(BF)
    early, late, small, d_normed0, d_normed1, *mixed1 = sync(early, late, small, d_normed0, d_normed1, *mixed1)
    shared = lax.all_gather(jnp.stack([late, early]), "dp", axis=1, tiled=True)
    mixed1 = scatter_pairs_far(*mixed1)
    small = add_low(small, *[swap_dp(small, 2 * k) for k in range(1, outer)])
    d_normed1 = scatter_tp(d_normed1)
    if whole:
        d_gate_up = gate_up_grads(None, moe0 + moe1, ran0 + ran1)
        d_down = down_grads(None, cot0 + cot1, ran0 + ran1)
    input_grads = []
    for m, (d_hidden, d_rows) in enumerate(((d_hidden0, d_normed0), (d_hidden1, d_normed1))):
        d_x_hat = d_rows * attn_gain
        d_tokens = d_hidden + x_scale[m] * (
            d_x_hat - x_hat[m] * jnp.mean(d_x_hat * x_hat[m], axis=1, keepdims=True)
        )
        input_grads.append(d_tokens.astype(BF))
    mixed = jnp.stack([mixed0 + more[0], mixed1 + more[1]])
    out = (hidden + mixed).astype(BF)
    d_gate_up = d_gate_up.reshape(width, local, 2, quarter)
    d_gate_up_out = jnp.stack([d_gate_up[:, e] for e in range(local)])
    shared, small, d_tokens, out, d_gate_up_out, d_down = sync(
        shared, small, jnp.stack(input_grads), out, d_gate_up_out, d_down
    )
    total_qkv = shared.reshape(4, width, columns)[:3]
    total_out = shared[1, width:].reshape(width // columns, columns, columns)
    total_out = jnp.concatenate([piece for piece in total_out], axis=1).astype(F32)
    return (
        out[:, None],
        d_tokens[:, None],
        small[0],
        jnp.transpose(total_qkv.astype(F32), (1, 0, 2)),
        small[-2:, :columns],
        total_out,
        small[1],
        small[2 : 2 + experts].T,
        d_gate_up_out.reshape(w_gateup.shape),
        d_down.reshape(w_down.shape),
    )


def solution(mesh):
    return jax.shard_map(
        shards,
        mesh=mesh,
        in_specs=(
            P(None, "dp", "tp", None),
            P(None, "dp", "tp", None),
            P(None, "dp", None, None),
            P(None, "dp", None),
            P(),
            P(None, None, "tp"),
            P(None, "tp"),
            P("tp", None),
            P(),
            P(),
            P("dp", None, None, "tp"),
            P("dp", "tp", None),
        ),
        out_specs=(
            P(None, "dp", "tp", None),
            P(None, "dp", "tp", None),
            P(),
            P(None, None, "tp"),
            P(None, "tp"),
            P("tp", None),
            P(),
            P(),
            P("dp", None, None, "tp"),
            P("dp", "tp", None),
        ),
        check_vma=False,
    )
```

```python
import functools

import jax
import jax.numpy as jnp
from jax import lax
from jax.experimental import pallas as pl
from jax.experimental.pallas import tpu as pltpu
from jax.sharding import PartitionSpec as P

HD = 128
EPSILON = 1e-05
LANES = 128
BF = jnp.bfloat16
F32 = jnp.float32
VMEM_BYTES = 56 * 1024 * 1024
EXPERT_TILE = 256
COST_SCALE = 8


def rms_scale(values):
    return lax.rsqrt(jnp.mean(values * values, axis=-1, keepdims=True) + EPSILON)


def contract(left, right, left_dim, right_dim):
    return lax.dot_general(
        left, right, (((left_dim,), (right_dim,)), ((), ())), preferred_element_type=F32
    )


def swap_tp(value, bits):
    size = lax.axis_size("tp")
    return lax.ppermute(value, "tp", [(i, i ^ bits) for i in range(size)])


def swap_dp(value, bits):
    size = lax.axis_size("dp")
    return lax.ppermute(value, "dp", [(i, i ^ bits) for i in range(size)])


def sync(*values):
    return lax.optimization_barrier(values)


def after(value, *deps):
    return lax.optimization_barrier((value, *deps))[0]


def add_low(*terms):
    total = terms[0].astype(F32)
    for term in terms[1:]:
        total = total + term.astype(F32)
    return total


def gather_tp(rows):
    size = lax.axis_size("tp")
    return jnp.concatenate([rows] + [swap_tp(rows, k) for k in range(1, size)], axis=-2)


def scatter_tp(rows):
    size = lax.axis_size("tp")
    n = rows.shape[-2] // size
    pieces = [rows[..., k * n : (k + 1) * n, :] for k in range(size)]
    return add_low(*[swap_tp(p, k) if k else p for k, p in enumerate(pieces)])


def scatter_tp_first(rows, later):
    size = lax.axis_size("tp")
    n = rows.shape[-2] // size
    pieces = [rows[..., k * n : (k + 1) * n, :] for k in range(size)]
    *pieces, later = lax.optimization_barrier((*pieces, later))
    return add_low(*[swap_tp(p, k) if k else p for k, p in enumerate(pieces)]), later


def sum_tp(rows):
    size = lax.axis_size("tp")
    n = rows.shape[-2] // size
    total = rows
    for k in range(1, size):
        other = swap_tp(rows, k)
        total = total + jnp.concatenate(
            [other[..., (j ^ k) * n : (j ^ k) * n + n, :] for j in range(size)], axis=-2
        )
    return total


def gather_outer(rows, partners):
    return jnp.concatenate([swap_dp(rows, 2 * k) if k else rows for k in partners], axis=-2)


def gather_plane_near(rows):
    return swap_tp(rows, 1), swap_tp(rows, 2)


def far_sends(near, far):
    n = near.shape[-2] // 2
    return sync(near[..., :n, :], far[..., n:, :])


def gather_plane_far(rows, near, far, sends=None):
    n = rows.shape[-2] // 2

    def top(value):
        return value[..., :n, :]

    def low(value):
        return value[..., n:, :]

    sent_a, sent_b = sends or far_sends(near, far)
    far_a, far_b = swap_tp(sent_a, 2), swap_tp(sent_b, 1)
    base = jnp.concatenate(
        [top(rows), top(far), top(near), top(rows), low(rows), low(near), low(far), top(rows)], axis=-2
    )
    base = lax.optimization_barrier(base)
    base = lax.dynamic_update_slice_in_dim(base, far_a, 3 * n, axis=-2)
    return lax.dynamic_update_slice_in_dim(base, far_b, 7 * n, axis=-2)


def cut(rows, count):
    n = rows.shape[-2] // count
    return [rows[..., i * n : (i + 1) * n, :] for i in range(count)]


def add_pieces(left, right):
    return [add_low(one, two).astype(BF) for one, two in zip(left, right)]


def scatter_core(own, other):
    return add_pieces(cut(own, 4), cut(swap_dp(other, 1), 4))


def scatter_plane_near(quarters):
    keep_a, send_a, keep_b, send_b = quarters
    got_a, got_b = swap_tp(send_a, 1), swap_tp(send_b, 2)
    return add_pieces(cut(keep_a, 2), cut(got_a, 2)) + add_pieces(cut(keep_b, 2), cut(got_b, 2))


def scatter_plane_far(eighths, partners):
    keep_a, send_a, keep_b, send_b = eighths
    got_a, got_b = swap_tp(send_a, 2), swap_tp(send_b, 1)
    half = len(partners) // 2
    return add_pieces(cut(keep_a, half), cut(got_a, half)) + add_pieces(cut(keep_b, half), cut(got_b, half))


def scatter_outer(pieces, partners):
    return add_low(*[swap_dp(p, 2 * k) if k else p for p, k in zip(pieces, partners)])


def scatter_pairs_near(pieces):
    own, one, two, three = pieces
    got_own, got_three = cut(swap_dp(jnp.concatenate([one, two], axis=0), 2), 2)
    return [add_low(own, got_own), add_low(three, got_three).astype(BF)]


def scatter_pairs_far(own, three):
    return own + swap_dp(three, 6).astype(F32)


def call_kernel(body, ins, outs, grid=(), in_specs=None, out_specs=None, flops=0, moved=0, **extra):
    whole = pl.BlockSpec(memory_space=pltpu.VMEM)
    return pl.pallas_call(
        body,
        out_shape=outs,
        grid=grid,
        in_specs=in_specs or [whole] * len(ins),
        out_specs=out_specs or [whole] * len(outs),
        compiler_params=pltpu.CompilerParams(vmem_limit_bytes=VMEM_BYTES),
        cost_estimate=pl.CostEstimate(
            flops=flops // COST_SCALE, bytes_accessed=moved // COST_SCALE, transcendentals=0
        ),
        **extra,
    )(*ins)


def project_kernel(rows_ref, gain_ref, weight_ref, normed_ref, packed_ref, squares_ref):
    part = pl.program_id(0)

    @pl.when(part == 0)
    def _():
        rows = rows_ref[...].astype(F32)
        normed_ref[...] = (rows * rms_scale(rows) * gain_ref[...]).astype(BF)
        squares_ref[...] = jnp.zeros_like(squares_ref)

    packed = jnp.dot(normed_ref[...], weight_ref[...], preferred_element_type=F32)
    packed_ref[...] = packed
    lane = lax.broadcasted_iota(jnp.int32, squares_ref.shape, 1)

    @pl.when(part < 2)
    def _():
        total = jnp.sum(packed * packed, axis=1, keepdims=True)
        squares_ref[...] += jnp.where(lane == part, total, 0.0)


def project(gathered, gain, qkv_parts):
    micro, group, width = gathered.shape
    columns = qkv_parts.shape[2]
    rows = micro * group
    normed, packed, squares = call_kernel(
        project_kernel,
        (gathered.reshape(rows, width), gain[None], qkv_parts),
        [
            jax.ShapeDtypeStruct((rows, width), BF),
            jax.ShapeDtypeStruct((rows, 3 * columns), F32),
            jax.ShapeDtypeStruct((rows, LANES), F32),
        ],
        grid=(3,),
        in_specs=[
            pl.BlockSpec((rows, width), lambda i: (0, 0)),
            pl.BlockSpec((1, width), lambda i: (0, 0)),
            pl.BlockSpec((None, width, columns), lambda i: (i, 0, 0)),
        ],
        out_specs=[
            pl.BlockSpec((rows, width), lambda i: (0, 0)),
            pl.BlockSpec((rows, columns), lambda i: (0, i)),
            pl.BlockSpec((rows, LANES), lambda i: (0, 0)),
        ],
        flops=2 * rows * width * 3 * columns,
        moved=2 * width * 3 * columns,
    )
    return (value.reshape(micro, group, -1) for value in (normed, packed, squares))


def attend_kernel(
    packed_ref, squares_ref, gain_ref, cos_ref, sin_ref, allowed_ref, out_weight_ref,
    used_ref, weights_ref, attended_ref, branch_ref, *, width,
):
    columns = packed_ref.shape[1] // 3
    heads = columns // HD
    cosine, sine = cos_ref[...], sin_ref[...]
    allowed = allowed_ref[...] > 0.0
    scales = lax.rsqrt(squares_ref[:, :2] / width + EPSILON)
    for h in range(heads):
        used = []
        for part in range(2):
            at = slice(part * columns + h * HD, part * columns + (h + 1) * HD)
            values = packed_ref[:, at] * scales[:, part : part + 1]
            values = values * gain_ref[part : part + 1, h * HD : (h + 1) * HD]
            values = (values * cosine + pltpu.roll(values, HD // 2, 1) * sine).astype(BF)
            used_ref[:, at] = values
            used.append(values)
        at = slice(2 * columns + h * HD, 2 * columns + (h + 1) * HD)
        value = packed_ref[:, at].astype(BF)
        used_ref[:, at] = value
        scores = contract(used[0], used[1], 1, 1) * HD ** (-0.5)
        masked = jnp.where(allowed, scores, -1e30)
        top_score = jnp.max(masked, axis=-1, keepdims=True)
        exponent = jnp.where(allowed, jnp.exp(masked - top_score), 0.0)
        weights = exponent / jnp.sum(exponent, axis=-1, keepdims=True)
        weights_ref[h] = weights
        attended_ref[:, h * HD : (h + 1) * HD] = jnp.dot(
            weights.astype(BF), value, preferred_element_type=F32
        ).astype(BF)
    branch_ref[...] = jnp.dot(
        attended_ref[...], out_weight_ref[...], preferred_element_type=F32
    ).astype(BF)


def attend(packed, squares, gain, cosine, sine, allowed, out_weight):
    micro, group = packed.shape[:2]
    columns, width = out_weight.shape
    heads = columns // HD

    def each(*shape):
        return pl.BlockSpec((None,) + shape, lambda m: (m,) + (0,) * len(shape))

    return call_kernel(
        functools.partial(attend_kernel, width=width),
        (packed, squares, gain, cosine, sine, allowed, out_weight),
        [
            jax.ShapeDtypeStruct((micro, group, 3 * columns), BF),
            jax.ShapeDtypeStruct((micro, heads, group, group), F32),
            jax.ShapeDtypeStruct((micro, group, columns), BF),
            jax.ShapeDtypeStruct((micro, group, width), BF),
        ],
        grid=(micro,),
        in_specs=[
            each(group, 3 * columns),
            each(group, LANES),
            pl.BlockSpec((2, columns), lambda m: (0, 0)),
            each(group, HD),
            each(group, HD),
            each(group, group),
            pl.BlockSpec((columns, width), lambda m: (0, 0)),
        ],
        out_specs=[
            each(group, 3 * columns),
            each(heads, group, group),
            each(group, columns),
            each(group, width),
        ],
        flops=2 * micro * group * columns * (width + 2 * group),
        moved=16 * micro * group * width,
    )


def attend_back_kernel(
    d_branch_ref, out_weight_ref, used_ref, weights_ref, packed_ref, squares_ref, gain_ref, cos_ref,
    sin_ref, d_hat_ref, d_value_ref, dots_ref, gain_grad_ref, *, width,
):
    columns = packed_ref.shape[1] // 3
    heads = columns // HD
    cosine, sine = cos_ref[...], sin_ref[...]
    scales = lax.rsqrt(squares_ref[:, :2] / width + EPSILON)
    d_attended = contract(d_branch_ref[...], out_weight_ref[...], 1, 1).astype(BF)
    dots = [0.0, 0.0]
    gain_grad_ref[...] = jnp.zeros_like(gain_grad_ref)
    for h in range(heads):
        own = slice(h * HD, (h + 1) * HD)
        query, key, value = (
            used_ref[:, part * columns + h * HD : part * columns + (h + 1) * HD] for part in range(3)
        )
        d_out = d_attended[:, own]
        weights = weights_ref[h]
        d_weights = contract(d_out, value, 1, 1)
        row_delta = jnp.sum(weights * d_weights, axis=-1, keepdims=True)
        d_scores = (weights * (d_weights - row_delta) * HD ** (-0.5)).astype(BF)
        d_value_ref[:, own] = contract(weights.astype(BF), d_out, 0, 0).astype(BF)
        grads = (
            jnp.dot(d_scores, key, preferred_element_type=F32),
            contract(d_scores, query, 0, 0),
        )
        for part in range(2):
            at = slice(part * columns + h * HD, part * columns + (h + 1) * HD)
            hat = packed_ref[:, at] * scales[:, part : part + 1]
            grad = grads[part] * cosine - pltpu.roll(grads[part], HD // 2, 1) * sine
            gain_grad_ref[part : part + 1, own] = jnp.sum(grad * hat, axis=0, keepdims=True)
            grad = grad * gain_ref[part : part + 1, own]
            d_hat_ref[:, at] = grad
            dots[part] = dots[part] + jnp.sum(grad * hat, axis=1, keepdims=True)
    lane = lax.broadcasted_iota(jnp.int32, dots_ref.shape, 1)
    dots_ref[...] = jnp.where(lane == 0, dots[0], jnp.where(lane == 1, dots[1], 0.0))


def attend_back(m, d_branch, out_weight, used, weights, packed, squares, gain, cosine, sine):
    group = packed.shape[1]
    columns, width = out_weight.shape
    heads = columns // HD

    def pick(*shape):
        return pl.BlockSpec((None,) + shape, lambda i: (m,) + (0,) * len(shape))

    def full(*shape):
        return pl.BlockSpec(shape, lambda i: (0,) * len(shape))

    return call_kernel(
        functools.partial(attend_back_kernel, width=width),
        (d_branch, out_weight, used, weights, packed, squares, gain, cosine, sine),
        [
            jax.ShapeDtypeStruct((group, 2 * columns), F32),
            jax.ShapeDtypeStruct((group, columns), BF),
            jax.ShapeDtypeStruct((group, LANES), F32),
            jax.ShapeDtypeStruct((8, columns), F32),
        ],
        grid=(1,),
        in_specs=[
            full(group, width),
            full(columns, width),
            pick(group, 3 * columns),
            pick(heads, group, group),
            pick(group, 3 * columns),
            pick(group, LANES),
            full(2, columns),
            pick(group, HD),
            pick(group, HD),
        ],
        out_specs=[
            full(group, 2 * columns),
            full(group, columns),
            full(group, LANES),
            full(8, columns),
        ],
        flops=2 * group * columns * (width + 5 * group),
        moved=20 * group * width,
    )


def unproject_kernel(
    d_hat_ref, d_value_ref, dots_ref, packed_ref, squares_ref, weight_ref, normed_ref, d_packed_ref,
    d_normed_ref, gain_grad_ref, *, width,
):
    columns = d_value_ref.shape[1]
    scales = lax.rsqrt(squares_ref[:, :2] / width + EPSILON)
    for part in range(2):
        at = slice(part * columns, (part + 1) * columns)
        scale = scales[:, part : part + 1]
        hat = packed_ref[:, at] * scale
        mean = dots_ref[:, part : part + 1] / width
        d_packed_ref[:, at] = (scale * (d_hat_ref[:, at] - hat * mean)).astype(BF)
    d_packed_ref[:, 2 * columns :] = d_value_ref[...]
    total = 0.0
    for part in range(3):
        at = slice(part * columns, (part + 1) * columns)
        total = total + contract(d_packed_ref[:, at], weight_ref[part], 1, 1)
    d_normed_ref[...] = total.astype(BF)
    column = jnp.sum(total * normed_ref[...].astype(F32), axis=0, keepdims=True)
    gain_grad_ref[...] = jnp.broadcast_to(column, gain_grad_ref.shape)


def unproject(m, d_hat, d_value, dots, packed, squares, qkv_parts, normed):
    group, columns = d_value.shape
    width = qkv_parts.shape[1]

    def pick(*shape):
        return pl.BlockSpec((None,) + shape, lambda i: (m,) + (0,) * len(shape))

    def full(*shape):
        return pl.BlockSpec(shape, lambda i: (0,) * len(shape))

    return call_kernel(
        functools.partial(unproject_kernel, width=width),
        (d_hat, d_value, dots, packed, squares, qkv_parts, normed),
        [
            jax.ShapeDtypeStruct((group, 3 * columns), BF),
            jax.ShapeDtypeStruct((group, width), BF),
            jax.ShapeDtypeStruct((8, width), F32),
        ],
        grid=(1,),
        in_specs=[
            full(group, 2 * columns),
            full(group, columns),
            full(group, LANES),
            pick(group, 3 * columns),
            pick(group, LANES),
            full(3, width, columns),
            pick(group, width),
        ],
        out_specs=[full(group, 3 * columns), full(group, width), full(8, width)],
        flops=2 * group * width * 3 * columns,
        moved=2 * width * 3 * columns + 8 * group * width,
    )


def rows_product_kernel(*refs, count):
    lefts, rights, starts, out_ref = refs[:count], refs[count : 2 * count], refs[2 * count : -1], refs[-1]
    total = starts[0][...] if starts else 0.0
    for left, right in zip(lefts, rights):
        total = total + contract(left[...], right[...], 0, 0)
    out_ref[...] = total


def rows_product(lefts, rights, start, tile, width, columns):
    count = len(lefts)
    rows = sum(left.shape[0] for left in lefts)
    once = pl.Buffered(1)
    starts = [] if start is None else [start]
    return call_kernel(
        functools.partial(rows_product_kernel, count=count),
        (*lefts, *rights, *starts),
        [jax.ShapeDtypeStruct((width, columns), F32)],
        grid=(width // tile,),
        in_specs=[pl.BlockSpec((left.shape[0], tile), lambda i: (0, i)) for left in lefts]
        + [
            pl.BlockSpec((right.shape[0], columns), lambda i: (0, 0), pipeline_mode=once)
            for right in rights
        ]
        + [pl.BlockSpec((tile, columns), lambda i: (i, 0)) for _ in starts],
        out_specs=[pl.BlockSpec((tile, columns), lambda i: (i, 0))],
        flops=2 * rows * width * columns,
        moved=2 * rows * (width + columns) + 4 * width * columns,
    )[0]


def rows_pair(left0_ref, left1_ref, right0, right1):
    return (contract(left0_ref[...], right0, 0, 0) + contract(left1_ref[...], right1, 0, 0)).astype(BF)


def early_grads_kernel(
    normed0_ref, normed1_ref, d_value0_ref, d_value1_ref, attended0_ref, attended1_ref, d_branch0_ref,
    d_branch1_ref, out_ref,
):
    columns = attended0_ref.shape[1]

    @pl.when(pl.program_id(0) == 0)
    def _():
        out_ref[...] = rows_pair(normed0_ref, normed1_ref, d_value0_ref[...], d_value1_ref[...])

    @pl.when(pl.program_id(0) == 1)
    def _():
        for start in range(0, out_ref.shape[0], columns):
            at = slice(start, start + columns)
            out_ref[at, :] = rows_pair(
                attended0_ref, attended1_ref, d_branch0_ref[:, at], d_branch1_ref[:, at]
            )


def early_grads(normed, d_value, attended, d_branch):
    micro, group, width = normed.shape
    columns = attended.shape[2]
    tile = width // 2
    normed_specs = [pl.BlockSpec((None, group, tile), lambda p, i, m=m: (m, 0, i)) for m in range(micro)]
    value_spec = pl.BlockSpec((group, columns), lambda p, i: (0, 0))
    attended_specs = [pl.BlockSpec((None, group, columns), lambda p, i, m=m: (m, 0, 0)) for m in range(micro)]
    branch_spec = pl.BlockSpec((group, tile), lambda p, i: (0, jnp.where(p == 1, i, 0)))
    return call_kernel(
        early_grads_kernel,
        (normed, normed, *d_value, attended, attended, *d_branch),
        [jax.ShapeDtypeStruct((2 * width, columns), BF)],
        grid=(2, 2),
        in_specs=normed_specs + [value_spec] * 2 + attended_specs + [branch_spec] * 2,
        out_specs=[pl.BlockSpec((tile, columns), lambda p, i: (2 * p + i, 0))],
        flops=2 * micro * group * width * 2 * columns,
        moved=2 * width * 2 * columns,
    )[0]


def late_grads_kernel(normed0_ref, normed1_ref, d_packed0_ref, d_packed1_ref, out_ref):
    out_ref[...] = rows_pair(normed0_ref, normed1_ref, d_packed0_ref[...], d_packed1_ref[...])


def late_grads(normed, d_packed):
    micro, group, width = normed.shape
    columns = d_packed[0].shape[1] // 3
    tile = width // 2
    normed_specs = [pl.BlockSpec((None, group, tile), lambda i, p, m=m: (m, 0, i)) for m in range(micro)]
    return call_kernel(
        late_grads_kernel,
        (normed, normed, *d_packed),
        [jax.ShapeDtypeStruct((2 * width, columns), BF)],
        grid=(2, 2),
        in_specs=normed_specs + [pl.BlockSpec((group, columns), lambda i, p: (0, p))] * 2,
        out_specs=[pl.BlockSpec((tile, columns), lambda i, p: (2 * p + i, 0))],
        flops=2 * micro * group * width * 2 * columns,
        moved=2 * width * 2 * columns,
    )[0]


def experts_kernel(
    ids_ref, moe_ref, cot_ref, router_ref, gate_up_ref, down_ref, d_rows_ref, scaled_ref, d_inner_ref,
    *, experts, local,
):
    width = moe_ref.shape[1]
    quarter = down_ref.shape[0] // local
    rows = moe_ref[...]
    lane = lax.broadcasted_iota(jnp.int32, (rows.shape[0], LANES), 1)
    logits = jnp.dot(rows, router_ref[...], preferred_element_type=F32)
    logits = jnp.where(lane < experts, logits, -1e30)
    exponent = jnp.exp(logits - jnp.max(logits, axis=1, keepdims=True))
    probs = exponent / jnp.sum(exponent, axis=1, keepdims=True)
    mask = cot_ref[:, width:].astype(F32)
    gates = probs * mask
    back = jnp.zeros_like(probs)
    for e in range(local):
        here = lane == ids_ref[0] + e
        gate = jnp.sum(jnp.where(here, gates, 0.0), axis=1, keepdims=True)
        at = slice(e * quarter, (e + 1) * quarter)
        gate_at = slice(2 * e * quarter, (2 * e + 1) * quarter)
        up_at = slice((2 * e + 1) * quarter, (2 * e + 2) * quarter)
        d_raw = contract(cot_ref[:, :width], down_ref[at, :], 1, 1)
        gate_pre = jnp.dot(rows, gate_up_ref[:, gate_at], preferred_element_type=F32)
        up_pre = jnp.dot(rows, gate_up_ref[:, up_at], preferred_element_type=F32)
        sigmoid = 1.0 / (1.0 + jnp.exp(-gate_pre))
        silu = gate_pre * sigmoid
        active = silu * up_pre
        term = jnp.sum(active * d_raw, axis=1, keepdims=True)
        back = jnp.where(here, term, back)
        scaled_ref[:, at] = (active * gate).astype(BF)
        d_active = d_raw * gate
        d_inner_ref[:, gate_at] = (
            d_active * up_pre * sigmoid * (1.0 + gate_pre * (1.0 - sigmoid))
        ).astype(BF)
        d_inner_ref[:, up_at] = (d_active * silu).astype(BF)
    d_rows_ref[:, width:] = jnp.where(mask > 0.0, back, 0.0).astype(BF)
    d_rows_ref[:, :width] = contract(d_inner_ref[...], gate_up_ref[...], 1, 1).astype(BF)


def run_experts(first_id, moe_all, cot_all, router_wide, gate_up, down, experts, local):
    total, width = moe_all.shape
    tile = min(total, EXPERT_TILE)
    inner = gate_up.shape[1]
    once = pl.Buffered(1)
    return call_kernel(
        functools.partial(experts_kernel, experts=experts, local=local),
        (first_id, moe_all, cot_all, router_wide, gate_up, down),
        [
            jax.ShapeDtypeStruct((total, width + LANES), BF),
            jax.ShapeDtypeStruct((total, inner // 2), BF),
            jax.ShapeDtypeStruct((total, inner), BF),
        ],
        grid=(total // tile,),
        in_specs=[
            pl.BlockSpec(memory_space=pltpu.SMEM),
            pl.BlockSpec((tile, width), lambda i: (i, 0)),
            pl.BlockSpec((tile, width + LANES), lambda i: (i, 0)),
            pl.BlockSpec((width, LANES), lambda i: (0, 0), pipeline_mode=once),
            pl.BlockSpec((width, inner), lambda i: (0, 0), pipeline_mode=once),
            pl.BlockSpec((inner // 2, width), lambda i: (0, 0), pipeline_mode=once),
        ],
        out_specs=[
            pl.BlockSpec((tile, width + LANES), lambda i: (i, 0)),
            pl.BlockSpec((tile, inner // 2), lambda i: (i, 0)),
            pl.BlockSpec((tile, inner), lambda i: (i, 0)),
        ],
        flops=2 * total * width * inner * 5 // 2,
        moved=total * width * 6,
    )


def shards(
    tokens, cotangent, routes, lengths, attn_gain, qkv_weight, qk_gain, out_weight, moe_gain,
    router, w_gateup, w_down,
):
    tp_size = lax.axis_size("tp")
    dp_size = lax.axis_size("dp")
    tp_rank = lax.axis_index("tp")
    dp_rank = lax.axis_index("dp")
    micro_count, _, own_rows, width = tokens.shape
    group = own_rows * tp_size
    experts = router.shape[1]
    local = w_gateup.shape[0]
    columns = qkv_weight.shape[2]
    quarter = w_down.shape[1]

    qkv_parts = jnp.transpose(qkv_weight, (1, 0, 2))
    gate_up = jnp.concatenate([w_gateup[e].reshape(width, 2 * quarter) for e in range(local)], axis=1)
    down = w_down.reshape(local * quarter, width)
    router_wide = jnp.pad(router, ((0, 0), (0, -experts % LANES)))
    expert_ids = jnp.arange(experts, dtype=jnp.int32)
    first_id = (dp_rank * local).astype(jnp.int32).reshape(1)

    places = jnp.concatenate(
        [(tp_rank ^ k) * own_rows + jnp.arange(own_rows, dtype=jnp.int32) for k in range(tp_size)]
    )
    own_places = tp_rank * own_rows + jnp.arange(own_rows, dtype=jnp.int32)
    frequency = jnp.exp(
        jnp.arange(HD // 2, dtype=F32) * (-2.0 * jnp.log(10000.0) / HD)
    )

    first_len = lengths[:, 0, 0][:, None]
    live_end = first_len + lengths[:, 0, 1][:, None]
    live_own = (own_places[None, :] < live_end).astype(F32)[:, :, None]
    d_mixed = cotangent[:, 0].astype(F32) * live_own
    own_routes = lax.dynamic_slice_in_dim(routes[:, 0], tp_rank * own_rows, own_rows, 1)
    chosen = jnp.any(own_routes[..., None] == expert_ids, axis=2)
    mask = jnp.pad(chosen.astype(BF), ((0, 0), (0, 0), (0, -experts % LANES)))
    cot_sent = jnp.concatenate([d_mixed.astype(BF), mask], axis=2)


    outer = dp_size // 2
    span = min(outer, 4)
    parts = [range(first, first + span) for first in range(0, outer, span)]
    zone = parts[0]

    x_own = tokens[:, 0].astype(F32)
    x_scale = rms_scale(x_own)
    x_hat = x_own * x_scale

    def experts_of(moe_half, cot_half):
        return run_experts(first_id, moe_half, cot_half, router_wide, gate_up, down, experts, local)

    def gate_up_grads(start, moe, ran):
        inner = 2 * local * quarter
        return rows_product(moe, [r[2] for r in ran], start, 256, width, inner)

    def down_grads(start, cot, ran):
        return rows_product([r[1] for r in ran], cot, start, 256, local * quarter, width)

    def mix(ran):
        return jnp.dot(ran[1], down, preferred_element_type=F32).astype(BF)

    gathered = gather_tp(tokens[:, 0])
    cot_z = [swap_dp(cot_sent, 2 * k) for k in zone[1:-1]]
    gathered, cot_late = sync(gathered, cot_sent)
    cot_z.append(swap_dp(cot_late, 2 * zone[-1]))

    segment = (places >= first_len).astype(jnp.int32) + (places >= live_end).astype(jnp.int32)
    starts = jnp.where(segment == 0, 0, jnp.where(segment == 1, first_len, live_end))
    angles = (places - starts).astype(F32)[:, :, None] * frequency
    cosine, sine = jnp.cos(angles), jnp.sin(angles)
    cosine = jnp.concatenate([cosine, cosine], axis=2)
    sine = jnp.concatenate([-sine, sine], axis=2)
    allowed = (segment[:, :, None] == segment[:, None, :]) & (places[None, :] <= places[:, None])

    normed, packed, squares = project(gathered, attn_gain, qkv_parts)
    squares = sum_tp(squares)
    used, weights, attended, branch = attend(
        packed, squares, qk_gain, cosine, sine, allowed.astype(F32), out_weight
    )
    branch, gate_up, down, router_wide, *cot_z = sync(branch, gate_up, down, router_wide, cot_sent, *cot_z)
    branch_own, cot_z = scatter_tp_first(branch, jnp.concatenate(cot_z, axis=1))
    cot_z0, cot_z1 = cot_z[0], cot_z[1]
    cot_near0 = gather_plane_near(cot_z0)
    hidden = x_own + branch_own
    h_scale = rms_scale(hidden)
    h_hat = hidden * h_scale
    moe_own = (h_hat * moe_gain).astype(BF)
    moe_z0 = gather_outer(moe_own[0], zone)

    moe_z0, moe_own1, cot_z0, cot_z1, *cot_near0 = sync(moe_z0, moe_own[1], cot_z0, cot_z1, *cot_near0)
    moe_near0 = gather_plane_near(moe_z0)
    moe_z1 = gather_outer(moe_own1, zone)

    cot_sends0 = far_sends(*cot_near0)
    moe_z0, moe_z1, cot_z0, cot_z1, *near = sync(
        moe_z0, moe_z1, cot_z0, cot_z1, *cot_near0, *moe_near0, *cot_sends0
    )
    cot_half0 = gather_plane_far(cot_z0, *near[:2], near[4:])
    moe_half0 = gather_plane_far(moe_z0, *near[2:4])

    moe_half0, cot_half0, moe_z1, cot_z1 = sync(moe_half0, cot_half0, moe_z1, cot_z1)
    moe_other0, cot_other0 = swap_dp(moe_half0, 1), swap_dp(cot_half0, 1)
    cot_near1 = gather_plane_near(cot_z1)
    own0 = experts_of(moe_half0, cot_half0)

    moe_other0, cot_other0, moe_z1, cot_z1, *rest = sync(
        moe_other0, cot_other0, moe_z1, cot_z1, *cot_near1, *own0
    )
    cot_near1, own0 = rest[:2], rest[2:]
    moe_near1 = gather_plane_near(moe_z1)
    other0 = experts_of(moe_other0, cot_other0)

    cot_sends1 = far_sends(*cot_near1)
    moe_z1, cot_z1, *rest = sync(
        moe_z1, cot_z1, *cot_near1, *moe_near1, *own0, *other0, *cot_sends1
    )
    own0, other0, cot_sends1 = rest[4:7], rest[7:10], rest[10:]
    core0 = scatter_core(own0[0], other0[0])
    cot_half1 = gather_plane_far(cot_z1, *rest[:2], cot_sends1)
    moe_half1 = gather_plane_far(moe_z1, *rest[2:4])
    mix0 = [mix(own0), mix(other0)]

    cot_half1, moe_half1, *rest = sync(cot_half1, moe_half1, *core0, *mix0, *own0, *other0)
    core0, mix0, own0, other0 = rest[:4], rest[4:6], rest[6:9], rest[9:]
    near0 = scatter_plane_near(core0)
    moe_other1, cot_other1 = swap_dp(moe_half1, 1), swap_dp(cot_half1, 1)
    own1 = experts_of(moe_half1, cot_half1)

    moe_other1, cot_other1, *rest = sync(moe_other1, cot_other1, *near0, *own1)
    near0, own1 = rest[:4], rest[4:]
    far0 = scatter_plane_far(near0, zone)
    other1 = experts_of(moe_other1, cot_other1)

    rest = sync(*far0, *mix0, *own1, *other1)
    far0, rest = rest[:span], rest[span:]
    mix0, own1, other1 = rest[:2], rest[2:5], rest[5:]
    core1 = scatter_core(own1[0], other1[0])
    back0 = scatter_outer(far0, zone)
    mix_core0 = scatter_core(*mix0)
    mix1 = [mix(own1), mix(other1)]

    back0, *rest = sync(back0, *core1, *mix_core0, *mix1, *own1, *other1)
    core1, mix_core0, mix1, own1, other1 = rest[:4], rest[4:8], rest[8:10], rest[10:13], rest[13:]
    near1 = scatter_plane_near(core1)
    mix_core1 = scatter_core(*mix1)

    def into_hidden(m, back):
        expert_grad = back[:, :width]
        probs = jax.nn.softmax(jnp.dot(moe_own[m], router, preferred_element_type=F32), axis=-1)
        d_choice = back[:, width : width + experts]
        d_logits = (probs * (d_choice - jnp.sum(probs * d_choice, axis=1, keepdims=True))).astype(BF)
        d_moe_in = expert_grad + contract(d_logits, router, 1, 1)
        d_h_hat = d_moe_in * moe_gain
        d_hidden = d_mixed[m] + h_scale[m] * (
            d_h_hat - h_hat[m] * jnp.mean(d_h_hat * h_hat[m], axis=1, keepdims=True)
        )
        small = (contract(moe_own[m], d_logits, 0, 0), jnp.sum(d_moe_in * h_hat[m], axis=0))
        return d_hidden, small

    def into_attention(m, d_branch):
        return attend_back(
            m, d_branch, out_weight, used, weights, packed, squares, qk_gain, cosine, sine
        )

    def into_packed(m, back, dots):
        return unproject(m, *back[:2], dots, packed, squares, qkv_parts, normed)

    ran0, moe0, cot0 = (own0, other0), (moe_half0, moe_other0), (cot_half0, cot_other0)
    ran1, moe1, cot1 = (own1, other1), (moe_half1, moe_other1), (cot_half1, cot_other1)
    whole = len(parts) == 1
    if whole:
        d_hidden0, small0 = into_hidden(0, back0)
        back0 = d_hidden0
    back0, *rest = sync(back0, *near1, *mix_core0, *mix_core1)
    near1, mix_core0, mix_core1 = rest[:4], rest[4:8], rest[8:]
    far1 = scatter_plane_far(near1, zone)
    if whole:
        d_branch0 = gather_tp(back0.astype(BF))
        d_branch0, *rest = sync(d_branch0, *far1, *mix_core0, *mix_core1)
    else:
        back0, *rest = sync(back0, *far1, *mix_core0, *mix_core1)
    far1, mix_core0, mix_core1 = rest[:span], rest[span : span + 4], rest[span + 4 :]
    back1 = scatter_outer(far1, zone)
    mix_near0 = scatter_plane_near(mix_core0)
    d_gate_up = d_down = None
    more = [0.0, 0.0]
    if whole:
        to_packed0 = into_attention(0, d_branch0)
        back1, *rest = sync(back1, *to_packed0, *mix_near0, *mix_core1)
        to_packed0, mix_near0, mix_core1 = rest[:4], rest[4:8], rest[8:]
    else:
        back = [back0, back1]
        d_gate_up = gate_up_grads(None, moe0 + moe1, ran0 + ran1)
        d_down = down_grads(None, cot0 + cot1, ran0 + ran1)
        for later in parts[1:]:
            for m in range(micro_count):
                sent, moe_sent, d_gate_up, d_down, back[m], more[m] = sync(
                    cot_sent[m], moe_own[m], d_gate_up, d_down, back[m], more[m]
                )
                halves = []
                for rows in (sent, moe_sent):
                    rows = gather_outer(rows, later)
                    rows = gather_plane_far(rows, *gather_plane_near(rows))
                    halves.append((rows, swap_dp(rows, 1)))
                cot, moe = halves
                ran = [experts_of(moe[j], cot[j]) for j in range(2)]
                d_gate_up = gate_up_grads(d_gate_up, moe, ran)
                d_down = down_grads(d_down, cot, ran)
                terms = []
                for pair in ([r[0] for r in ran], [mix(r) for r in ran]):
                    near = scatter_plane_near(scatter_core(*pair))
                    terms.append(scatter_outer(scatter_plane_far(near, later), later))
                back[m], more[m] = back[m] + terms[0], more[m] + terms[1]
        d_hidden0, small0 = into_hidden(0, back[0])
        back1 = back[1]
        d_branch0 = gather_tp(d_hidden0.astype(BF))
        to_packed0 = into_attention(0, d_branch0)

    d_hidden1, small1 = into_hidden(1, back1)
    d_branch1 = gather_tp(d_hidden1.astype(BF))
    dots0 = sum_tp(to_packed0[2])
    d_branch1, dots0, *rest = sync(d_branch1, dots0, *mix_near0, *mix_core1)
    mix_near0, mix_core1 = rest[:4], rest[4:]
    to_packed1 = into_attention(1, d_branch1)
    mix_far0 = scatter_plane_far(mix_near0, zone)
    dots1 = sum_tp(to_packed1[2])
    d_value = (to_packed0[1], to_packed1[1])
    early = early_grads(normed, d_value, attended, (d_branch0, d_branch1))
    early = lax.psum_scatter(early, "dp", scatter_dimension=0, tiled=True)
    end0 = into_packed(0, to_packed0, dots0)
    dots1, *rest = sync(dots1, *end0, *mix_far0)
    end0, mix_far0 = rest[:3], rest[3:]
    mixed0 = scatter_pairs_far(*scatter_pairs_near(mix_far0))
    end1 = into_packed(1, to_packed1, dots1)
    late = late_grads(normed, (end0[0], end1[0]))
    late, *rest = sync(late, *mix_core1, *end0[1:], *end1[1:])
    mix_core1, d_normed, attn_terms = rest[:4], (rest[4], rest[6]), (rest[5], rest[7])

    late = lax.psum_scatter(late, "dp", scatter_dimension=0, tiled=True)
    mix_near1 = scatter_plane_near(mix_core1)
    d_normed0 = scatter_tp(d_normed[0])
    grad_attn_gain = (attn_terms[0] + attn_terms[1])[0] / attn_gain
    grad_qk = (to_packed0[3] + to_packed1[3])[:2]
    wide_qk = jnp.pad(grad_qk, ((0, 0), (0, width - columns)))
    grad_router, grad_moe_gain = (one + two for one, two in zip(small0, small1))
    small = jnp.concatenate([grad_attn_gain[None], grad_moe_gain[None], grad_router.T], axis=0)
    small, mixed0, d_normed0, d_normed1, *mix_near1 = sync(small, mixed0, d_normed0, d_normed[1], *mix_near1)
    mix_far1 = scatter_plane_far(mix_near1, zone)
    total = small
    for k in range(1, tp_size):
        total = total + swap_tp(small, k)
    small = jnp.concatenate([total, wide_qk], axis=0)
    small, d_normed0, d_normed1, *mix_far1 = sync(small, d_normed0, d_normed1, *mix_far1)
    mixed1 = scatter_pairs_near(mix_far1)
    small = (small + swap_dp(small, 1)).astype(BF)
    early, late, small, d_normed0, d_normed1, *mixed1 = sync(early, late, small, d_normed0, d_normed1, *mixed1)
    shared = lax.all_gather(jnp.stack([late, early]), "dp", axis=1, tiled=True)
    mixed1 = scatter_pairs_far(*mixed1)
    small = add_low(small, *[swap_dp(small, 2 * k) for k in range(1, outer)])
    d_normed1 = scatter_tp(d_normed1)
    if whole:
        d_gate_up = gate_up_grads(None, moe0 + moe1, ran0 + ran1)
        d_down = down_grads(None, cot0 + cot1, ran0 + ran1)
    input_grads = []
    for m, (d_hidden, d_rows) in enumerate(((d_hidden0, d_normed0), (d_hidden1, d_normed1))):
        d_x_hat = d_rows * attn_gain
        d_tokens = d_hidden + x_scale[m] * (
            d_x_hat - x_hat[m] * jnp.mean(d_x_hat * x_hat[m], axis=1, keepdims=True)
        )
        input_grads.append(d_tokens.astype(BF))
    mixed = jnp.stack([mixed0 + more[0], mixed1 + more[1]])
    out = (hidden + mixed).astype(BF)
    d_gate_up = d_gate_up.reshape(width, local, 2, quarter)
    d_gate_up_out = jnp.stack([d_gate_up[:, e] for e in range(local)])
    shared, small, d_tokens, out, d_gate_up_out, d_down = sync(
        shared, small, jnp.stack(input_grads), out, d_gate_up_out, d_down
    )
    total_qkv = shared.reshape(4, width, columns)[:3]
    total_out = shared[1, width:].reshape(width // columns, columns, columns)
    total_out = jnp.concatenate([piece for piece in total_out], axis=1).astype(F32)
    return (
        out[:, None],
        d_tokens[:, None],
        small[0],
        jnp.transpose(total_qkv.astype(F32), (1, 0, 2)),
        small[-2:, :columns],
        total_out,
        small[1],
        small[2 : 2 + experts].T,
        d_gate_up_out.reshape(w_gateup.shape),
        d_down.reshape(w_down.shape),
    )


def solution(mesh):
    return jax.shard_map(
        shards,
        mesh=mesh,
        in_specs=(
            P(None, "dp", "tp", None),
            P(None, "dp", "tp", None),
            P(None, "dp", None, None),
            P(None, "dp", None),
            P(),
            P(None, None, "tp"),
            P(None, "tp"),
            P("tp", None),
            P(),
            P(),
            P("dp", None, None, "tp"),
            P("dp", "tp", None),
        ),
        out_specs=(
            P(None, "dp", "tp", None),
            P(None, "dp", "tp", None),
            P(),
            P(None, None, "tp"),
            P(None, "tp"),
            P("tp", None),
            P(),
            P(),
            P("dp", None, None, "tp"),
            P("dp", "tp", None),
        ),
        check_vma=False,
    )
```

```python
import functools

import jax
import jax.numpy as jnp
from jax import lax
from jax.experimental import pallas as pl
from jax.experimental.pallas import tpu as pltpu
from jax.sharding import PartitionSpec as P

HD = 128
EPSILON = 1e-05
LANES = 128
BF = jnp.bfloat16
F32 = jnp.float32
VMEM_BYTES = 56 * 1024 * 1024
EXPERT_TILE = 256
COST_SCALE = 8


def rms_scale(values):
    return lax.rsqrt(jnp.mean(values * values, axis=-1, keepdims=True) + EPSILON)


def contract(left, right, left_dim, right_dim):
    return lax.dot_general(
        left, right, (((left_dim,), (right_dim,)), ((), ())), preferred_element_type=F32
    )


def swap_tp(value, bits):
    size = lax.axis_size("tp")
    return lax.ppermute(value, "tp", [(i, i ^ bits) for i in range(size)])


def swap_dp(value, bits):
    size = lax.axis_size("dp")
    return lax.ppermute(value, "dp", [(i, i ^ bits) for i in range(size)])


def sync(*values):
    return lax.optimization_barrier(values)


def after(value, *deps):
    return lax.optimization_barrier((value, *deps))[0]


def add_low(*terms):
    total = terms[0].astype(F32)
    for term in terms[1:]:
        total = total + term.astype(F32)
    return total


def gather_tp(rows):
    size = lax.axis_size("tp")
    return jnp.concatenate([rows] + [swap_tp(rows, k) for k in range(1, size)], axis=-2)


def scatter_tp(rows):
    size = lax.axis_size("tp")
    n = rows.shape[-2] // size
    pieces = [rows[..., k * n : (k + 1) * n, :] for k in range(size)]
    return add_low(*[swap_tp(p, k) if k else p for k, p in enumerate(pieces)])


def scatter_tp_first(rows, later):
    size = lax.axis_size("tp")
    n = rows.shape[-2] // size
    pieces = [rows[..., k * n : (k + 1) * n, :] for k in range(size)]
    *pieces, later = lax.optimization_barrier((*pieces, later))
    return add_low(*[swap_tp(p, k) if k else p for k, p in enumerate(pieces)]), later


def sum_tp(rows):
    size = lax.axis_size("tp")
    n = rows.shape[-2] // size
    total = rows
    for k in range(1, size):
        other = swap_tp(rows, k)
        total = total + jnp.concatenate(
            [other[..., (j ^ k) * n : (j ^ k) * n + n, :] for j in range(size)], axis=-2
        )
    return total


def gather_outer(rows, partners):
    return jnp.concatenate([swap_dp(rows, 2 * k) if k else rows for k in partners], axis=-2)


def gather_plane_near(rows):
    return swap_tp(rows, 1), swap_tp(rows, 2)


def far_sends(near, far):
    n = near.shape[-2] // 2
    return sync(near[..., :n, :], far[..., n:, :])


def far_base(rows, near, far):
    n = rows.shape[-2] // 2
    (top, low), (near_top, near_low), (far_top, far_low) = (
        (value[..., :n, :], value[..., n:, :]) for value in (rows, near, far)
    )
    base = jnp.concatenate([top, far_top, near_top, top, low, near_low, far_low, top], axis=-2)
    return lax.optimization_barrier(base)


def far_join(base, far_a, far_b):
    n = far_a.shape[-2]
    base = lax.dynamic_update_slice_in_dim(base, far_a, 3 * n, axis=-2)
    return lax.dynamic_update_slice_in_dim(base, far_b, 7 * n, axis=-2)


def gather_plane_far(rows, near, far, sends=None):
    sent_a, sent_b = sends or far_sends(near, far)
    return far_join(far_base(rows, near, far), swap_tp(sent_a, 2), swap_tp(sent_b, 1))


def gather_pair_far(early, early_base, late):
    first_a, first_b = swap_tp(early[0], 2), swap_tp(early[1], 1)
    rows, near, far = late
    sent_a, sent_b = far_sends(near, far)
    late_a, late_b = swap_tp(sent_a, 2), swap_tp(sent_b, 1)
    first_a, rows, near, far = sync(first_a, rows, near, far)
    return far_join(early_base, first_a, first_b), far_join(far_base(rows, near, far), late_a, late_b)


def cut(rows, count):
    n = rows.shape[-2] // count
    return [rows[..., i * n : (i + 1) * n, :] for i in range(count)]


def add_pieces(left, right):
    return [add_low(one, two).astype(BF) for one, two in zip(left, right)]


def scatter_core(own, other):
    return add_pieces(cut(own, 4), cut(swap_dp(other, 1), 4))


def scatter_plane_near(quarters):
    keep_a, send_a, keep_b, send_b = quarters
    got_a, got_b = swap_tp(send_a, 1), swap_tp(send_b, 2)
    return add_pieces(cut(keep_a, 2), cut(got_a, 2)) + add_pieces(cut(keep_b, 2), cut(got_b, 2))


def scatter_plane_far(eighths, partners):
    keep_a, send_a, keep_b, send_b = eighths
    got_a, got_b = swap_tp(send_a, 2), swap_tp(send_b, 1)
    half = len(partners) // 2
    return add_pieces(cut(keep_a, half), cut(got_a, half)) + add_pieces(cut(keep_b, half), cut(got_b, half))


def scatter_outer(pieces, partners):
    return add_low(*[swap_dp(p, 2 * k) if k else p for p, k in zip(pieces, partners)])


def scatter_pairs_near(pieces):
    own, one, two, three = pieces
    got_own, got_three = cut(swap_dp(jnp.concatenate([one, two], axis=0), 2), 2)
    return [add_low(own, got_own), add_low(three, got_three).astype(BF)]


def scatter_pairs_far(own, three):
    return own + swap_dp(three, 6).astype(F32)


def call_kernel(body, ins, outs, grid=(), in_specs=None, out_specs=None, flops=0, moved=0, **extra):
    whole = pl.BlockSpec(memory_space=pltpu.VMEM)
    return pl.pallas_call(
        body,
        out_shape=outs,
        grid=grid,
        in_specs=in_specs or [whole] * len(ins),
        out_specs=out_specs or [whole] * len(outs),
        compiler_params=pltpu.CompilerParams(vmem_limit_bytes=VMEM_BYTES),
        cost_estimate=pl.CostEstimate(
            flops=flops // COST_SCALE, bytes_accessed=moved // COST_SCALE, transcendentals=0
        ),
        **extra,
    )(*ins)


def project_kernel(rows_ref, gain_ref, weight_ref, normed_ref, packed_ref, squares_ref):
    part = pl.program_id(0)

    @pl.when(part == 0)
    def _():
        rows = rows_ref[...].astype(F32)
        normed_ref[...] = (rows * rms_scale(rows) * gain_ref[...]).astype(BF)
        squares_ref[...] = jnp.zeros_like(squares_ref)

    packed = jnp.dot(normed_ref[...], weight_ref[...], preferred_element_type=F32)
    packed_ref[...] = packed
    lane = lax.broadcasted_iota(jnp.int32, squares_ref.shape, 1)

    @pl.when(part < 2)
    def _():
        total = jnp.sum(packed * packed, axis=1, keepdims=True)
        squares_ref[...] += jnp.where(lane == part, total, 0.0)


def project(gathered, gain, qkv_parts):
    micro, group, width = gathered.shape
    columns = qkv_parts.shape[2]
    rows = micro * group
    normed, packed, squares = call_kernel(
        project_kernel,
        (gathered.reshape(rows, width), gain[None], qkv_parts),
        [
            jax.ShapeDtypeStruct((rows, width), BF),
            jax.ShapeDtypeStruct((rows, 3 * columns), F32),
            jax.ShapeDtypeStruct((rows, LANES), F32),
        ],
        grid=(3,),
        in_specs=[
            pl.BlockSpec((rows, width), lambda i: (0, 0)),
            pl.BlockSpec((1, width), lambda i: (0, 0)),
            pl.BlockSpec((None, width, columns), lambda i: (i, 0, 0)),
        ],
        out_specs=[
            pl.BlockSpec((rows, width), lambda i: (0, 0)),
            pl.BlockSpec((rows, columns), lambda i: (0, i)),
            pl.BlockSpec((rows, LANES), lambda i: (0, 0)),
        ],
        flops=2 * rows * width * 3 * columns,
        moved=2 * width * 3 * columns,
    )
    return (value.reshape(micro, group, -1) for value in (normed, packed, squares))


def attend_kernel(
    packed_ref, squares_ref, gain_ref, cos_ref, sin_ref, allowed_ref, out_weight_ref,
    used_ref, weights_ref, attended_ref, branch_ref, *, width,
):
    columns = packed_ref.shape[1] // 3
    heads = columns // HD
    cosine, sine = cos_ref[...], sin_ref[...]
    allowed = allowed_ref[...] > 0.0
    scales = lax.rsqrt(squares_ref[:, :2] / width + EPSILON)
    for h in range(heads):
        used = []
        for part in range(2):
            at = slice(part * columns + h * HD, part * columns + (h + 1) * HD)
            values = packed_ref[:, at] * scales[:, part : part + 1]
            values = values * gain_ref[part : part + 1, h * HD : (h + 1) * HD]
            values = (values * cosine + pltpu.roll(values, HD // 2, 1) * sine).astype(BF)
            used_ref[:, at] = values
            used.append(values)
        at = slice(2 * columns + h * HD, 2 * columns + (h + 1) * HD)
        value = packed_ref[:, at].astype(BF)
        used_ref[:, at] = value
        scores = contract(used[0], used[1], 1, 1) * HD ** (-0.5)
        masked = jnp.where(allowed, scores, -1e30)
        top_score = jnp.max(masked, axis=-1, keepdims=True)
        exponent = jnp.where(allowed, jnp.exp(masked - top_score), 0.0)
        weights = exponent / jnp.sum(exponent, axis=-1, keepdims=True)
        weights_ref[h] = weights
        attended_ref[:, h * HD : (h + 1) * HD] = jnp.dot(
            weights.astype(BF), value, preferred_element_type=F32
        ).astype(BF)
    branch_ref[...] = jnp.dot(
        attended_ref[...], out_weight_ref[...], preferred_element_type=F32
    ).astype(BF)


def attend(packed, squares, gain, cosine, sine, allowed, out_weight):
    micro, group = packed.shape[:2]
    columns, width = out_weight.shape
    heads = columns // HD

    def each(*shape):
        return pl.BlockSpec((None,) + shape, lambda m: (m,) + (0,) * len(shape))

    return call_kernel(
        functools.partial(attend_kernel, width=width),
        (packed, squares, gain, cosine, sine, allowed, out_weight),
        [
            jax.ShapeDtypeStruct((micro, group, 3 * columns), BF),
            jax.ShapeDtypeStruct((micro, heads, group, group), F32),
            jax.ShapeDtypeStruct((micro, group, columns), BF),
            jax.ShapeDtypeStruct((micro, group, width), BF),
        ],
        grid=(micro,),
        in_specs=[
            each(group, 3 * columns),
            each(group, LANES),
            pl.BlockSpec((2, columns), lambda m: (0, 0)),
            each(group, HD),
            each(group, HD),
            each(group, group),
            pl.BlockSpec((columns, width), lambda m: (0, 0)),
        ],
        out_specs=[
            each(group, 3 * columns),
            each(heads, group, group),
            each(group, columns),
            each(group, width),
        ],
        flops=2 * micro * group * columns * (width + 2 * group),
        moved=16 * micro * group * width,
    )


def attend_back_kernel(
    d_branch_ref, out_weight_ref, used_ref, weights_ref, packed_ref, squares_ref, gain_ref, cos_ref,
    sin_ref, d_hat_ref, d_value_ref, dots_ref, gain_grad_ref, *, width,
):
    columns = packed_ref.shape[1] // 3
    heads = columns // HD
    cosine, sine = cos_ref[...], sin_ref[...]
    scales = lax.rsqrt(squares_ref[:, :2] / width + EPSILON)
    d_attended = contract(d_branch_ref[...], out_weight_ref[...], 1, 1).astype(BF)
    dots = [0.0, 0.0]
    gain_grad_ref[...] = jnp.zeros_like(gain_grad_ref)
    for h in range(heads):
        own = slice(h * HD, (h + 1) * HD)
        query, key, value = (
            used_ref[:, part * columns + h * HD : part * columns + (h + 1) * HD] for part in range(3)
        )
        d_out = d_attended[:, own]
        weights = weights_ref[h]
        d_weights = contract(d_out, value, 1, 1)
        row_delta = jnp.sum(weights * d_weights, axis=-1, keepdims=True)
        d_scores = (weights * (d_weights - row_delta) * HD ** (-0.5)).astype(BF)
        d_value_ref[:, own] = contract(weights.astype(BF), d_out, 0, 0).astype(BF)
        grads = (
            jnp.dot(d_scores, key, preferred_element_type=F32),
            contract(d_scores, query, 0, 0),
        )
        for part in range(2):
            at = slice(part * columns + h * HD, part * columns + (h + 1) * HD)
            hat = packed_ref[:, at] * scales[:, part : part + 1]
            grad = grads[part] * cosine - pltpu.roll(grads[part], HD // 2, 1) * sine
            gain_grad_ref[part : part + 1, own] = jnp.sum(grad * hat, axis=0, keepdims=True)
            grad = grad * gain_ref[part : part + 1, own]
            d_hat_ref[:, at] = grad
            dots[part] = dots[part] + jnp.sum(grad * hat, axis=1, keepdims=True)
    lane = lax.broadcasted_iota(jnp.int32, dots_ref.shape, 1)
    dots_ref[...] = jnp.where(lane == 0, dots[0], jnp.where(lane == 1, dots[1], 0.0))


def attend_back(m, d_branch, out_weight, used, weights, packed, squares, gain, cosine, sine):
    group = packed.shape[1]
    columns, width = out_weight.shape
    heads = columns // HD

    def pick(*shape):
        return pl.BlockSpec((None,) + shape, lambda i: (m,) + (0,) * len(shape))

    def full(*shape):
        return pl.BlockSpec(shape, lambda i: (0,) * len(shape))

    return call_kernel(
        functools.partial(attend_back_kernel, width=width),
        (d_branch, out_weight, used, weights, packed, squares, gain, cosine, sine),
        [
            jax.ShapeDtypeStruct((group, 2 * columns), F32),
            jax.ShapeDtypeStruct((group, columns), BF),
            jax.ShapeDtypeStruct((group, LANES), F32),
            jax.ShapeDtypeStruct((8, columns), F32),
        ],
        grid=(1,),
        in_specs=[
            full(group, width),
            full(columns, width),
            pick(group, 3 * columns),
            pick(heads, group, group),
            pick(group, 3 * columns),
            pick(group, LANES),
            full(2, columns),
            pick(group, HD),
            pick(group, HD),
        ],
        out_specs=[
            full(group, 2 * columns),
            full(group, columns),
            full(group, LANES),
            full(8, columns),
        ],
        flops=2 * group * columns * (width + 5 * group),
        moved=20 * group * width,
    )


def unproject_kernel(
    d_hat_ref, d_value_ref, dots_ref, packed_ref, squares_ref, weight_ref, normed_ref, d_packed_ref,
    d_normed_ref, gain_grad_ref, *, width,
):
    columns = d_value_ref.shape[1]
    scales = lax.rsqrt(squares_ref[:, :2] / width + EPSILON)
    for part in range(2):
        at = slice(part * columns, (part + 1) * columns)
        scale = scales[:, part : part + 1]
        hat = packed_ref[:, at] * scale
        mean = dots_ref[:, part : part + 1] / width
        d_packed_ref[:, at] = (scale * (d_hat_ref[:, at] - hat * mean)).astype(BF)
    d_packed_ref[:, 2 * columns :] = d_value_ref[...]
    total = 0.0
    for part in range(3):
        at = slice(part * columns, (part + 1) * columns)
        total = total + contract(d_packed_ref[:, at], weight_ref[part], 1, 1)
    d_normed_ref[...] = total.astype(BF)
    column = jnp.sum(total * normed_ref[...].astype(F32), axis=0, keepdims=True)
    gain_grad_ref[...] = jnp.broadcast_to(column, gain_grad_ref.shape)


def unproject(m, d_hat, d_value, dots, packed, squares, qkv_parts, normed):
    group, columns = d_value.shape
    width = qkv_parts.shape[1]

    def pick(*shape):
        return pl.BlockSpec((None,) + shape, lambda i: (m,) + (0,) * len(shape))

    def full(*shape):
        return pl.BlockSpec(shape, lambda i: (0,) * len(shape))

    return call_kernel(
        functools.partial(unproject_kernel, width=width),
        (d_hat, d_value, dots, packed, squares, qkv_parts, normed),
        [
            jax.ShapeDtypeStruct((group, 3 * columns), BF),
            jax.ShapeDtypeStruct((group, width), BF),
            jax.ShapeDtypeStruct((8, width), F32),
        ],
        grid=(1,),
        in_specs=[
            full(group, 2 * columns),
            full(group, columns),
            full(group, LANES),
            pick(group, 3 * columns),
            pick(group, LANES),
            full(3, width, columns),
            pick(group, width),
        ],
        out_specs=[full(group, 3 * columns), full(group, width), full(8, width)],
        flops=2 * group * width * 3 * columns,
        moved=2 * width * 3 * columns + 8 * group * width,
    )


def rows_product_kernel(*refs, count):
    lefts, rights, starts, out_ref = refs[:count], refs[count : 2 * count], refs[2 * count : -1], refs[-1]
    total = starts[0][...] if starts else 0.0
    for left, right in zip(lefts, rights):
        total = total + contract(left[...], right[...], 0, 0)
    out_ref[...] = total


def rows_product(lefts, rights, start, tile, width, columns):
    count = len(lefts)
    rows = sum(left.shape[0] for left in lefts)
    once = pl.Buffered(1)
    starts = [] if start is None else [start]
    return call_kernel(
        functools.partial(rows_product_kernel, count=count),
        (*lefts, *rights, *starts),
        [jax.ShapeDtypeStruct((width, columns), F32)],
        grid=(width // tile,),
        in_specs=[pl.BlockSpec((left.shape[0], tile), lambda i: (0, i)) for left in lefts]
        + [
            pl.BlockSpec((right.shape[0], columns), lambda i: (0, 0), pipeline_mode=once)
            for right in rights
        ]
        + [pl.BlockSpec((tile, columns), lambda i: (i, 0)) for _ in starts],
        out_specs=[pl.BlockSpec((tile, columns), lambda i: (i, 0))],
        flops=2 * rows * width * columns,
        moved=2 * rows * (width + columns) + 4 * width * columns,
    )[0]


def rows_pair(left0_ref, left1_ref, right0, right1):
    return (contract(left0_ref[...], right0, 0, 0) + contract(left1_ref[...], right1, 0, 0)).astype(BF)


def early_grads_kernel(
    normed0_ref, normed1_ref, d_value0_ref, d_value1_ref, attended0_ref, attended1_ref, d_branch0_ref,
    d_branch1_ref, out_ref,
):
    columns = attended0_ref.shape[1]

    @pl.when(pl.program_id(0) == 0)
    def _():
        out_ref[...] = rows_pair(normed0_ref, normed1_ref, d_value0_ref[...], d_value1_ref[...])

    @pl.when(pl.program_id(0) == 1)
    def _():
        for start in range(0, out_ref.shape[0], columns):
            at = slice(start, start + columns)
            out_ref[at, :] = rows_pair(
                attended0_ref, attended1_ref, d_branch0_ref[:, at], d_branch1_ref[:, at]
            )


def early_grads(normed, d_value, attended, d_branch):
    micro, group, width = normed.shape
    columns = attended.shape[2]
    tile = width // 2
    normed_specs = [pl.BlockSpec((None, group, tile), lambda p, i, m=m: (m, 0, i)) for m in range(micro)]
    value_spec = pl.BlockSpec((group, columns), lambda p, i: (0, 0))
    attended_specs = [pl.BlockSpec((None, group, columns), lambda p, i, m=m: (m, 0, 0)) for m in range(micro)]
    branch_spec = pl.BlockSpec((group, tile), lambda p, i: (0, jnp.where(p == 1, i, 0)))
    return call_kernel(
        early_grads_kernel,
        (normed, normed, *d_value, attended, attended, *d_branch),
        [jax.ShapeDtypeStruct((2 * width, columns), BF)],
        grid=(2, 2),
        in_specs=normed_specs + [value_spec] * 2 + attended_specs + [branch_spec] * 2,
        out_specs=[pl.BlockSpec((tile, columns), lambda p, i: (2 * p + i, 0))],
        flops=2 * micro * group * width * 2 * columns,
        moved=2 * width * 2 * columns,
    )[0]


def late_grads_kernel(normed0_ref, normed1_ref, d_packed0_ref, d_packed1_ref, out_ref):
    out_ref[...] = rows_pair(normed0_ref, normed1_ref, d_packed0_ref[...], d_packed1_ref[...])


def late_grads(normed, d_packed):
    micro, group, width = normed.shape
    columns = d_packed[0].shape[1] // 3
    tile = width // 2
    normed_specs = [pl.BlockSpec((None, group, tile), lambda i, p, m=m: (m, 0, i)) for m in range(micro)]
    return call_kernel(
        late_grads_kernel,
        (normed, normed, *d_packed),
        [jax.ShapeDtypeStruct((2 * width, columns), BF)],
        grid=(2, 2),
        in_specs=normed_specs + [pl.BlockSpec((group, columns), lambda i, p: (0, p))] * 2,
        out_specs=[pl.BlockSpec((tile, columns), lambda i, p: (2 * p + i, 0))],
        flops=2 * micro * group * width * 2 * columns,
        moved=2 * width * 2 * columns,
    )[0]


def experts_kernel(
    ids_ref, moe_ref, cot_ref, router_ref, gate_up_ref, down_ref, d_rows_ref, scaled_ref, d_inner_ref,
    *, experts, local,
):
    width = moe_ref.shape[1]
    quarter = down_ref.shape[0] // local
    rows = moe_ref[...]
    lane = lax.broadcasted_iota(jnp.int32, (rows.shape[0], LANES), 1)
    logits = jnp.dot(rows, router_ref[...], preferred_element_type=F32)
    logits = jnp.where(lane < experts, logits, -1e30)
    exponent = jnp.exp(logits - jnp.max(logits, axis=1, keepdims=True))
    probs = exponent / jnp.sum(exponent, axis=1, keepdims=True)
    mask = cot_ref[:, width:].astype(F32)
    gates = probs * mask
    back = jnp.zeros_like(probs)
    for e in range(local):
        here = lane == ids_ref[0] + e
        gate = jnp.sum(jnp.where(here, gates, 0.0), axis=1, keepdims=True)
        at = slice(e * quarter, (e + 1) * quarter)
        gate_at = slice(2 * e * quarter, (2 * e + 1) * quarter)
        up_at = slice((2 * e + 1) * quarter, (2 * e + 2) * quarter)
        d_raw = contract(cot_ref[:, :width], down_ref[at, :], 1, 1)
        gate_pre = jnp.dot(rows, gate_up_ref[:, gate_at], preferred_element_type=F32)
        up_pre = jnp.dot(rows, gate_up_ref[:, up_at], preferred_element_type=F32)
        sigmoid = 1.0 / (1.0 + jnp.exp(-gate_pre))
        silu = gate_pre * sigmoid
        active = silu * up_pre
        term = jnp.sum(active * d_raw, axis=1, keepdims=True)
        back = jnp.where(here, term, back)
        scaled_ref[:, at] = (active * gate).astype(BF)
        d_active = d_raw * gate
        d_inner_ref[:, gate_at] = (
            d_active * up_pre * sigmoid * (1.0 + gate_pre * (1.0 - sigmoid))
        ).astype(BF)
        d_inner_ref[:, up_at] = (d_active * silu).astype(BF)
    d_rows_ref[:, width:] = jnp.where(mask > 0.0, back, 0.0).astype(BF)
    d_rows_ref[:, :width] = contract(d_inner_ref[...], gate_up_ref[...], 1, 1).astype(BF)


def run_experts(first_id, moe_all, cot_all, router_wide, gate_up, down, experts, local):
    total, width = moe_all.shape
    tile = min(total, EXPERT_TILE)
    inner = gate_up.shape[1]
    once = pl.Buffered(1)
    return call_kernel(
        functools.partial(experts_kernel, experts=experts, local=local),
        (first_id, moe_all, cot_all, router_wide, gate_up, down),
        [
            jax.ShapeDtypeStruct((total, width + LANES), BF),
            jax.ShapeDtypeStruct((total, inner // 2), BF),
            jax.ShapeDtypeStruct((total, inner), BF),
        ],
        grid=(total // tile,),
        in_specs=[
            pl.BlockSpec(memory_space=pltpu.SMEM),
            pl.BlockSpec((tile, width), lambda i: (i, 0)),
            pl.BlockSpec((tile, width + LANES), lambda i: (i, 0)),
            pl.BlockSpec((width, LANES), lambda i: (0, 0), pipeline_mode=once),
            pl.BlockSpec((width, inner), lambda i: (0, 0), pipeline_mode=once),
            pl.BlockSpec((inner // 2, width), lambda i: (0, 0), pipeline_mode=once),
        ],
        out_specs=[
            pl.BlockSpec((tile, width + LANES), lambda i: (i, 0)),
            pl.BlockSpec((tile, inner // 2), lambda i: (i, 0)),
            pl.BlockSpec((tile, inner), lambda i: (i, 0)),
        ],
        flops=2 * total * width * inner * 5 // 2,
        moved=total * width * 6,
    )


def shards(
    tokens, cotangent, routes, lengths, attn_gain, qkv_weight, qk_gain, out_weight, moe_gain,
    router, w_gateup, w_down,
):
    tp_size = lax.axis_size("tp")
    dp_size = lax.axis_size("dp")
    tp_rank = lax.axis_index("tp")
    dp_rank = lax.axis_index("dp")
    micro_count, _, own_rows, width = tokens.shape
    group = own_rows * tp_size
    experts = router.shape[1]
    local = w_gateup.shape[0]
    columns = qkv_weight.shape[2]
    quarter = w_down.shape[1]

    qkv_parts = jnp.transpose(qkv_weight, (1, 0, 2))
    gate_up = jnp.concatenate([w_gateup[e].reshape(width, 2 * quarter) for e in range(local)], axis=1)
    down = w_down.reshape(local * quarter, width)
    router_wide = jnp.pad(router, ((0, 0), (0, -experts % LANES)))
    expert_ids = jnp.arange(experts, dtype=jnp.int32)
    first_id = (dp_rank * local).astype(jnp.int32).reshape(1)

    places = jnp.concatenate(
        [(tp_rank ^ k) * own_rows + jnp.arange(own_rows, dtype=jnp.int32) for k in range(tp_size)]
    )
    own_places = tp_rank * own_rows + jnp.arange(own_rows, dtype=jnp.int32)
    frequency = jnp.exp(
        jnp.arange(HD // 2, dtype=F32) * (-2.0 * jnp.log(10000.0) / HD)
    )

    first_len = lengths[:, 0, 0][:, None]
    live_end = first_len + lengths[:, 0, 1][:, None]
    live_own = (own_places[None, :] < live_end).astype(F32)[:, :, None]
    d_mixed = cotangent[:, 0].astype(F32) * live_own
    own_routes = lax.dynamic_slice_in_dim(routes[:, 0], tp_rank * own_rows, own_rows, 1)
    chosen = jnp.any(own_routes[..., None] == expert_ids, axis=2)
    mask = jnp.pad(chosen.astype(BF), ((0, 0), (0, 0), (0, -experts % LANES)))
    cot_sent = jnp.concatenate([d_mixed.astype(BF), mask], axis=2)


    outer = dp_size // 2
    span = min(outer, 4)
    parts = [range(first, first + span) for first in range(0, outer, span)]
    zone = parts[0]

    x_own = tokens[:, 0].astype(F32)
    x_scale = rms_scale(x_own)
    x_hat = x_own * x_scale

    def experts_of(moe_half, cot_half):
        return run_experts(first_id, moe_half, cot_half, router_wide, gate_up, down, experts, local)

    def gate_up_grads(start, moe, ran):
        inner = 2 * local * quarter
        return rows_product(moe, [r[2] for r in ran], start, 256, width, inner)

    def down_grads(start, cot, ran):
        return rows_product([r[1] for r in ran], cot, start, 256, local * quarter, width)

    def mix(ran):
        return jnp.dot(ran[1], down, preferred_element_type=F32).astype(BF)

    gathered = gather_tp(tokens[:, 0])
    cot_z = [swap_dp(cot_sent, 2 * k) for k in zone[1:-1]]
    gathered, cot_late = sync(gathered, cot_sent)
    cot_z.append(swap_dp(cot_late, 2 * zone[-1]))

    segment = (places >= first_len).astype(jnp.int32) + (places >= live_end).astype(jnp.int32)
    starts = jnp.where(segment == 0, 0, jnp.where(segment == 1, first_len, live_end))
    angles = (places - starts).astype(F32)[:, :, None] * frequency
    cosine, sine = jnp.cos(angles), jnp.sin(angles)
    cosine = jnp.concatenate([cosine, cosine], axis=2)
    sine = jnp.concatenate([-sine, sine], axis=2)
    allowed = (segment[:, :, None] == segment[:, None, :]) & (places[None, :] <= places[:, None])

    normed, packed, squares = project(gathered, attn_gain, qkv_parts)
    squares = sum_tp(squares)
    used, weights, attended, branch = attend(
        packed, squares, qk_gain, cosine, sine, allowed.astype(F32), out_weight
    )
    branch, gate_up, down, router_wide, *cot_z = sync(branch, gate_up, down, router_wide, cot_sent, *cot_z)
    branch_own, cot_z = scatter_tp_first(branch, jnp.concatenate(cot_z, axis=1))
    cot_z0, cot_z1 = cot_z[0], cot_z[1]
    cot_near0 = gather_plane_near(cot_z0)
    hidden = x_own + branch_own
    h_scale = rms_scale(hidden)
    h_hat = hidden * h_scale
    moe_own = (h_hat * moe_gain).astype(BF)
    moe_z0 = gather_outer(moe_own[0], zone)

    moe_z0, moe_own1, cot_z0, cot_z1, *cot_near0 = sync(moe_z0, moe_own[1], cot_z0, cot_z1, *cot_near0)
    moe_near0 = gather_plane_near(moe_z0)
    moe_z1 = gather_outer(moe_own1, zone)

    cot_sends0 = [*far_sends(*cot_near0), far_base(cot_z0, *cot_near0)]
    moe_z0, moe_z1, cot_z0, cot_z1, *near = sync(
        moe_z0, moe_z1, cot_z0, cot_z1, *cot_near0, *moe_near0, *cot_sends0
    )
    cot_half0, moe_half0 = gather_pair_far(near[4:6], near[6], (moe_z0, *near[2:4]))

    moe_half0, cot_half0, moe_z1, cot_z1 = sync(moe_half0, cot_half0, moe_z1, cot_z1)
    moe_other0, cot_other0 = swap_dp(moe_half0, 1), swap_dp(cot_half0, 1)
    cot_near1 = gather_plane_near(cot_z1)
    own0 = experts_of(moe_half0, cot_half0)

    moe_other0, cot_other0, moe_z1, cot_z1, *rest = sync(
        moe_other0, cot_other0, moe_z1, cot_z1, *cot_near1, *own0
    )
    cot_near1, own0 = rest[:2], rest[2:]
    moe_near1 = gather_plane_near(moe_z1)
    other0 = experts_of(moe_other0, cot_other0)

    cot_sends1 = far_sends(*cot_near1)
    moe_z1, cot_z1, *rest = sync(
        moe_z1, cot_z1, *cot_near1, *moe_near1, *own0, *other0, *cot_sends1
    )
    own0, other0, cot_sends1 = rest[4:7], rest[7:10], rest[10:]
    core0 = scatter_core(own0[0], other0[0])
    cot_half1 = gather_plane_far(cot_z1, *rest[:2], cot_sends1)
    moe_half1 = gather_plane_far(moe_z1, *rest[2:4])
    mix0 = [mix(own0), mix(other0)]

    cot_half1, moe_half1, *rest = sync(cot_half1, moe_half1, *core0, *mix0, *own0, *other0)
    core0, mix0, own0, other0 = rest[:4], rest[4:6], rest[6:9], rest[9:]
    near0 = scatter_plane_near(core0)
    moe_other1, cot_other1 = swap_dp(moe_half1, 1), swap_dp(cot_half1, 1)
    own1 = experts_of(moe_half1, cot_half1)

    moe_other1, cot_other1, *rest = sync(moe_other1, cot_other1, *near0, *own1)
    near0, own1 = rest[:4], rest[4:]
    far0 = scatter_plane_far(near0, zone)
    other1 = experts_of(moe_other1, cot_other1)

    rest = sync(*far0, *mix0, *own1, *other1)
    far0, rest = rest[:span], rest[span:]
    mix0, own1, other1 = rest[:2], rest[2:5], rest[5:]
    core1 = scatter_core(own1[0], other1[0])
    back0 = scatter_outer(far0, zone)
    mix_core0 = scatter_core(*mix0)
    mix1 = [mix(own1), mix(other1)]

    back0, *rest = sync(back0, *core1, *mix_core0, *mix1, *own1, *other1)
    core1, mix_core0, mix1, own1, other1 = rest[:4], rest[4:8], rest[8:10], rest[10:13], rest[13:]
    near1 = scatter_plane_near(core1)
    mix_core1 = scatter_core(*mix1)

    def into_hidden(m, back):
        expert_grad = back[:, :width]
        probs = jax.nn.softmax(jnp.dot(moe_own[m], router, preferred_element_type=F32), axis=-1)
        d_choice = back[:, width : width + experts]
        d_logits = (probs * (d_choice - jnp.sum(probs * d_choice, axis=1, keepdims=True))).astype(BF)
        d_moe_in = expert_grad + contract(d_logits, router, 1, 1)
        d_h_hat = d_moe_in * moe_gain
        d_hidden = d_mixed[m] + h_scale[m] * (
            d_h_hat - h_hat[m] * jnp.mean(d_h_hat * h_hat[m], axis=1, keepdims=True)
        )
        small = (contract(moe_own[m], d_logits, 0, 0), jnp.sum(d_moe_in * h_hat[m], axis=0))
        return d_hidden, small

    def into_attention(m, d_branch):
        return attend_back(
            m, d_branch, out_weight, used, weights, packed, squares, qk_gain, cosine, sine
        )

    def into_packed(m, back, dots):
        return unproject(m, *back[:2], dots, packed, squares, qkv_parts, normed)

    ran0, moe0, cot0 = (own0, other0), (moe_half0, moe_other0), (cot_half0, cot_other0)
    ran1, moe1, cot1 = (own1, other1), (moe_half1, moe_other1), (cot_half1, cot_other1)
    whole = len(parts) == 1
    if whole:
        d_hidden0, small0 = into_hidden(0, back0)
        back0 = d_hidden0
    back0, *rest = sync(back0, *near1, *mix_core0, *mix_core1)
    near1, mix_core0, mix_core1 = rest[:4], rest[4:8], rest[8:]
    far1 = scatter_plane_far(near1, zone)
    if whole:
        d_branch0 = gather_tp(back0.astype(BF))
        d_branch0, *rest = sync(d_branch0, *far1, *mix_core0, *mix_core1)
    else:
        back0, *rest = sync(back0, *far1, *mix_core0, *mix_core1)
    far1, mix_core0, mix_core1 = rest[:span], rest[span : span + 4], rest[span + 4 :]
    back1 = scatter_outer(far1, zone)
    mix_near0 = scatter_plane_near(mix_core0)
    d_gate_up = d_down = None
    more = [0.0, 0.0]
    if whole:
        to_packed0 = into_attention(0, d_branch0)
        back1, *rest = sync(back1, *to_packed0, *mix_near0, *mix_core1)
        to_packed0, mix_near0, mix_core1 = rest[:4], rest[4:8], rest[8:]
    else:
        back = [back0, back1]
        d_gate_up = gate_up_grads(None, moe0 + moe1, ran0 + ran1)
        d_down = down_grads(None, cot0 + cot1, ran0 + ran1)
        for later in parts[1:]:
            for m in range(micro_count):
                sent, moe_sent, d_gate_up, d_down, back[m], more[m] = sync(
                    cot_sent[m], moe_own[m], d_gate_up, d_down, back[m], more[m]
                )
                halves = []
                for rows in (sent, moe_sent):
                    rows = gather_outer(rows, later)
                    rows = gather_plane_far(rows, *gather_plane_near(rows))
                    halves.append((rows, swap_dp(rows, 1)))
                cot, moe = halves
                ran = [experts_of(moe[j], cot[j]) for j in range(2)]
                d_gate_up = gate_up_grads(d_gate_up, moe, ran)
                d_down = down_grads(d_down, cot, ran)
                terms = []
                for pair in ([r[0] for r in ran], [mix(r) for r in ran]):
                    near = scatter_plane_near(scatter_core(*pair))
                    terms.append(scatter_outer(scatter_plane_far(near, later), later))
                back[m], more[m] = back[m] + terms[0], more[m] + terms[1]
        d_hidden0, small0 = into_hidden(0, back[0])
        back1 = back[1]
        d_branch0 = gather_tp(d_hidden0.astype(BF))
        to_packed0 = into_attention(0, d_branch0)

    d_hidden1, small1 = into_hidden(1, back1)
    d_branch1 = gather_tp(d_hidden1.astype(BF))
    dots0 = sum_tp(to_packed0[2])
    d_branch1, dots0, *rest = sync(d_branch1, dots0, *mix_near0, *mix_core1)
    mix_near0, mix_core1 = rest[:4], rest[4:]
    to_packed1 = into_attention(1, d_branch1)
    mix_far0 = scatter_plane_far(mix_near0, zone)
    dots1 = sum_tp(to_packed1[2])
    d_value = (to_packed0[1], to_packed1[1])
    early = early_grads(normed, d_value, attended, (d_branch0, d_branch1))
    early = lax.psum_scatter(early, "dp", scatter_dimension=0, tiled=True)
    end0 = into_packed(0, to_packed0, dots0)
    dots1, *rest = sync(dots1, *end0, *mix_far0)
    end0, mix_far0 = rest[:3], rest[3:]
    mixed0 = scatter_pairs_far(*scatter_pairs_near(mix_far0))
    end1 = into_packed(1, to_packed1, dots1)
    late = late_grads(normed, (end0[0], end1[0]))
    late, *rest = sync(late, *mix_core1, *end0[1:], *end1[1:])
    mix_core1, d_normed, attn_terms = rest[:4], (rest[4], rest[6]), (rest[5], rest[7])

    late = lax.psum_scatter(late, "dp", scatter_dimension=0, tiled=True)
    mix_near1 = scatter_plane_near(mix_core1)
    d_normed0 = scatter_tp(d_normed[0])
    grad_attn_gain = (attn_terms[0] + attn_terms[1])[0] / attn_gain
    grad_qk = (to_packed0[3] + to_packed1[3])[:2]
    wide_qk = jnp.pad(grad_qk, ((0, 0), (0, width - columns)))
    grad_router, grad_moe_gain = (one + two for one, two in zip(small0, small1))
    small = jnp.concatenate([grad_attn_gain[None], grad_moe_gain[None], grad_router.T], axis=0)
    small, mixed0, d_normed0, d_normed1, *mix_near1 = sync(small, mixed0, d_normed0, d_normed[1], *mix_near1)
    mix_far1 = scatter_plane_far(mix_near1, zone)
    total = small
    for k in range(1, tp_size):
        total = total + swap_tp(small, k)
    small = jnp.concatenate([total, wide_qk], axis=0)
    small, d_normed0, d_normed1, *mix_far1 = sync(small, d_normed0, d_normed1, *mix_far1)
    mixed1 = scatter_pairs_near(mix_far1)
    small = (small + swap_dp(small, 1)).astype(BF)
    early, late, small, d_normed0, d_normed1, *mixed1 = sync(early, late, small, d_normed0, d_normed1, *mixed1)
    shared = lax.all_gather(jnp.stack([late, early]), "dp", axis=1, tiled=True)
    mixed1 = scatter_pairs_far(*mixed1)
    small = add_low(small, *[swap_dp(small, 2 * k) for k in range(1, outer)])
    d_normed1 = scatter_tp(d_normed1)
    if whole:
        d_gate_up = gate_up_grads(None, moe0 + moe1, ran0 + ran1)
        d_down = down_grads(None, cot0 + cot1, ran0 + ran1)
    input_grads = []
    for m, (d_hidden, d_rows) in enumerate(((d_hidden0, d_normed0), (d_hidden1, d_normed1))):
        d_x_hat = d_rows * attn_gain
        d_tokens = d_hidden + x_scale[m] * (
            d_x_hat - x_hat[m] * jnp.mean(d_x_hat * x_hat[m], axis=1, keepdims=True)
        )
        input_grads.append(d_tokens.astype(BF))
    mixed = jnp.stack([mixed0 + more[0], mixed1 + more[1]])
    out = (hidden + mixed).astype(BF)
    d_gate_up = d_gate_up.reshape(width, local, 2, quarter)
    d_gate_up_out = jnp.stack([d_gate_up[:, e] for e in range(local)])
    shared, small, d_tokens, out, d_gate_up_out, d_down = sync(
        shared, small, jnp.stack(input_grads), out, d_gate_up_out, d_down
    )
    total_qkv = shared.reshape(4, width, columns)[:3]
    total_out = shared[1, width:].reshape(width // columns, columns, columns)
    total_out = jnp.concatenate([piece for piece in total_out], axis=1).astype(F32)
    return (
        out[:, None],
        d_tokens[:, None],
        small[0],
        jnp.transpose(total_qkv.astype(F32), (1, 0, 2)),
        small[-2:, :columns],
        total_out,
        small[1],
        small[2 : 2 + experts].T,
        d_gate_up_out.reshape(w_gateup.shape),
        d_down.reshape(w_down.shape),
    )


def solution(mesh):
    return jax.shard_map(
        shards,
        mesh=mesh,
        in_specs=(
            P(None, "dp", "tp", None),
            P(None, "dp", "tp", None),
            P(None, "dp", None, None),
            P(None, "dp", None),
            P(),
            P(None, None, "tp"),
            P(None, "tp"),
            P("tp", None),
            P(),
            P(),
            P("dp", None, None, "tp"),
            P("dp", "tp", None),
        ),
        out_specs=(
            P(None, "dp", "tp", None),
            P(None, "dp", "tp", None),
            P(),
            P(None, None, "tp"),
            P(None, "tp"),
            P("tp", None),
            P(),
            P(),
            P("dp", None, None, "tp"),
            P("dp", "tp", None),
        ),
        check_vma=False,
    )
```

```python
import functools

import jax
import jax.numpy as jnp
from jax import lax
from jax.experimental import pallas as pl
from jax.experimental.pallas import tpu as pltpu
from jax.sharding import PartitionSpec as P

HD = 128
EPSILON = 1e-05
LANES = 128
BF = jnp.bfloat16
F32 = jnp.float32
VMEM_BYTES = 56 * 1024 * 1024
EXPERT_TILE = 128
COST_SCALE = 8


def rms_scale(values):
    return lax.rsqrt(jnp.mean(values * values, axis=-1, keepdims=True) + EPSILON)


def contract(left, right, left_dim, right_dim):
    return lax.dot_general(
        left, right, (((left_dim,), (right_dim,)), ((), ())), preferred_element_type=F32
    )


def swap_tp(value, bits):
    size = lax.axis_size("tp")
    return lax.ppermute(value, "tp", [(i, i ^ bits) for i in range(size)])


def swap_dp(value, bits):
    size = lax.axis_size("dp")
    return lax.ppermute(value, "dp", [(i, i ^ bits) for i in range(size)])


def sync(*values):
    return lax.optimization_barrier(values)


def after(value, *deps):
    return lax.optimization_barrier((value, *deps))[0]


def add_low(*terms):
    total = terms[0].astype(F32)
    for term in terms[1:]:
        total = total + term.astype(F32)
    return total


def gather_tp(rows):
    size = lax.axis_size("tp")
    return jnp.concatenate([rows] + [swap_tp(rows, k) for k in range(1, size)], axis=-2)


def scatter_tp(rows):
    size = lax.axis_size("tp")
    n = rows.shape[-2] // size
    pieces = [rows[..., k * n : (k + 1) * n, :] for k in range(size)]
    return add_low(*[swap_tp(p, k) if k else p for k, p in enumerate(pieces)])


def scatter_tp_first(rows, later):
    size = lax.axis_size("tp")
    n = rows.shape[-2] // size
    pieces = [rows[..., k * n : (k + 1) * n, :] for k in range(size)]
    *pieces, later = lax.optimization_barrier((*pieces, later))
    return add_low(*[swap_tp(p, k) if k else p for k, p in enumerate(pieces)]), later


def sum_tp(rows):
    size = lax.axis_size("tp")
    n = rows.shape[-2] // size
    total = rows
    for k in range(1, size):
        other = swap_tp(rows, k)
        total = total + jnp.concatenate(
            [other[..., (j ^ k) * n : (j ^ k) * n + n, :] for j in range(size)], axis=-2
        )
    return total


def gather_outer(rows, partners):
    return jnp.concatenate([swap_dp(rows, 2 * k) if k else rows for k in partners], axis=-2)


def gather_plane_near(rows):
    return swap_tp(rows, 1), swap_tp(rows, 2)


def far_sends(near, far):
    n = near.shape[-2] // 2
    return sync(near[..., :n, :], far[..., n:, :])


def far_base(rows, near, far):
    n = rows.shape[-2] // 2
    (top, low), (near_top, near_low), (far_top, far_low) = (
        (value[..., :n, :], value[..., n:, :]) for value in (rows, near, far)
    )
    base = jnp.concatenate([top, far_top, near_top, top, low, near_low, far_low, top], axis=-2)
    return lax.optimization_barrier(base)


def far_join(base, far_a, far_b):
    n = far_a.shape[-2]
    base = lax.dynamic_update_slice_in_dim(base, far_a, 3 * n, axis=-2)
    return lax.dynamic_update_slice_in_dim(base, far_b, 7 * n, axis=-2)


def gather_plane_far(rows, near, far, sends=None):
    sent_a, sent_b = sends or far_sends(near, far)
    return far_join(far_base(rows, near, far), swap_tp(sent_a, 2), swap_tp(sent_b, 1))


def gather_pair_far(early, early_base, late):
    first_a, first_b = swap_tp(early[0], 2), swap_tp(early[1], 1)
    rows, near, far = late
    sent_a, sent_b = far_sends(near, far)
    late_a, late_b = swap_tp(sent_a, 2), swap_tp(sent_b, 1)
    first_a, rows, near, far = sync(first_a, rows, near, far)
    return far_join(early_base, first_a, first_b), far_join(far_base(rows, near, far), late_a, late_b)


def cut(rows, count):
    n = rows.shape[-2] // count
    return [rows[..., i * n : (i + 1) * n, :] for i in range(count)]


def add_pieces(left, right):
    return [add_low(one, two).astype(BF) for one, two in zip(left, right)]


def scatter_core(own, other):
    return add_pieces(cut(own, 4), cut(swap_dp(other, 1), 4))


def scatter_plane_near(quarters):
    keep_a, send_a, keep_b, send_b = quarters
    got_a, got_b = swap_tp(send_a, 1), swap_tp(send_b, 2)
    return add_pieces(cut(keep_a, 2), cut(got_a, 2)) + add_pieces(cut(keep_b, 2), cut(got_b, 2))


def scatter_plane_far(eighths, partners):
    keep_a, send_a, keep_b, send_b = eighths
    got_a, got_b = swap_tp(send_a, 2), swap_tp(send_b, 1)
    half = len(partners) // 2
    return add_pieces(cut(keep_a, half), cut(got_a, half)) + add_pieces(cut(keep_b, half), cut(got_b, half))


def scatter_outer(pieces, partners):
    return add_low(*[swap_dp(p, 2 * k) if k else p for p, k in zip(pieces, partners)])


def scatter_pairs_near(pieces):
    own, one, two, three = pieces
    got_own, got_three = cut(swap_dp(jnp.concatenate([one, two], axis=0), 2), 2)
    return [add_low(own, got_own), add_low(three, got_three).astype(BF)]


def scatter_pairs_far(own, three):
    return own + swap_dp(three, 6).astype(F32)


def call_kernel(body, ins, outs, grid=(), in_specs=None, out_specs=None, flops=0, moved=0, **extra):
    whole = pl.BlockSpec(memory_space=pltpu.VMEM)
    return pl.pallas_call(
        body,
        out_shape=outs,
        grid=grid,
        in_specs=in_specs or [whole] * len(ins),
        out_specs=out_specs or [whole] * len(outs),
        compiler_params=pltpu.CompilerParams(vmem_limit_bytes=VMEM_BYTES),
        cost_estimate=pl.CostEstimate(
            flops=flops // COST_SCALE, bytes_accessed=moved // COST_SCALE, transcendentals=0
        ),
        **extra,
    )(*ins)


def project_kernel(rows_ref, gain_ref, weight_ref, normed_ref, packed_ref, squares_ref):
    part = pl.program_id(0)

    @pl.when(part == 0)
    def _():
        rows = rows_ref[...].astype(F32)
        normed_ref[...] = (rows * rms_scale(rows) * gain_ref[...]).astype(BF)
        squares_ref[...] = jnp.zeros_like(squares_ref)

    packed = jnp.dot(normed_ref[...], weight_ref[...], preferred_element_type=F32)
    packed_ref[...] = packed
    lane = lax.broadcasted_iota(jnp.int32, squares_ref.shape, 1)

    @pl.when(part < 2)
    def _():
        total = jnp.sum(packed * packed, axis=1, keepdims=True)
        squares_ref[...] += jnp.where(lane == part, total, 0.0)


def project(gathered, gain, qkv_parts):
    micro, group, width = gathered.shape
    columns = qkv_parts.shape[2]
    rows = micro * group
    normed, packed, squares = call_kernel(
        project_kernel,
        (gathered.reshape(rows, width), gain[None], qkv_parts),
        [
            jax.ShapeDtypeStruct((rows, width), BF),
            jax.ShapeDtypeStruct((rows, 3 * columns), F32),
            jax.ShapeDtypeStruct((rows, LANES), F32),
        ],
        grid=(3,),
        in_specs=[
            pl.BlockSpec((rows, width), lambda i: (0, 0)),
            pl.BlockSpec((1, width), lambda i: (0, 0)),
            pl.BlockSpec((None, width, columns), lambda i: (i, 0, 0)),
        ],
        out_specs=[
            pl.BlockSpec((rows, width), lambda i: (0, 0)),
            pl.BlockSpec((rows, columns), lambda i: (0, i)),
            pl.BlockSpec((rows, LANES), lambda i: (0, 0)),
        ],
        flops=2 * rows * width * 3 * columns,
        moved=2 * width * 3 * columns,
    )
    return (value.reshape(micro, group, -1) for value in (normed, packed, squares))


def attend_kernel(
    packed_ref, squares_ref, gain_ref, cos_ref, sin_ref, allowed_ref, out_weight_ref,
    used_ref, weights_ref, attended_ref, branch_ref, *, width,
):
    columns = packed_ref.shape[1] // 3
    heads = columns // HD
    cosine, sine = cos_ref[...], sin_ref[...]
    allowed = allowed_ref[...] > 0.0
    scales = lax.rsqrt(squares_ref[:, :2] / width + EPSILON)
    for h in range(heads):
        used = []
        for part in range(2):
            at = slice(part * columns + h * HD, part * columns + (h + 1) * HD)
            values = packed_ref[:, at] * scales[:, part : part + 1]
            values = values * gain_ref[part : part + 1, h * HD : (h + 1) * HD]
            values = (values * cosine + pltpu.roll(values, HD // 2, 1) * sine).astype(BF)
            used_ref[:, at] = values
            used.append(values)
        at = slice(2 * columns + h * HD, 2 * columns + (h + 1) * HD)
        value = packed_ref[:, at].astype(BF)
        used_ref[:, at] = value
        scores = contract(used[0], used[1], 1, 1) * HD ** (-0.5)
        masked = jnp.where(allowed, scores, -1e30)
        top_score = jnp.max(masked, axis=-1, keepdims=True)
        exponent = jnp.where(allowed, jnp.exp(masked - top_score), 0.0)
        weights = exponent / jnp.sum(exponent, axis=-1, keepdims=True)
        weights_ref[h] = weights
        attended_ref[:, h * HD : (h + 1) * HD] = jnp.dot(
            weights.astype(BF), value, preferred_element_type=F32
        ).astype(BF)
    branch_ref[...] = jnp.dot(
        attended_ref[...], out_weight_ref[...], preferred_element_type=F32
    ).astype(BF)


def attend(packed, squares, gain, cosine, sine, allowed, out_weight):
    micro, group = packed.shape[:2]
    columns, width = out_weight.shape
    heads = columns // HD

    def each(*shape):
        return pl.BlockSpec((None,) + shape, lambda m: (m,) + (0,) * len(shape))

    return call_kernel(
        functools.partial(attend_kernel, width=width),
        (packed, squares, gain, cosine, sine, allowed, out_weight),
        [
            jax.ShapeDtypeStruct((micro, group, 3 * columns), BF),
            jax.ShapeDtypeStruct((micro, heads, group, group), F32),
            jax.ShapeDtypeStruct((micro, group, columns), BF),
            jax.ShapeDtypeStruct((micro, group, width), BF),
        ],
        grid=(micro,),
        in_specs=[
            each(group, 3 * columns),
            each(group, LANES),
            pl.BlockSpec((2, columns), lambda m: (0, 0)),
            each(group, HD),
            each(group, HD),
            each(group, group),
            pl.BlockSpec((columns, width), lambda m: (0, 0)),
        ],
        out_specs=[
            each(group, 3 * columns),
            each(heads, group, group),
            each(group, columns),
            each(group, width),
        ],
        flops=2 * micro * group * columns * (width + 2 * group),
        moved=16 * micro * group * width,
    )


def attend_back_kernel(
    d_branch_ref, out_weight_ref, used_ref, weights_ref, packed_ref, squares_ref, gain_ref, cos_ref,
    sin_ref, d_hat_ref, d_value_ref, dots_ref, gain_grad_ref, *, width,
):
    columns = packed_ref.shape[1] // 3
    heads = columns // HD
    cosine, sine = cos_ref[...], sin_ref[...]
    scales = lax.rsqrt(squares_ref[:, :2] / width + EPSILON)
    d_attended = contract(d_branch_ref[...], out_weight_ref[...], 1, 1).astype(BF)
    dots = [0.0, 0.0]
    gain_grad_ref[...] = jnp.zeros_like(gain_grad_ref)
    for h in range(heads):
        own = slice(h * HD, (h + 1) * HD)
        query, key, value = (
            used_ref[:, part * columns + h * HD : part * columns + (h + 1) * HD] for part in range(3)
        )
        d_out = d_attended[:, own]
        weights = weights_ref[h]
        d_weights = contract(d_out, value, 1, 1)
        row_delta = jnp.sum(weights * d_weights, axis=-1, keepdims=True)
        d_scores = (weights * (d_weights - row_delta) * HD ** (-0.5)).astype(BF)
        d_value_ref[:, own] = contract(weights.astype(BF), d_out, 0, 0).astype(BF)
        grads = (
            jnp.dot(d_scores, key, preferred_element_type=F32),
            contract(d_scores, query, 0, 0),
        )
        for part in range(2):
            at = slice(part * columns + h * HD, part * columns + (h + 1) * HD)
            hat = packed_ref[:, at] * scales[:, part : part + 1]
            grad = grads[part] * cosine - pltpu.roll(grads[part], HD // 2, 1) * sine
            gain_grad_ref[part : part + 1, own] = jnp.sum(grad * hat, axis=0, keepdims=True)
            grad = grad * gain_ref[part : part + 1, own]
            d_hat_ref[:, at] = grad
            dots[part] = dots[part] + jnp.sum(grad * hat, axis=1, keepdims=True)
    lane = lax.broadcasted_iota(jnp.int32, dots_ref.shape, 1)
    dots_ref[...] = jnp.where(lane == 0, dots[0], jnp.where(lane == 1, dots[1], 0.0))


def attend_back(m, d_branch, out_weight, used, weights, packed, squares, gain, cosine, sine):
    group = packed.shape[1]
    columns, width = out_weight.shape
    heads = columns // HD

    def pick(*shape):
        return pl.BlockSpec((None,) + shape, lambda i: (m,) + (0,) * len(shape))

    def full(*shape):
        return pl.BlockSpec(shape, lambda i: (0,) * len(shape))

    return call_kernel(
        functools.partial(attend_back_kernel, width=width),
        (d_branch, out_weight, used, weights, packed, squares, gain, cosine, sine),
        [
            jax.ShapeDtypeStruct((group, 2 * columns), F32),
            jax.ShapeDtypeStruct((group, columns), BF),
            jax.ShapeDtypeStruct((group, LANES), F32),
            jax.ShapeDtypeStruct((8, columns), F32),
        ],
        grid=(1,),
        in_specs=[
            full(group, width),
            full(columns, width),
            pick(group, 3 * columns),
            pick(heads, group, group),
            pick(group, 3 * columns),
            pick(group, LANES),
            full(2, columns),
            pick(group, HD),
            pick(group, HD),
        ],
        out_specs=[
            full(group, 2 * columns),
            full(group, columns),
            full(group, LANES),
            full(8, columns),
        ],
        flops=2 * group * columns * (width + 5 * group),
        moved=20 * group * width,
    )


def unproject_kernel(
    d_hat_ref, d_value_ref, dots_ref, packed_ref, squares_ref, weight_ref, normed_ref, d_packed_ref,
    d_normed_ref, gain_grad_ref, *, width,
):
    columns = d_value_ref.shape[1]
    scales = lax.rsqrt(squares_ref[:, :2] / width + EPSILON)
    for part in range(2):
        at = slice(part * columns, (part + 1) * columns)
        scale = scales[:, part : part + 1]
        hat = packed_ref[:, at] * scale
        mean = dots_ref[:, part : part + 1] / width
        d_packed_ref[:, at] = (scale * (d_hat_ref[:, at] - hat * mean)).astype(BF)
    d_packed_ref[:, 2 * columns :] = d_value_ref[...]
    total = 0.0
    for part in range(3):
        at = slice(part * columns, (part + 1) * columns)
        total = total + contract(d_packed_ref[:, at], weight_ref[part], 1, 1)
    d_normed_ref[...] = total.astype(BF)
    column = jnp.sum(total * normed_ref[...].astype(F32), axis=0, keepdims=True)
    gain_grad_ref[...] = jnp.broadcast_to(column, gain_grad_ref.shape)


def unproject(m, d_hat, d_value, dots, packed, squares, qkv_parts, normed):
    group, columns = d_value.shape
    width = qkv_parts.shape[1]

    def pick(*shape):
        return pl.BlockSpec((None,) + shape, lambda i: (m,) + (0,) * len(shape))

    def full(*shape):
        return pl.BlockSpec(shape, lambda i: (0,) * len(shape))

    return call_kernel(
        functools.partial(unproject_kernel, width=width),
        (d_hat, d_value, dots, packed, squares, qkv_parts, normed),
        [
            jax.ShapeDtypeStruct((group, 3 * columns), BF),
            jax.ShapeDtypeStruct((group, width), BF),
            jax.ShapeDtypeStruct((8, width), F32),
        ],
        grid=(1,),
        in_specs=[
            full(group, 2 * columns),
            full(group, columns),
            full(group, LANES),
            pick(group, 3 * columns),
            pick(group, LANES),
            full(3, width, columns),
            pick(group, width),
        ],
        out_specs=[full(group, 3 * columns), full(group, width), full(8, width)],
        flops=2 * group * width * 3 * columns,
        moved=2 * width * 3 * columns + 8 * group * width,
    )


def rows_product_kernel(*refs, count):
    lefts, rights, starts, out_ref = refs[:count], refs[count : 2 * count], refs[2 * count : -1], refs[-1]
    total = starts[0][...] if starts else 0.0
    for left, right in zip(lefts, rights):
        total = total + contract(left[...], right[...], 0, 0)
    out_ref[...] = total


def rows_product(lefts, rights, start, tile, width, columns):
    count = len(lefts)
    rows = sum(left.shape[0] for left in lefts)
    once = pl.Buffered(1)
    starts = [] if start is None else [start]
    return call_kernel(
        functools.partial(rows_product_kernel, count=count),
        (*lefts, *rights, *starts),
        [jax.ShapeDtypeStruct((width, columns), F32)],
        grid=(width // tile,),
        in_specs=[pl.BlockSpec((left.shape[0], tile), lambda i: (0, i)) for left in lefts]
        + [
            pl.BlockSpec((right.shape[0], columns), lambda i: (0, 0), pipeline_mode=once)
            for right in rights
        ]
        + [pl.BlockSpec((tile, columns), lambda i: (i, 0)) for _ in starts],
        out_specs=[pl.BlockSpec((tile, columns), lambda i: (i, 0))],
        flops=2 * rows * width * columns,
        moved=2 * rows * (width + columns) + 4 * width * columns,
    )[0]


def rows_pair(left0_ref, left1_ref, right0, right1):
    return (contract(left0_ref[...], right0, 0, 0) + contract(left1_ref[...], right1, 0, 0)).astype(BF)


def early_grads_kernel(
    normed0_ref, normed1_ref, d_value0_ref, d_value1_ref, attended0_ref, attended1_ref, d_branch0_ref,
    d_branch1_ref, out_ref,
):
    columns = attended0_ref.shape[1]

    @pl.when(pl.program_id(0) == 0)
    def _():
        out_ref[...] = rows_pair(normed0_ref, normed1_ref, d_value0_ref[...], d_value1_ref[...])

    @pl.when(pl.program_id(0) == 1)
    def _():
        for start in range(0, out_ref.shape[0], columns):
            at = slice(start, start + columns)
            out_ref[at, :] = rows_pair(
                attended0_ref, attended1_ref, d_branch0_ref[:, at], d_branch1_ref[:, at]
            )


def early_grads(normed, d_value, attended, d_branch):
    micro, group, width = normed.shape
    columns = attended.shape[2]
    tile = width // 2
    normed_specs = [pl.BlockSpec((None, group, tile), lambda p, i, m=m: (m, 0, i)) for m in range(micro)]
    value_spec = pl.BlockSpec((group, columns), lambda p, i: (0, 0))
    attended_specs = [pl.BlockSpec((None, group, columns), lambda p, i, m=m: (m, 0, 0)) for m in range(micro)]
    branch_spec = pl.BlockSpec((group, tile), lambda p, i: (0, jnp.where(p == 1, i, 0)))
    return call_kernel(
        early_grads_kernel,
        (normed, normed, *d_value, attended, attended, *d_branch),
        [jax.ShapeDtypeStruct((2 * width, columns), BF)],
        grid=(2, 2),
        in_specs=normed_specs + [value_spec] * 2 + attended_specs + [branch_spec] * 2,
        out_specs=[pl.BlockSpec((tile, columns), lambda p, i: (2 * p + i, 0))],
        flops=2 * micro * group * width * 2 * columns,
        moved=2 * width * 2 * columns,
    )[0]


def late_grads_kernel(normed0_ref, normed1_ref, d_packed0_ref, d_packed1_ref, out_ref):
    out_ref[...] = rows_pair(normed0_ref, normed1_ref, d_packed0_ref[...], d_packed1_ref[...])


def late_grads(normed, d_packed):
    micro, group, width = normed.shape
    columns = d_packed[0].shape[1] // 3
    tile = width // 2
    normed_specs = [pl.BlockSpec((None, group, tile), lambda i, p, m=m: (m, 0, i)) for m in range(micro)]
    return call_kernel(
        late_grads_kernel,
        (normed, normed, *d_packed),
        [jax.ShapeDtypeStruct((2 * width, columns), BF)],
        grid=(2, 2),
        in_specs=normed_specs + [pl.BlockSpec((group, columns), lambda i, p: (0, p))] * 2,
        out_specs=[pl.BlockSpec((tile, columns), lambda i, p: (2 * p + i, 0))],
        flops=2 * micro * group * width * 2 * columns,
        moved=2 * width * 2 * columns,
    )[0]


def experts_kernel(
    ids_ref, moe_ref, cot_ref, router_ref, gate_up_ref, down_ref, d_rows_ref, scaled_ref, d_inner_ref,
    *, experts, local,
):
    width = moe_ref.shape[1]
    quarter = down_ref.shape[0] // local
    rows = moe_ref[...]
    lane = lax.broadcasted_iota(jnp.int32, (rows.shape[0], LANES), 1)
    logits = jnp.dot(rows, router_ref[...], preferred_element_type=F32)
    logits = jnp.where(lane < experts, logits, -1e30)
    exponent = jnp.exp(logits - jnp.max(logits, axis=1, keepdims=True))
    probs = exponent / jnp.sum(exponent, axis=1, keepdims=True)
    mask = cot_ref[:, width:].astype(F32)
    gates = probs * mask
    back = jnp.zeros_like(probs)
    for e in range(local):
        here = lane == ids_ref[0] + e
        gate = jnp.sum(jnp.where(here, gates, 0.0), axis=1, keepdims=True)
        at = slice(e * quarter, (e + 1) * quarter)
        gate_at = slice(2 * e * quarter, (2 * e + 1) * quarter)
        up_at = slice((2 * e + 1) * quarter, (2 * e + 2) * quarter)
        d_raw = contract(cot_ref[:, :width], down_ref[at, :], 1, 1)
        gate_pre = jnp.dot(rows, gate_up_ref[:, gate_at], preferred_element_type=F32)
        up_pre = jnp.dot(rows, gate_up_ref[:, up_at], preferred_element_type=F32)
        sigmoid = 1.0 / (1.0 + jnp.exp(-gate_pre))
        silu = gate_pre * sigmoid
        active = silu * up_pre
        term = jnp.sum(active * d_raw, axis=1, keepdims=True)
        back = jnp.where(here, term, back)
        scaled_ref[:, at] = (active * gate).astype(BF)
        d_active = d_raw * gate
        d_inner_ref[:, gate_at] = (
            d_active * up_pre * sigmoid * (1.0 + gate_pre * (1.0 - sigmoid))
        ).astype(BF)
        d_inner_ref[:, up_at] = (d_active * silu).astype(BF)
    d_rows_ref[:, width:] = jnp.where(mask > 0.0, back, 0.0).astype(BF)
    d_rows_ref[:, :width] = contract(d_inner_ref[...], gate_up_ref[...], 1, 1).astype(BF)


def run_experts(first_id, moe_all, cot_all, router_wide, gate_up, down, experts, local):
    total, width = moe_all.shape
    tile = min(total, EXPERT_TILE)
    inner = gate_up.shape[1]
    once = pl.Buffered(1)
    return call_kernel(
        functools.partial(experts_kernel, experts=experts, local=local),
        (first_id, moe_all, cot_all, router_wide, gate_up, down),
        [
            jax.ShapeDtypeStruct((total, width + LANES), BF),
            jax.ShapeDtypeStruct((total, inner // 2), BF),
            jax.ShapeDtypeStruct((total, inner), BF),
        ],
        grid=(total // tile,),
        in_specs=[
            pl.BlockSpec(memory_space=pltpu.SMEM),
            pl.BlockSpec((tile, width), lambda i: (i, 0)),
            pl.BlockSpec((tile, width + LANES), lambda i: (i, 0)),
            pl.BlockSpec((width, LANES), lambda i: (0, 0), pipeline_mode=once),
            pl.BlockSpec((width, inner), lambda i: (0, 0), pipeline_mode=once),
            pl.BlockSpec((inner // 2, width), lambda i: (0, 0), pipeline_mode=once),
        ],
        out_specs=[
            pl.BlockSpec((tile, width + LANES), lambda i: (i, 0)),
            pl.BlockSpec((tile, inner // 2), lambda i: (i, 0)),
            pl.BlockSpec((tile, inner), lambda i: (i, 0)),
        ],
        flops=2 * total * width * inner * 5 // 2,
        moved=total * width * 6,
    )


def shards(
    tokens, cotangent, routes, lengths, attn_gain, qkv_weight, qk_gain, out_weight, moe_gain,
    router, w_gateup, w_down,
):
    tp_size = lax.axis_size("tp")
    dp_size = lax.axis_size("dp")
    tp_rank = lax.axis_index("tp")
    dp_rank = lax.axis_index("dp")
    micro_count, _, own_rows, width = tokens.shape
    group = own_rows * tp_size
    experts = router.shape[1]
    local = w_gateup.shape[0]
    columns = qkv_weight.shape[2]
    quarter = w_down.shape[1]

    qkv_parts = jnp.transpose(qkv_weight, (1, 0, 2))
    gate_up = jnp.concatenate([w_gateup[e].reshape(width, 2 * quarter) for e in range(local)], axis=1)
    down = w_down.reshape(local * quarter, width)
    router_wide = jnp.pad(router, ((0, 0), (0, -experts % LANES)))
    expert_ids = jnp.arange(experts, dtype=jnp.int32)
    first_id = (dp_rank * local).astype(jnp.int32).reshape(1)

    places = jnp.concatenate(
        [(tp_rank ^ k) * own_rows + jnp.arange(own_rows, dtype=jnp.int32) for k in range(tp_size)]
    )
    own_places = tp_rank * own_rows + jnp.arange(own_rows, dtype=jnp.int32)
    frequency = jnp.exp(
        jnp.arange(HD // 2, dtype=F32) * (-2.0 * jnp.log(10000.0) / HD)
    )

    first_len = lengths[:, 0, 0][:, None]
    live_end = first_len + lengths[:, 0, 1][:, None]
    live_own = (own_places[None, :] < live_end).astype(F32)[:, :, None]
    d_mixed = cotangent[:, 0].astype(F32) * live_own
    own_routes = lax.dynamic_slice_in_dim(routes[:, 0], tp_rank * own_rows, own_rows, 1)
    chosen = jnp.any(own_routes[..., None] == expert_ids, axis=2)
    mask = jnp.pad(chosen.astype(BF), ((0, 0), (0, 0), (0, -experts % LANES)))
    cot_sent = jnp.concatenate([d_mixed.astype(BF), mask], axis=2)


    outer = dp_size // 2
    span = min(outer, 4)
    parts = [range(first, first + span) for first in range(0, outer, span)]
    zone = parts[0]

    x_own = tokens[:, 0].astype(F32)
    x_scale = rms_scale(x_own)
    x_hat = x_own * x_scale

    def experts_of(moe_half, cot_half):
        return run_experts(first_id, moe_half, cot_half, router_wide, gate_up, down, experts, local)

    def gate_up_grads(start, moe, ran):
        inner = 2 * local * quarter
        return rows_product(moe, [r[2] for r in ran], start, 256, width, inner)

    def down_grads(start, cot, ran):
        return rows_product([r[1] for r in ran], cot, start, 256, local * quarter, width)

    def mix(ran):
        return jnp.dot(ran[1], down, preferred_element_type=F32).astype(BF)

    gathered = gather_tp(tokens[:, 0])
    cot_z = [swap_dp(cot_sent, 2 * k) for k in zone[1:-1]]
    gathered, cot_late = sync(gathered, cot_sent)
    cot_z.append(swap_dp(cot_late, 2 * zone[-1]))

    segment = (places >= first_len).astype(jnp.int32) + (places >= live_end).astype(jnp.int32)
    starts = jnp.where(segment == 0, 0, jnp.where(segment == 1, first_len, live_end))
    angles = (places - starts).astype(F32)[:, :, None] * frequency
    cosine, sine = jnp.cos(angles), jnp.sin(angles)
    cosine = jnp.concatenate([cosine, cosine], axis=2)
    sine = jnp.concatenate([-sine, sine], axis=2)
    allowed = (segment[:, :, None] == segment[:, None, :]) & (places[None, :] <= places[:, None])

    normed, packed, squares = project(gathered, attn_gain, qkv_parts)
    squares = sum_tp(squares)
    used, weights, attended, branch = attend(
        packed, squares, qk_gain, cosine, sine, allowed.astype(F32), out_weight
    )
    branch, gate_up, down, router_wide, *cot_z = sync(branch, gate_up, down, router_wide, cot_sent, *cot_z)
    branch_own, cot_z = scatter_tp_first(branch, jnp.concatenate(cot_z, axis=1))
    cot_z0, cot_z1 = cot_z[0], cot_z[1]
    cot_near0 = gather_plane_near(cot_z0)
    hidden = x_own + branch_own
    h_scale = rms_scale(hidden)
    h_hat = hidden * h_scale
    moe_own = (h_hat * moe_gain).astype(BF)
    moe_z0 = gather_outer(moe_own[0], zone)

    moe_z0, moe_own1, cot_z0, cot_z1, *cot_near0 = sync(moe_z0, moe_own[1], cot_z0, cot_z1, *cot_near0)
    moe_near0 = gather_plane_near(moe_z0)
    moe_z1 = gather_outer(moe_own1, zone)

    cot_sends0 = [*far_sends(*cot_near0), far_base(cot_z0, *cot_near0)]
    moe_z0, moe_z1, cot_z0, cot_z1, *near = sync(
        moe_z0, moe_z1, cot_z0, cot_z1, *cot_near0, *moe_near0, *cot_sends0
    )
    cot_half0, moe_half0 = gather_pair_far(near[4:6], near[6], (moe_z0, *near[2:4]))

    moe_half0, cot_half0, moe_z1, cot_z1 = sync(moe_half0, cot_half0, moe_z1, cot_z1)
    moe_other0, cot_other0 = swap_dp(moe_half0, 1), swap_dp(cot_half0, 1)
    cot_near1 = gather_plane_near(cot_z1)
    own0 = experts_of(moe_half0, cot_half0)

    moe_other0, cot_other0, moe_z1, cot_z1, *rest = sync(
        moe_other0, cot_other0, moe_z1, cot_z1, *cot_near1, *own0
    )
    cot_near1, own0 = rest[:2], rest[2:]
    moe_near1 = gather_plane_near(moe_z1)
    other0 = experts_of(moe_other0, cot_other0)

    cot_sends1 = far_sends(*cot_near1)
    moe_z1, cot_z1, *rest = sync(
        moe_z1, cot_z1, *cot_near1, *moe_near1, *own0, *other0, *cot_sends1
    )
    own0, other0, cot_sends1 = rest[4:7], rest[7:10], rest[10:]
    core0 = scatter_core(own0[0], other0[0])
    cot_half1 = gather_plane_far(cot_z1, *rest[:2], cot_sends1)
    moe_half1 = gather_plane_far(moe_z1, *rest[2:4])
    mix0 = [mix(own0), mix(other0)]

    cot_half1, moe_half1, *rest = sync(cot_half1, moe_half1, *core0, *mix0, *own0, *other0)
    core0, mix0, own0, other0 = rest[:4], rest[4:6], rest[6:9], rest[9:]
    near0 = scatter_plane_near(core0)
    moe_other1, cot_other1 = swap_dp(moe_half1, 1), swap_dp(cot_half1, 1)
    own1 = experts_of(moe_half1, cot_half1)

    moe_other1, cot_other1, *rest = sync(moe_other1, cot_other1, *near0, *own1)
    near0, own1 = rest[:4], rest[4:]
    far0 = scatter_plane_far(near0, zone)
    other1 = experts_of(moe_other1, cot_other1)

    rest = sync(*far0, *mix0, *own1, *other1)
    far0, rest = rest[:span], rest[span:]
    mix0, own1, other1 = rest[:2], rest[2:5], rest[5:]
    core1 = scatter_core(own1[0], other1[0])
    back0 = scatter_outer(far0, zone)
    mix_core0 = scatter_core(*mix0)
    mix1 = [mix(own1), mix(other1)]

    back0, *rest = sync(back0, *core1, *mix_core0, *mix1, *own1, *other1)
    core1, mix_core0, mix1, own1, other1 = rest[:4], rest[4:8], rest[8:10], rest[10:13], rest[13:]
    near1 = scatter_plane_near(core1)
    mix_core1 = scatter_core(*mix1)

    def into_hidden(m, back):
        expert_grad = back[:, :width]
        probs = jax.nn.softmax(jnp.dot(moe_own[m], router, preferred_element_type=F32), axis=-1)
        d_choice = back[:, width : width + experts]
        d_logits = (probs * (d_choice - jnp.sum(probs * d_choice, axis=1, keepdims=True))).astype(BF)
        d_moe_in = expert_grad + contract(d_logits, router, 1, 1)
        d_h_hat = d_moe_in * moe_gain
        d_hidden = d_mixed[m] + h_scale[m] * (
            d_h_hat - h_hat[m] * jnp.mean(d_h_hat * h_hat[m], axis=1, keepdims=True)
        )
        small = (contract(moe_own[m], d_logits, 0, 0), jnp.sum(d_moe_in * h_hat[m], axis=0))
        return d_hidden, small

    def into_attention(m, d_branch):
        return attend_back(
            m, d_branch, out_weight, used, weights, packed, squares, qk_gain, cosine, sine
        )

    def into_packed(m, back, dots):
        return unproject(m, *back[:2], dots, packed, squares, qkv_parts, normed)

    ran0, moe0, cot0 = (own0, other0), (moe_half0, moe_other0), (cot_half0, cot_other0)
    ran1, moe1, cot1 = (own1, other1), (moe_half1, moe_other1), (cot_half1, cot_other1)
    whole = len(parts) == 1
    if whole:
        d_hidden0, small0 = into_hidden(0, back0)
        back0 = d_hidden0
    back0, *rest = sync(back0, *near1, *mix_core0, *mix_core1)
    near1, mix_core0, mix_core1 = rest[:4], rest[4:8], rest[8:]
    far1 = scatter_plane_far(near1, zone)
    if whole:
        d_branch0 = gather_tp(back0.astype(BF))
        d_branch0, *rest = sync(d_branch0, *far1, *mix_core0, *mix_core1)
    else:
        back0, *rest = sync(back0, *far1, *mix_core0, *mix_core1)
    far1, mix_core0, mix_core1 = rest[:span], rest[span : span + 4], rest[span + 4 :]
    back1 = scatter_outer(far1, zone)
    mix_near0 = scatter_plane_near(mix_core0)
    d_gate_up = d_down = None
    more = [0.0, 0.0]
    if whole:
        to_packed0 = into_attention(0, d_branch0)
        back1, *rest = sync(back1, *to_packed0, *mix_near0, *mix_core1)
        to_packed0, mix_near0, mix_core1 = rest[:4], rest[4:8], rest[8:]
    else:
        back = [back0, back1]
        d_gate_up = gate_up_grads(None, moe0 + moe1, ran0 + ran1)
        d_down = down_grads(None, cot0 + cot1, ran0 + ran1)
        for later in parts[1:]:
            for m in range(micro_count):
                sent, moe_sent, d_gate_up, d_down, back[m], more[m] = sync(
                    cot_sent[m], moe_own[m], d_gate_up, d_down, back[m], more[m]
                )
                halves = []
                for rows in (sent, moe_sent):
                    rows = gather_outer(rows, later)
                    rows = gather_plane_far(rows, *gather_plane_near(rows))
                    halves.append((rows, swap_dp(rows, 1)))
                cot, moe = halves
                ran = [experts_of(moe[j], cot[j]) for j in range(2)]
                d_gate_up = gate_up_grads(d_gate_up, moe, ran)
                d_down = down_grads(d_down, cot, ran)
                terms = []
                for pair in ([r[0] for r in ran], [mix(r) for r in ran]):
                    near = scatter_plane_near(scatter_core(*pair))
                    terms.append(scatter_outer(scatter_plane_far(near, later), later))
                back[m], more[m] = back[m] + terms[0], more[m] + terms[1]
        d_hidden0, small0 = into_hidden(0, back[0])
        back1 = back[1]
        d_branch0 = gather_tp(d_hidden0.astype(BF))
        to_packed0 = into_attention(0, d_branch0)

    d_hidden1, small1 = into_hidden(1, back1)
    d_branch1 = gather_tp(d_hidden1.astype(BF))
    dots0 = sum_tp(to_packed0[2])
    d_branch1, dots0, *rest = sync(d_branch1, dots0, *mix_near0, *mix_core1)
    mix_near0, mix_core1 = rest[:4], rest[4:]
    to_packed1 = into_attention(1, d_branch1)
    mix_far0 = scatter_plane_far(mix_near0, zone)
    dots1 = sum_tp(to_packed1[2])
    d_value = (to_packed0[1], to_packed1[1])
    early = early_grads(normed, d_value, attended, (d_branch0, d_branch1))
    early = lax.psum_scatter(early, "dp", scatter_dimension=0, tiled=True)
    end0 = into_packed(0, to_packed0, dots0)
    dots1, *rest = sync(dots1, *end0, *mix_far0)
    end0, mix_far0 = rest[:3], rest[3:]
    mixed0 = scatter_pairs_far(*scatter_pairs_near(mix_far0))
    end1 = into_packed(1, to_packed1, dots1)
    late = late_grads(normed, (end0[0], end1[0]))
    late, *rest = sync(late, *mix_core1, *end0[1:], *end1[1:])
    mix_core1, d_normed, attn_terms = rest[:4], (rest[4], rest[6]), (rest[5], rest[7])

    late = lax.psum_scatter(late, "dp", scatter_dimension=0, tiled=True)
    mix_near1 = scatter_plane_near(mix_core1)
    d_normed0 = scatter_tp(d_normed[0])
    grad_attn_gain = (attn_terms[0] + attn_terms[1])[0] / attn_gain
    grad_qk = (to_packed0[3] + to_packed1[3])[:2]
    wide_qk = jnp.pad(grad_qk, ((0, 0), (0, width - columns)))
    grad_router, grad_moe_gain = (one + two for one, two in zip(small0, small1))
    small = jnp.concatenate([grad_attn_gain[None], grad_moe_gain[None], grad_router.T], axis=0)
    small, mixed0, d_normed0, d_normed1, *mix_near1 = sync(small, mixed0, d_normed0, d_normed[1], *mix_near1)
    mix_far1 = scatter_plane_far(mix_near1, zone)
    total = small
    for k in range(1, tp_size):
        total = total + swap_tp(small, k)
    small = jnp.concatenate([total, wide_qk], axis=0)
    small, d_normed0, d_normed1, *mix_far1 = sync(small, d_normed0, d_normed1, *mix_far1)
    mixed1 = scatter_pairs_near(mix_far1)
    small = (small + swap_dp(small, 1)).astype(BF)
    early, late, small, d_normed0, d_normed1, *mixed1 = sync(early, late, small, d_normed0, d_normed1, *mixed1)
    shared = lax.all_gather(jnp.stack([late, early]), "dp", axis=1, tiled=True)
    mixed1 = scatter_pairs_far(*mixed1)
    small = add_low(small, *[swap_dp(small, 2 * k) for k in range(1, outer)])
    d_normed1 = scatter_tp(d_normed1)
    if whole:
        d_gate_up = gate_up_grads(None, moe0 + moe1, ran0 + ran1)
        d_down = down_grads(None, cot0 + cot1, ran0 + ran1)
    input_grads = []
    for m, (d_hidden, d_rows) in enumerate(((d_hidden0, d_normed0), (d_hidden1, d_normed1))):
        d_x_hat = d_rows * attn_gain
        d_tokens = d_hidden + x_scale[m] * (
            d_x_hat - x_hat[m] * jnp.mean(d_x_hat * x_hat[m], axis=1, keepdims=True)
        )
        input_grads.append(d_tokens.astype(BF))
    mixed = jnp.stack([mixed0 + more[0], mixed1 + more[1]])
    out = (hidden + mixed).astype(BF)
    d_gate_up = d_gate_up.reshape(width, local, 2, quarter)
    d_gate_up_out = jnp.stack([d_gate_up[:, e] for e in range(local)])
    shared, small, d_tokens, out, d_gate_up_out, d_down = sync(
        shared, small, jnp.stack(input_grads), out, d_gate_up_out, d_down
    )
    total_qkv = shared.reshape(4, width, columns)[:3]
    total_out = shared[1, width:].reshape(width // columns, columns, columns)
    total_out = jnp.concatenate([piece for piece in total_out], axis=1).astype(F32)
    return (
        out[:, None],
        d_tokens[:, None],
        small[0],
        jnp.transpose(total_qkv.astype(F32), (1, 0, 2)),
        small[-2:, :columns],
        total_out,
        small[1],
        small[2 : 2 + experts].T,
        d_gate_up_out.reshape(w_gateup.shape),
        d_down.reshape(w_down.shape),
    )


def solution(mesh):
    return jax.shard_map(
        shards,
        mesh=mesh,
        in_specs=(
            P(None, "dp", "tp", None),
            P(None, "dp", "tp", None),
            P(None, "dp", None, None),
            P(None, "dp", None),
            P(),
            P(None, None, "tp"),
            P(None, "tp"),
            P("tp", None),
            P(),
            P(),
            P("dp", None, None, "tp"),
            P("dp", "tp", None),
        ),
        out_specs=(
            P(None, "dp", "tp", None),
            P(None, "dp", "tp", None),
            P(),
            P(None, None, "tp"),
            P(None, "tp"),
            P("tp", None),
            P(),
            P(),
            P("dp", None, None, "tp"),
            P("dp", "tp", None),
        ),
        check_vma=False,
    )
```
